32 devices in a mesh: dp: 8 (over y, x, core), mp: 4 (over z).
Axes of the slice: x: 2, y: 2, z: 4, core: 2. Of those that a mesh axis runs over, the one named last changes fastest.
Arguments:
- inputs: bfloat16 [16, 48, 48, 800], P('dp', None, None, 'mp')
- crop_sizes: int32 [16, 2], P('dp'), may hold values from 24 to 48, as said below
- land_mask: int32 [16, 48, 48], P('dp'), may hold values 0 or 1
- conv_weight: bfloat16 [7, 7, 800], P(None, None, 'mp'), may hold values from -0.875 to 0.875
- norm_gain: bfloat16 [800], P('mp'), may hold values from 0.5 to 1.5
- norm_shift: bfloat16 [800], P('mp'), may hold values from -3 to 3
- up_weight: bfloat16 [800, 3200], P(None, 'mp'), may hold values from -0.21875 to 0.21875
- up_bias: bfloat16 [3200], P('mp'), may hold values from -3 to 3
- down_weight: bfloat16 [3200, 800], P('mp'), may hold values from -0.21875 to 0.21875
- down_bias: bfloat16 [800], P('mp'), may hold values from -3 to 3
- cotangent: bfloat16 [16, 48, 48, 800], P('dp', None, None, 'mp'), may hold values from -6 to 6
Outputs:
- output: bfloat16 [16, 48, 48, 800], P('dp', None, None, 'mp')
- input_grad: bfloat16 [16, 48, 48, 800], P('dp', None, None, 'mp')
- conv_weight_grad: float32 [7, 7, 800], P(None, None, 'mp')
- gain_grad: float32 [800], P('mp')
- shift_grad: float32 [800], P('mp')
- up_weight_grad: float32 [800, 3200], P(None, 'mp')
- up_bias_grad: float32 [3200], P('mp')
- down_weight_grad: float32 [3200, 800], P('mp')
- down_bias_grad: float32 [800], P('mp')
The draws below stay inside these ranges and needn't reach their ends.
Inputs may be any that keep to these rules, and one draw needn't show every extreme that they name: `crop_sizes`: crop 0 always covers all 48 x 48 cells.
All inputs are finite; a program needn't handle non-finite values. No bound on the sum of `land_mask` on one device may be relied on, other than what follows from the above.
Results may differ from the reference program's by a relative error of at most 0.018.
Values may be sent and summed in bfloat16 or wider, within the bound.
No kernel may reach another device: no remote copies, remote signals or barrier semaphores. Data moves between devices by JAX's collectives and lax.ppermute only.
A program may use at most 128 MiB of HBM per device.

```python
import jax
import jax.numpy as jnp
from jax import lax

C = 800
FF = 3200
KS = 7
SIDE = 48
CROPS = 16


def draw_inputs(key, part):
    key = jax.random.fold_in(key, 11)
    subkeys = jax.random.split(key, 3)
    position = jnp.arange(CROPS, dtype=jnp.float32) / max(CROPS - 1, 1)
    crop_scale = 3.0 ** position
    channel_scale = jnp.exp(jax.random.uniform(subkeys[1], (C,), minval=-0.7, maxval=0.7))
    offset = 0.4 * jax.random.normal(subkeys[2], (C,))
    noise_field = jax.random.normal(subkeys[0], (CROPS, SIDE, SIDE, C))
    values = crop_scale[:, None, None, None] * (noise_field * channel_scale + offset)
    return values.astype(jnp.float32).astype(jnp.bfloat16)


def draw_crop_sizes(key, part):
    key = jax.random.fold_in(key, 23)
    crop_dims = jax.random.randint(key, (CROPS, 2), SIDE // 2, SIDE + 1)
    return crop_dims.at[0].set(SIDE).astype(jnp.int32)


def plant(array, key, least, top_value):
    extent = array.shape
    place = [jax.random.randint(jax.random.fold_in(key, axis), (), 0, extent[axis]) for axis in range(len(extent))]
    array = array.at[tuple(place)].set(least)
    longest = extent.index(max(extent))
    place[longest] = (place[longest] + 1) % extent[longest]
    return array.at[tuple(place)].set(top_value)


def levels(rng, dims, shards, least, top_value):
    loudness = 1.0
    for dim, shards_of in shards:
        draws = jax.random.uniform(jax.random.fold_in(jax.random.fold_in(rng, 6), dim), (shards_of,), jnp.float32, least / len(shards), top_value / len(shards))
        loudness = loudness * jnp.repeat(jnp.exp(draws), dims[dim] // shards_of).reshape((-1,) + (1,) * (len(dims) - 1 - dim))
    return loudness


def noise(key, dims, scale, bound, pieces=(), kind=jnp.bfloat16):
    values = scale * jax.random.normal(key, dims, jnp.float32)
    if pieces:
        values = values * levels(key, dims, pieces, -0.22, 0.18)
    return jnp.clip(values, -bound, bound).astype(kind)


def setup_inputs(seed: int = 0) -> dict:
    streams_of = jax.random.split(jax.random.key(seed), 12)
    inputs = draw_inputs(jax.random.fold_in(streams_of[11], 71), 0)
    crop_sizes = draw_crop_sizes(jax.random.fold_in(streams_of[11], 71), 0)
    land_mask = plant((jax.random.randint(streams_of[2], (CROPS, SIDE, SIDE), 0, 4) < 3).astype(jnp.int32), jax.random.fold_in(streams_of[2], 1), 0, 1)
    conv_weight = noise(streams_of[3], (KS, KS, C), (KS * KS) ** -0.5, 0.875, ((2, 4),))
    norm_gain = jnp.clip(0.5 + 1.0 * jax.random.uniform(streams_of[4], (C,), jnp.float32) ** levels(streams_of[4], (C,), ((0, 4),), -0.2, 0.2), 0.5, 1.5).astype(jnp.bfloat16)
    norm_shift = noise(streams_of[5], (C,), 0.5, 3.0, ((0, 4),))
    up_weight = noise(streams_of[6], (C, FF), C ** -0.5, 0.21875, ((1, 4),))
    up_bias = noise(streams_of[7], (FF,), 0.5, 3.0, ((0, 4),))
    down_weight = noise(streams_of[8], (FF, C), (FF // 4) ** -0.5, 0.21875, ((0, 4),))
    down_bias = noise(streams_of[9], (C,), 0.5, 3.0, ((0, 4),))
    cotangent = noise(streams_of[10], (CROPS, SIDE, SIDE, C), 1.0, 6.0, ((0, 8), (3, 4)))
    return {"inputs": inputs, "crop_sizes": crop_sizes, "land_mask": land_mask, "conv_weight": conv_weight, "norm_gain": norm_gain, "norm_shift": norm_shift, "up_weight": up_weight, "up_bias": up_bias, "down_weight": down_weight, "down_bias": down_bias, "cotangent": cotangent}


EPSILON = 1e-05
HIGH = lax.Precision.HIGHEST

@jax.custom_vjp
def low(v):
    return lax.optimization_barrier(v.astype(jnp.bfloat16)).astype(jnp.float32)

@jax.custom_vjp
def low_back(v):
    return v

def low_keep(v):
    return (low(v), None)

def low_pass(kept, grad):
    return (grad,)

def back_keep(v):
    return (v, None)

def back_low(kept, grad):
    return (low(grad),)
low.defvjp(low_keep, low_pass)
low_back.defvjp(back_keep, back_low)

def validity(crop_dims, land_mask, side_cells):
    cell_index = jnp.arange(side_cells, dtype=jnp.int32)
    inside = (cell_index[None, :, None] < crop_dims[:, 0][:, None, None]) & (cell_index[None, None, :] < crop_dims[:, 1][:, None, None])
    return jnp.where(inside, land_mask, 0).astype(jnp.float32)[..., None]

def gelu_exact(value):
    return 0.5 * value * (1.0 + lax.erf(value * 0.7071067811865476))

def reference(inputs, crop_sizes, land_mask, conv_weight, norm_gain, norm_shift, up_weight, up_bias, down_weight, down_bias, cotangent):
    usable = validity(crop_sizes, land_mask, SIDE)
    half_width = KS // 2
    floats = tuple((item.astype(jnp.float32) for item in (inputs, conv_weight, norm_gain, norm_shift, up_weight, up_bias, down_weight, down_bias)))

    def forward(source, kernel, gain_vec, shift_vec, w_up, b_up, w_down, b_down):
        masked = source * usable
        padded = jnp.pad(masked, ((0, 0), (half_width, half_width), (half_width, half_width), (0, 0)))
        convolved = jnp.zeros(masked.shape, jnp.float32)
        for row_tap in range(KS):
            for col_tap in range(KS):
                convolved = convolved + padded[:, row_tap:row_tap + SIDE, col_tap:col_tap + SIDE, :] * kernel[row_tap, col_tap]
        ocean_count = jnp.sum(usable)
        channel_mean = lax.optimization_barrier(jnp.sum(usable * convolved, axis=(0, 1, 2))) / ocean_count
        second = lax.optimization_barrier(jnp.sum(usable * convolved * convolved, axis=(0, 1, 2))) / ocean_count
        inv_std = lax.rsqrt(second - channel_mean * channel_mean + EPSILON)
        normed = low(gain_vec * (convolved - channel_mean) * inv_std + shift_vec)
        flat = normed.reshape(CROPS, SIDE * SIDE, C)

        def feed_forward(block_rows):
            preact = low_back(jnp.dot(block_rows, w_up, precision=HIGH) + b_up)
            hidden = low(gelu_exact(preact))
            return jnp.dot(hidden, w_down, precision=HIGH)
        branch = lax.map(jax.checkpoint(feed_forward), flat).reshape(masked.shape)
        return usable * (source + low_back(branch) + b_down)
    output, pullback = jax.vjp(forward, *floats)
    gradients = pullback(cotangent.astype(jnp.float32))
    return (output.astype(jnp.bfloat16), gradients[0].astype(jnp.bfloat16), gradients[1], gradients[2], gradients[3], gradients[4], gradients[5], gradients[6], gradients[7])
```

```python
import functools

import jax
import jax.numpy as jnp
import numpy as np
from jax import lax
from jax.experimental import pallas as pl
from jax.experimental.pallas import tpu as pltpu
from jax.sharding import Mesh
from jax.sharding import PartitionSpec as P

F32 = jnp.float32
BF = jnp.bfloat16
EPSILON = 1e-05
INV_ROOT_TWO_PI = 0.3989422804014327
LANES = 128
LEFT = 8
MIB = 2**20
TILE = 256


def ceil_to(value, unit):
    return -(-value // unit) * unit


def lane_tiles(width):
    return -(-width // LANES)


def spread_rows(rows):
    count, width = rows.shape
    tiles = lane_tiles(width)
    flat = jnp.pad(rows.astype(F32), ((0, 0), (0, tiles * LANES - width)))
    flat = flat.reshape(count, tiles, 1, LANES).transpose(1, 0, 2, 3)
    return jnp.broadcast_to(flat, (tiles, count, 8, LANES))


def after(*values):
    return lax.optimization_barrier(values)


def params(mib, **more):
    return pltpu.CompilerParams(vmem_limit_bytes=mib * MIB, **more)


def cost(micros):
    return pl.CostEstimate(flops=int(micros * 1.15e9), bytes_accessed=0, transcendentals=0)


def clear_borders(dst, half, side):
    tiles, _, cols, _ = dst.shape
    for t in range(tiles):
        for r in list(range(half)) + list(range(half + side, side + 2 * half)):
            dst[t, r] = jnp.zeros((cols, LANES), F32)

        @pl.loop(0, side)
        def _(r):
            dst[t, r + half, 0:LEFT, :] = jnp.zeros((LEFT, LANES), F32)
            dst[t, r + half, LEFT + side : cols, :] = jnp.zeros((cols - LEFT - side, LANES), F32)


def fill_masked(dst, x_ref, m_ref, half):
    _, side, _, width = x_ref.shape
    for t in range(lane_tiles(width)):
        lo, hi = t * LANES, min((t + 1) * LANES, width)

        @pl.loop(0, side)
        def _(r):
            value = x_ref[0, r, :, lo:hi].astype(F32) * m_ref[0, r, :, : hi - lo].astype(F32)
            dst[t, r + half, LEFT : LEFT + side, 0 : hi - lo] = value


def conv_rows(src, w_ref, t, r0, c0, rows, groups, taps, flipped):
    half = taps // 2
    acc = [jnp.zeros((groups, 8, LANES), F32) for _ in range(rows)]
    for b in range(taps):
        shift = (taps - 1 - b) if flipped else b
        weights = [w_ref[t, a * taps + b] for a in range(taps)]
        for i in range(rows + taps - 1):
            x = src[t, r0 + i, pl.ds(LEFT + c0 + shift - half, groups * 8), :].reshape(groups, 8, LANES)
            for r in range(max(0, i - taps + 1), min(rows, i + 1)):
                a = taps - 1 - (i - r) if flipped else i - r
                acc[r] = acc[r] + x * weights[a][None]
    return acc


def forward_kernel(x_ref, m_ref, w_ref, conv_ref, stat_ref, xs, *, taps, rows, groups):
    _, side, _, width = x_ref.shape
    parts = conv_ref.shape[0]
    half = taps // 2
    clear_borders(xs, half, side)
    fill_masked(xs, x_ref, m_ref, half)
    for t in range(lane_tiles(width)):
        lo, hi = t * LANES, min((t + 1) * LANES, width)

        def block(i, carry):
            first, second = carry
            r0 = i * rows
            for c0 in range(0, side, groups * 8):
                acc = conv_rows(xs, w_ref, t, r0, c0, rows, groups, taps, False)
                for r in range(rows):
                    m = m_ref[0, r0 + r, c0 : c0 + groups * 8, :].astype(F32).reshape(groups, 8, LANES)
                    cm = acc[r] * m
                    first = first + jnp.sum(cm, axis=0)
                    second = second + jnp.sum(cm * acc[r], axis=0)
                    if rows % parts == 0:
                        part, row = r % parts, i * (rows // parts) + r // parts
                    else:
                        part, row = lax.rem(r0 + r, parts), lax.div(r0 + r, parts)
                    conv_ref[part, 0, row, c0 : c0 + groups * 8, lo:hi] = acc[r].reshape(groups * 8, LANES)[:, : hi - lo]
            return first, second

        zero = jnp.zeros((8, LANES), F32)
        first, second = lax.fori_loop(0, side // rows, block, (zero, zero))
        stat_ref[0, 0, t] = first
        stat_ref[0, 1, t] = second


def conv_forward(x, lane_mask, wide_taps, taps, parts, rows=12, groups=2):
    crops, side, _, width = x.shape
    tiles, half = lane_tiles(width), taps // 2
    return pl.pallas_call(
        functools.partial(forward_kernel, taps=taps, rows=rows, groups=groups),
        grid=(crops,),
        in_specs=[
            pl.BlockSpec((1, side, side, width), lambda n: (n, 0, 0, 0)),
            pl.BlockSpec((1, side, side, LANES), lambda n: (n, 0, 0, 0)),
            pl.BlockSpec(wide_taps.shape, lambda n: (0, 0, 0, 0)),
        ],
        out_specs=[
            pl.BlockSpec((parts, 1, side // parts, side, width), lambda n: (0, n, 0, 0, 0)),
            pl.BlockSpec((1, 2, tiles, 8, LANES), lambda n: (n, 0, 0, 0, 0)),
        ],
        out_shape=[
            jax.ShapeDtypeStruct((parts, crops, side // parts, side, width), F32),
            jax.ShapeDtypeStruct((crops, 2, tiles, 8, LANES), F32),
        ],
        scratch_shapes=[pltpu.VMEM((tiles, side + 2 * half, LEFT + side + 8, LANES), F32)],
        compiler_params=params(32),
        cost_estimate=cost(22),
        name="depthwise_forward",
    )(x, lane_mask, wide_taps)


def chooser(slot_of_cell, start, count):
    cells = slot_of_cell.shape[1]
    rows = lax.broadcasted_iota(jnp.int32, (count, cells), 0) + start
    return jnp.where(rows == slot_of_cell, 1.0, 0.0).astype(BF)


def nt(left, right):
    return lax.dot_general(left, right, (((1,), (1,)), ((), ())), preferred_element_type=F32)


def nn(left, right):
    return jnp.dot(left, right, preferred_element_type=F32)


def segments(base, over):
    return [
        (is_over, lo, lo + (base if is_over else 0), min(TILE, n - lo))
        for is_over, n in ((0, base), (1, over))
        for lo in range(0, n, TILE)
    ]


def pack_columns(k, values, slots, used, base_refs, over_refs):
    base, over = base_refs[0].shape[1], over_refs[0].shape[1]
    width = values.shape[0]
    for is_over, lo, start, count in segments(base, over):
        for j, ref in enumerate(over_refs if is_over else base_refs):

            @pl.when((k == j) & (start < used))
            def _():
                ref[:width, lo : lo + count] = nt(values, chooser(slots, start, count)).astype(BF)

            @pl.when((k == j) & (start >= used))
            def _():
                ref[:width, lo : lo + count] = jnp.zeros((width, count), BF)

            if width < ref.shape[0]:

                @pl.when(k == j)
                def _():
                    ref[width:, lo : lo + count] = jnp.zeros((ref.shape[0] - width, count), BF)


def packed_shapes(parts, width, base, over):
    wide = ceil_to(width, 8)
    specs = [pl.BlockSpec((wide, n), lambda k, at: (0, 0)) for n in (base, over) for _ in range(parts)]
    return specs, [jax.ShapeDtypeStruct((wide, n), BF) for n in (base, over) for _ in range(parts)]


def pack_normed_kernel(at_ref, conv_ref, vec_ref, slot_ref, *out_refs):
    k = pl.program_id(0)
    parts = len(out_refs) // 2
    normed = (conv_ref[0] * vec_ref[0:1, :] + vec_ref[1:2, :]).T.astype(BF)
    used = at_ref[1 + lax.rem(at_ref[0] + k, parts)]
    pack_columns(k, normed, slot_ref[0], used, out_refs[:parts], out_refs[parts:])


def pack_normed(at, conv, vec, slots, base, over):
    parts, cells, width = conv.shape
    part = lambda k, at: (lax.rem(at[0] + k, parts), 0, 0)
    specs, shapes = packed_shapes(parts, width, base, over)
    out = pl.pallas_call(
        pack_normed_kernel,
        grid_spec=pltpu.PrefetchScalarGridSpec(
            num_scalar_prefetch=1,
            grid=(parts,),
            in_specs=[
                pl.BlockSpec((1, cells, width), part),
                pl.BlockSpec(vec.shape, lambda k, at: (0, 0)),
                pl.BlockSpec((1, 1, cells), part),
            ],
            out_specs=specs,
        ),
        out_shape=shapes,
        compiler_params=params(32),
        cost_estimate=cost(8),
        name="pack_normed",
    )(at, conv, vec, slots)
    return out[:parts], out[parts:]


def pack_cotangent_kernel(at_ref, cot_ref, m_ref, slot_ref, *refs):
    out_refs, sum_ref, rows = refs[:-2], refs[-2], refs[-1]
    parts = len(out_refs) // 2
    crops, side, _, width = cot_ref.shape
    per = side // parts
    k = pl.program_id(0)
    part = lax.rem(at_ref[0] + k, parts)
    total = jnp.zeros((8, width), F32)
    for n in range(crops):

        def body(i, total):
            r = i * parts + part
            masks = [m_ref[n, r, :, : min(LANES, width - lo)] for lo in range(0, width, LANES)]
            mask = jnp.concatenate(masks, axis=1) if len(masks) > 1 else masks[0]
            value = cot_ref[n, r].astype(F32) * mask.astype(F32)
            rows[pl.ds(pl.multiple_of((n * per + i) * side, 8), side), :] = value
            return total + jnp.sum(value.reshape(side // 8, 8, width), axis=0)

        total = lax.fori_loop(0, per, body, total)

    @pl.when(k == 0)
    def _():
        sum_ref[...] = total

    @pl.when(k > 0)
    def _():
        sum_ref[...] += total

    pack_columns(k, rows[...].T.astype(BF), slot_ref[0], at_ref[1 + part], out_refs[:parts], out_refs[parts:])


def pack_cotangent(at, cot, lane_mask, slots, base, over):
    crops, side, _, width = cot.shape
    parts, _, cells = slots.shape
    specs, shapes = packed_shapes(parts, width, base, over)
    *out, sums = pl.pallas_call(
        pack_cotangent_kernel,
        grid_spec=pltpu.PrefetchScalarGridSpec(
            num_scalar_prefetch=1,
            grid=(parts,),
            in_specs=[
                pl.BlockSpec(cot.shape, lambda k, at: (0, 0, 0, 0)),
                pl.BlockSpec(lane_mask.shape, lambda k, at: (0, 0, 0, 0)),
                pl.BlockSpec((1, 1, cells), lambda k, at: (lax.rem(at[0] + k, parts), 0, 0)),
            ],
            out_specs=specs + [pl.BlockSpec((8, width), lambda k, at: (0, 0))],
            scratch_shapes=[pltpu.VMEM((cells, width), F32)],
        ),
        out_shape=shapes + [jax.ShapeDtypeStruct((8, width), F32)],
        compiler_params=params(40),
        cost_estimate=cost(10),
        name="pack_cotangent",
    )(at, cot, lane_mask, slots)
    return out[:parts], out[parts:], sums


def expand(base_ref, over_ref, slot_column, used, acc):
    cells, width = acc.shape
    acc[...] = jnp.zeros_like(acc)
    for is_over, lo, start, count in segments(base_ref.shape[1], over_ref.shape[1]):
        ref = over_ref if is_over else base_ref

        @pl.when(start < used)
        def _():
            lanes = lax.broadcasted_iota(jnp.int32, (cells, LANES), 1) + start
            choice = jnp.concatenate(
                [jnp.where(lanes + j == slot_column, 1.0, 0.0).astype(BF) for j in range(0, count, LANES)], axis=1
            )
            acc[...] += nt(choice, ref[:width, lo : lo + count])


def output_kernel(at_ref, x_ref, m_ref, bias_ref, column_ref, *refs):
    piece_refs, out_ref, acc = refs[:-2], refs[-2], refs[-1]
    parts = len(piece_refs) // 2
    _, side, _, width = x_ref.shape
    per = side // parts
    for k in range(parts):
        part = lax.rem(at_ref[0] + k, parts)
        expand(piece_refs[k], piece_refs[parts + k], column_ref[part, 0], at_ref[1 + part], acc)

        @pl.loop(0, per)
        def _(i):
            r = i * parts + part
            start = pl.multiple_of(i * side, 8)
            for lo in range(0, width, LANES):
                hi = min(lo + LANES, width)
                value = x_ref[0, r, :, lo:hi].astype(F32) + acc[pl.ds(start, side), lo:hi] + bias_ref[0:1, lo:hi]
                out_ref[0, r, :, lo:hi] = (m_ref[0, r, :, : hi - lo].astype(F32) * value).astype(BF)


def make_output(at, x, lane_mask, bias, columns, pieces):
    parts = len(pieces) // 2
    crops, side, _, width = x.shape
    cells = side * side // parts
    field = pl.BlockSpec((1, side, side, width), lambda n, at: (n, 0, 0, 0))
    return pl.pallas_call(
        output_kernel,
        grid_spec=pltpu.PrefetchScalarGridSpec(
            num_scalar_prefetch=1,
            grid=(crops,),
            in_specs=[
                field,
                pl.BlockSpec((1, side, side, LANES), lambda n, at: (n, 0, 0, 0)),
                pl.BlockSpec((1, width), lambda n, at: (0, 0)),
                pl.BlockSpec((parts, 1, cells, LANES), lambda n, at: (0, n, 0, 0)),
            ]
            + [pl.BlockSpec(p.shape, lambda n, at: (0, 0)) for p in pieces],
            out_specs=field,
            scratch_shapes=[pltpu.VMEM((cells, width), F32)],
        ),
        out_shape=jax.ShapeDtypeStruct(x.shape, BF),
        compiler_params=params(40),
        cost_estimate=cost(12),
        name="make_output",
    )(at, x, lane_mask, bias, columns, *pieces)


def backward_kernel(
    at_ref, x_ref, m_ref, cot_ref, conv_ref, w_ref, v_ref, column_ref, *refs, taps, rows, groups, rows2, groups2
):
    piece_refs, dx_ref, dw_ref, xs, gs, acc_ref = refs[:-5], refs[-5], refs[-4], refs[-3], refs[-2], refs[-1]
    parts = len(piece_refs) // 2
    _, side, _, width = x_ref.shape
    per = side // parts
    half = taps // 2

    @pl.when(pl.program_id(0) == 0)
    def _():
        dw_ref[...] = jnp.zeros_like(dw_ref)

    clear_borders(xs, half, side)
    clear_borders(gs, half, side)
    fill_masked(xs, x_ref, m_ref, half)
    for k in range(parts):
        part = lax.rem(at_ref[0] + k, parts)
        expand(piece_refs[k], piece_refs[parts + k], column_ref[part, 0], at_ref[1 + part], acc_ref)

        @pl.loop(0, per)
        def _(i):
            r = i * parts + part
            start = pl.multiple_of(i * side, 8)
            for t in range(lane_tiles(width)):
                lo, hi = t * LANES, min((t + 1) * LANES, width)
                n = hi - lo
                shape = (side // 8, 8, n)
                m = m_ref[0, r, :, :n].astype(F32).reshape(shape)
                centred = conv_ref[part, 0, i, :, lo:hi].reshape(shape) - v_ref[t, 0, :, :n][None]
                gn = acc_ref[pl.ds(start, side), lo:hi].reshape(shape)
                g = v_ref[t, 1, :, :n][None] * gn - m * (v_ref[t, 2, :, :n][None] + centred * v_ref[t, 3, :, :n][None])
                gs[t, r + half, LEFT : LEFT + side, 0:n] = g.reshape(side, n)

    for t in range(lane_tiles(width)):
        lo, hi = t * LANES, min((t + 1) * LANES, width)
        n = hi - lo

        @pl.loop(0, side // rows)
        def _(i):
            r0 = i * rows
            for c0 in range(0, side, groups * 8):
                acc = conv_rows(gs, w_ref, t, r0, c0, rows, groups, taps, True)
                for r in range(rows):
                    m = m_ref[0, r0 + r, c0 : c0 + groups * 8, :n].astype(F32)
                    cot = cot_ref[0, r0 + r, c0 : c0 + groups * 8, lo:hi].astype(F32)
                    value = m * (cot + acc[r].reshape(groups * 8, LANES)[:, :n])
                    dx_ref[0, r0 + r, c0 : c0 + groups * 8, lo:hi] = value.astype(BF)

        @pl.loop(0, side // rows2)
        def _(i):
            r0 = i * rows2
            for c0 in range(0, side, groups2 * 8):
                span = groups2 * 8
                grads = [
                    gs[t, r0 + half + r, LEFT + c0 : LEFT + c0 + span, :].reshape(groups2, 8, LANES)
                    for r in range(rows2)
                ]
                for b in range(taps):
                    acc = [jnp.zeros((groups2, 8, LANES), F32) for _ in range(taps)]
                    for j in range(rows2 + taps - 1):
                        x = xs[t, r0 + j, pl.ds(LEFT + c0 + b - half, span), :].reshape(groups2, 8, LANES)
                        for r in range(max(0, j - taps + 1), min(rows2, j + 1)):
                            acc[j - r] = acc[j - r] + x * grads[r]
                    for a in range(taps):
                        dw_ref[t, a * taps + b] += jnp.sum(acc[a], axis=0)


def conv_backward(
    at, x, lane_mask, cot, conv, wide_taps, vectors, columns, pieces, taps, rows=12, groups=2, rows2=8, groups2=2
):
    parts = len(pieces) // 2
    crops, side, _, width = x.shape
    tiles, half = lane_tiles(width), taps // 2
    cells = side * side // parts
    field = pl.BlockSpec((1, side, side, width), lambda n, at: (n, 0, 0, 0))
    padded = pltpu.VMEM((tiles, side + 2 * half, LEFT + side + 8, LANES), F32)
    return pl.pallas_call(
        functools.partial(
            backward_kernel, taps=taps, rows=rows, groups=groups, rows2=rows2, groups2=groups2
        ),
        grid_spec=pltpu.PrefetchScalarGridSpec(
            num_scalar_prefetch=1,
            grid=(crops,),
            in_specs=[
                field,
                pl.BlockSpec((1, side, side, LANES), lambda n, at: (n, 0, 0, 0)),
                field,
                pl.BlockSpec((parts, 1, side // parts, side, width), lambda n, at: (0, n, 0, 0, 0)),
                pl.BlockSpec(wide_taps.shape, lambda n, at: (0, 0, 0, 0)),
                pl.BlockSpec(vectors.shape, lambda n, at: (0, 0, 0, 0)),
                pl.BlockSpec((parts, 1, cells, LANES), lambda n, at: (0, n, 0, 0)),
            ]
            + [pl.BlockSpec(p.shape, lambda n, at: (0, 0)) for p in pieces],
            out_specs=[field, pl.BlockSpec(wide_taps.shape, lambda n, at: (0, 0, 0, 0))],
            scratch_shapes=[padded, padded, pltpu.VMEM((cells, width), F32)],
        ),
        out_shape=[jax.ShapeDtypeStruct(x.shape, BF), jax.ShapeDtypeStruct(wide_taps.shape, F32)],
        compiler_params=params(52),
        cost_estimate=cost(50),
        name="depthwise_backward",
    )(at, x, lane_mask, cot, conv, wide_taps, vectors, columns, *pieces)


def gelu_pair(value):
    size = jnp.abs(value)
    t = 1.0 / (1.0 + 0.23164189 * size)
    bell = jnp.exp(-0.5 * value * value)
    poly = 0.530702715
    for term in (-0.7265760135, 0.7107068705, -0.142248368, 0.127414796):
        poly = poly * t + term
    tail = poly * t * bell
    below = jnp.where(value >= 0, 1.0 - tail, tail)
    return value * below, below + value * bell * INV_ROOT_TWO_PI


def pointwise_kernel(at_ref, *refs, chips, parts, width, base, over):
    up_refs, down_refs = refs[:chips], refs[chips : 2 * chips]
    data, rest = refs[2 * chips : 2 * chips + 8], refs[2 * chips + 8 :]
    outs, (weight_grad_ref, sums_ref) = rest[:8], rest[8:10]
    up_w, down_w, up_t, down_t, up_acc, down_acc, x_place, g_place, hidden, grad_pre = rest[10:]
    whose, c = pl.program_id(0), pl.program_id(1)
    last = (whose == 1) & (c == pl.num_programs(1) - 1)
    _, slab, wide = up_refs[0].shape
    units = chips * parts * slab
    channels = parts * width
    block = units // 4
    me, chip = at_ref[0], at_ref[1 + 2 * parts]
    used = at_ref[1 + whose * parts + me]

    @pl.when((whose == 0) & (c == 0))
    def _():
        for refs, dst in ((up_refs, up_w), (down_refs, down_w)):
            for p in range(chips):
                for q in range(0, parts, 2):
                    pair = jnp.concatenate([refs[p][q].astype(F32), refs[p][q + 1].astype(F32)], axis=0)
                    row = (p * parts + q) * slab
                    dst[row : row + 2 * slab, :] = pair.astype(BF)
        for u in range(0, units, LANES):
            for src, dst in ((up_w, up_t), (down_w, down_t)):
                dst[:, u : u + LANES] = src[u : u + LANES, :].astype(F32).T[:channels, :].astype(BF)
        up_acc[...] = jnp.zeros_like(up_acc)
        down_acc[...] = jnp.zeros_like(down_acc)
        sums_ref[...] = jnp.zeros_like(sums_ref)
        ones = jnp.where(lax.broadcasted_iota(jnp.int32, (8, TILE), 0) == 0, 1.0, 0.0)
        x_place[channels:, :] = ones
        g_place[channels:, :] = jnp.zeros((8, TILE), F32)

    def spots(step):
        first, end = step * TILE, (step + 1) * TILE
        found = []
        if first < base:
            n = min(end, base) - first
            found.append((0, slice(0, n), slice(0, n)))
        if end > base and first < base + over:
            lo, hi = max(first, base), min(end, base + over)
            found.append((1, slice(lo - base, hi - base), slice(lo - first, hi - first)))
        return found

    whole = base // TILE
    steps = -(-(base + over) // TILE)
    cases = ([(c < whole, spots(0))] if whole else []) + [(c == step, spots(step)) for step in range(whole, steps)]
    for side in range(2):
        for case, found in cases:
            here = (whose == side) & case
            x_refs, g_refs = data[2 * side : 2 * side + 2], data[4 + 2 * side : 6 + 2 * side]

            @pl.when(here & (c * TILE < used))
            def _():
                for refs, place in ((x_refs, x_place), (g_refs, g_place)):
                    for k in range(parts):
                        at = pl.ds(pl.multiple_of(lax.rem(me - k + parts, parts) * width, 8), width)
                        values = [refs[is_over][k, :, lanes].astype(F32) for is_over, lanes, _ in found]
                        filled = sum(v.shape[1] for v in values)
                        if filled < TILE:
                            values.append(jnp.zeros((width, TILE - filled), F32))
                        place[at, :] = jnp.concatenate(values, axis=1) if len(values) > 1 else values[0]

            @pl.when(here & (c * TILE >= used))
            def _():
                for is_over, lanes, _ in found:
                    for ref in (outs[2 * side + is_over], outs[4 + 2 * side + is_over]):
                        ref[:, :, lanes] = jnp.zeros((parts, width, lanes.stop - lanes.start), ref.dtype)

    @pl.when(c * TILE < used)
    def _():
        x = x_place[...].astype(BF)
        g = g_place[...].astype(BF)

        @pl.loop(0, units // block)
        def _(i):
            at = pl.ds(pl.multiple_of(i * block, 16), block)
            pre = nn(up_w[at, :], x)
            grad_hidden = nn(down_w[at, :], g)
            value, slope = gelu_pair(pre)
            h = value.astype(BF)
            gp = (grad_hidden * slope).astype(BF)
            hidden[at, :] = h
            grad_pre[at, :] = gp
            up_acc[at, :] += nt(gp, x)
            down_acc[at, :] += nt(h, g)

        def fold(v):
            return sum(v[:, lo : lo + LANES] for lo in range(0, TILE, LANES))

        for s in range(parts):
            rows = slice(s * width, (s + 1) * width)
            k = lax.rem(me - s + parts, parts)
            branch = nn(down_t[rows, :], hidden[...])
            normed = nn(up_t[rows, :], grad_pre[...])
            sums_ref[0, rows, :] += fold(normed)
            sums_ref[1, rows, :] += fold(normed * x_place[rows, :])
            for side in range(2):
                for case, found in cases:

                    @pl.when((whose == side) & case)
                    def _():
                        for is_over, lanes, tile in found:
                            to = 2 * side + is_over
                            for value, ref in ((branch, outs[to]), (normed, outs[4 + to])):
                                ref[k, :, lanes] = value[:, tile].astype(ref.dtype)

    @pl.when(last)
    def _():
        for p in range(chips):
            for q in range(parts):
                row = (p * parts + q) * slab
                to = (chip ^ p, lax.rem(me - q + parts, parts))
                weight_grad_ref[to[0], to[1], 0] = up_acc[row : row + slab, :].astype(BF)
                weight_grad_ref[to[0], to[1], 1] = down_acc[row : row + slab, :].astype(BF)


def pointwise(at, ups, downs, data):
    chips = len(ups)
    parts, width, base = data[0].shape
    over = data[1].shape[2]
    _, slab, wide = ups[0].shape
    units, channels = chips * parts * slab, parts * width
    base_tiles = -(-base // TILE)

    def tile(side, is_over):
        if is_over:
            return pl.BlockSpec((parts, width, over), lambda whose, c, at: (0, 0, 0))

        def place(whose, c, at):
            return (0, 0, jnp.where(whose == side, jnp.minimum(c, base_tiles - 1), 0 if side else base_tiles - 1))

        return pl.BlockSpec((parts, width, TILE), place)

    tiles = [tile(side, is_over) for side in range(2) for is_over in range(2)]
    kinds = [F32, F32, BF, BF]
    result = [jax.ShapeDtypeStruct((parts, width, n), kind) for n, kind in zip((base, over, base, over), kinds)]
    return pl.pallas_call(
        functools.partial(pointwise_kernel, chips=chips, parts=parts, width=width, base=base, over=over),
        grid_spec=pltpu.PrefetchScalarGridSpec(
            num_scalar_prefetch=1,
            grid=(2, -(-(base + over) // TILE)),
            in_specs=[
                pl.BlockSpec(ups[0].shape, lambda w, c, at: (0, 0, 0), pipeline_mode=pl.Buffered(1))
                for _ in range(2 * chips)
            ]
            + tiles
            + tiles,
            out_specs=tiles
            + tiles
            + [
                pl.BlockSpec((chips, parts, 2, slab, wide), lambda w, c, at: (0, 0, 0, 0, 0)),
                pl.BlockSpec((2, channels, LANES), lambda w, c, at: (0, 0, 0)),
            ],
            scratch_shapes=[
                pltpu.VMEM((units, wide), BF),
                pltpu.VMEM((units, wide), BF),
                pltpu.VMEM((channels, units), BF),
                pltpu.VMEM((channels, units), BF),
                pltpu.VMEM((units, wide), F32),
                pltpu.VMEM((units, wide), F32),
                pltpu.VMEM((wide, TILE), F32),
                pltpu.VMEM((wide, TILE), F32),
                pltpu.VMEM((units, TILE), BF),
                pltpu.VMEM((units, TILE), BF),
            ],
        ),
        out_shape=result
        + result
        + [
            jax.ShapeDtypeStruct((chips, parts, 2, slab, wide), BF),
            jax.ShapeDtypeStruct((2, channels, LANES), F32),
        ],
        compiler_params=params(62),
        cost_estimate=cost(70),
        name="pointwise",
    )(at, *ups, *downs, *data)


def per_device(
    inputs,
    crop_sizes,
    land_mask,
    conv_weight,
    norm_gain,
    norm_shift,
    up_weight,
    up_bias,
    down_weight,
    down_bias,
    cotangent,
    *,
    sizes,
):
    chips, cores, parts = sizes
    crops, side, _, width = inputs.shape
    taps = conv_weight.shape[0]
    cells = crops * side * side // parts
    local_units = up_weight.shape[1]
    channels = up_weight.shape[0]
    me = lax.axis_index("mp")
    core = lax.axis_index("core")
    chip = lax.axis_index("xy")

    def ring(k):
        return [(i, (i + k) % parts) for i in range(parts)]

    def everywhere(value, axes):
        for axis in axes:
            size = {"xy": chips, "core": cores, "mp": parts}[axis]
            step = 1
            while step < size:
                value = value + lax.ppermute(value, axis, [(i, i ^ step) for i in range(size)])
                step *= 2
        return value

    def ring_back(k):
        return [(i, (i - k) % parts) for i in range(parts)]

    def to_parts(pieces, ring=ring):
        return [pieces[0]] + [lax.ppermute(pieces[k], "mp", ring(k)) for k in range(1, parts)]

    swap = [(i, cores - 1 - i) for i in range(cores)]

    def to_core(value):
        return lax.ppermute(value, "core", swap)

    share = -(-local_units // (chips * cores))
    slab = ceil_to(share, 8)
    wide_width = ceil_to(width, 8)
    wide = parts * wide_width + 8
    rank = chip * cores + core
    spare = chips * cores * share - local_units

    def take(rows):
        rows = jnp.pad(rows, ((0, spare), (0, 0))) if spare else rows
        rows = lax.dynamic_slice_in_dim(rows, rank * share, share, axis=0)
        if wide_width > width:
            rows = jnp.pad(rows.reshape(share, parts, width), ((0, 0), (0, 0), (0, wide_width - width)))
        return rows.reshape(share, -1)

    own_bias = up_bias[:, None]
    own_bias = jnp.pad(own_bias, ((0, spare), (0, 0))) if spare else own_bias
    own_bias = lax.dynamic_slice_in_dim(own_bias, rank * share, share, axis=0)
    up_rows = jnp.pad(jnp.concatenate([take(up_weight.T), own_bias], axis=1), ((0, slab - share), (0, 7)))
    down_rows = jnp.pad(take(down_weight), ((0, slab - share), (0, 8)))
    rows = to_parts([jnp.stack([up_rows, down_rows])] * parts)

    def over_plane(own, bits):
        held = {0: own}
        for bit in bits:
            pairs = [(i, i ^ bit) for i in range(chips)]
            held.update({p ^ bit: lax.ppermute(value, "xy", pairs) for p, value in list(held.items())})
        return [held[p] for p in range(chips)]

    index = jnp.arange(side, dtype=jnp.int32)
    inside = (index[None, :, None] < crop_sizes[:, 0][:, None, None]) & (
        index[None, None, :] < crop_sizes[:, 1][:, None, None]
    )
    usable = jnp.where(inside, land_mask, 0)
    lane_mask = jnp.broadcast_to(usable[..., None].astype(BF), usable.shape + (LANES,))
    by_part = usable.reshape(crops, side // parts, parts, side).transpose(2, 0, 1, 3).reshape(parts, -1, side)
    by_part = by_part.astype(F32)
    lines = by_part.shape[1]
    upto = jnp.dot(by_part, jnp.triu(jnp.ones((side, side), F32)))
    before = jnp.dot(upto[:, :, -1], jnp.triu(jnp.ones((lines, lines), F32), 1))
    slots = jnp.where(by_part > 0, upto + before[:, :, None] - 1, -1).astype(jnp.int32)
    counts = jnp.sum(by_part, axis=(1, 2)).astype(jnp.int32)
    columns = jnp.broadcast_to(slots.reshape(parts, crops, -1)[..., None], (parts, crops, cells // crops, LANES))
    slots = slots.reshape(parts, 1, cells)
    at = jnp.concatenate([me[None].astype(jnp.int32), counts, to_core(counts), chip[None].astype(jnp.int32)])

    base = ceil_to(cells * 7 // 9, LANES)
    over = ceil_to(cells, LANES) - base
    crowded = jnp.where(jnp.max(counts) > base, 1.0, 0.0)

    cot_base, cot_over, down_bias_local = pack_cotangent(at, cotangent, lane_mask, slots, base, over)
    inputs, *cot_base = after(inputs, *cot_base)

    wide_taps = spread_rows(conv_weight.reshape(taps * taps, width))
    convolved, stats = conv_forward(inputs, lane_mask, wide_taps, taps, parts)
    stats, *rows = after(stats, *rows)
    grad_pieces = to_parts(cot_base)
    bits = [1 << j for j in range(chips.bit_length() - 1)]

    def double(held, bit):
        pairs = [(i, i ^ bit) for i in range(chips)]
        return {**held, **{p ^ bit: lax.ppermute(value, "xy", pairs) for p, value in held.items()}}

    ups, downs = {0: jnp.stack([r[0] for r in rows])}, {0: jnp.stack([r[1] for r in rows])}
    ups, downs = double(ups, bits[0]), double(downs, bits[-1])
    stats = jnp.sum(stats, axis=(0, 3)).reshape(2, -1)[:, :width]
    extra = jnp.pad(jnp.stack([jnp.sum(by_part), crowded])[None], ((0, 0), (0, width - 2)))
    stats = everywhere(jnp.concatenate([stats, extra, jnp.sum(down_bias_local, axis=0)[None]]), ("core", "xy"))
    ocean_count = stats[2, 0]
    overflows = stats[2, 1] > 0
    down_bias_grad = stats[3]
    channel_mean = stats[0] / ocean_count
    inv_std = lax.rsqrt(stats[1] / ocean_count - channel_mean * channel_mean + EPSILON)
    gain = norm_gain.astype(F32)
    shift = norm_shift.astype(F32)
    scale = gain * inv_std

    affine = jnp.stack([scale, shift - channel_mean * scale])
    places = sorted(ups), sorted(downs)
    convolved, *held = after(convolved, *[ups[p] for p in places[0]], *[downs[p] for p in places[1]])
    ups = dict(zip(places[0], held))
    downs = dict(zip(places[1], held[len(ups) :]))
    for j in range(1, len(bits)):
        ups, downs = double(ups, bits[j]), double(downs, bits[-1 - j])
    ups, downs = [ups[p] for p in range(chips)], [downs[p] for p in range(chips)]
    normed_base, normed_over = pack_normed(at, convolved.reshape(parts, cells, width), affine, slots, base, over)
    *both, = after(*normed_base, *grad_pieces)
    normed_base, grad_base = both[:parts], jnp.stack(both[parts:])
    x_base = jnp.stack(to_parts(normed_base))
    none = jnp.zeros((parts, wide_width, over), BF)

    def overflow_in():
        x, g = jnp.stack(to_parts(normed_over)), jnp.stack(to_parts(cot_over))
        return x, g, to_core(x), to_core(g)

    x_over, g_over, x_far_over, g_far_over = lax.cond(overflows, overflow_in, lambda: (none,) * 4)
    data = [x_base, x_over, to_core(x_base), x_far_over, grad_base, g_over, to_core(grad_base), g_far_over]
    *sums_out, weight_grad, sums = pointwise(at, ups, downs, data)
    branch, normed = list(sums_out[:4]), list(sums_out[4:])

    def home(own, far):
        total = (own + to_core(far).astype(F32)).astype(BF)
        return to_parts([total[k] for k in range(parts)], ring_back)

    normed_base = home(normed[0], normed[2])
    branch[0], branch[2], _ = after(branch[0], branch[2], normed_base[-1])
    branch_base = home(branch[0], branch[2])
    nothing = [jnp.zeros((wide_width, over), BF)] * parts
    branch_over, normed_over = lax.cond(
        overflows, lambda: (home(branch[1], branch[3]), home(normed[1], normed[3])), lambda: (nothing, nothing)
    )

    sums = everywhere(jnp.sum(sums, axis=2), ("core", "xy", "mp"))
    sums = lax.dynamic_slice_in_dim(sums, me * wide_width, wide_width, axis=1)[:, :width]
    shift_grad = sums[0]
    gain_grad = (sums[1] - shift * shift_grad) / gain
    vectors = jnp.stack([channel_mean, scale, scale * shift_grad / ocean_count, scale * inv_std * gain_grad / ocean_count])
    input_grad, taps_local = conv_backward(
        at,
        inputs,
        lane_mask,
        cotangent,
        convolved,
        wide_taps,
        spread_rows(vectors),
        columns,
        [*normed_base, *normed_over],
        taps,
    )
    output = make_output(at, inputs, lane_mask, down_bias.astype(F32)[None], columns, [*branch_base, *branch_over])
    taps_local = jnp.sum(taps_local, axis=2).transpose(1, 0, 2).reshape(taps * taps, -1)
    conv_weight_grad = everywhere(taps_local, ("core", "xy"))[:, :width].reshape(taps, taps, width)

    own = lax.psum_scatter(weight_grad, "xy", scatter_dimension=0, tiled=False)
    own, _ = after(own, taps_local)
    own = lax.psum_scatter(own, "mp", scatter_dimension=0, tiled=False)
    both = lax.all_gather(own, ("xy", "core"), axis=0, tiled=False)
    both = both[:, :, :share].transpose(1, 0, 2, 3).reshape(2, -1, wide)[:, :local_units]
    up_bias_grad = both[0, :, -8].astype(F32)
    both = both[:, :, :-8].reshape(2, local_units, parts, wide_width)[..., :width].reshape(2, local_units, channels)
    up_weight_grad = both[0].T.astype(F32)
    down_weight_grad = both[1].astype(F32)
    return (
        output,
        input_grad,
        conv_weight_grad,
        gain_grad,
        shift_grad,
        up_weight_grad,
        up_bias_grad,
        down_weight_grad,
        down_bias_grad,
    )


def solution(mesh):
    cores = 2
    parts = mesh.shape["mp"]
    chips = mesh.shape["dp"] // cores
    fine = Mesh(np.asarray(mesh.devices).reshape(chips, cores, parts), ("xy", "core", "mp"))
    dp = ("xy", "core")
    specs = (
        P(dp, None, None, "mp"),
        P(dp, None),
        P(dp, None, None),
        P(None, None, "mp"),
        P("mp"),
        P("mp"),
        P(None, "mp"),
        P("mp"),
        P("mp", None),
        P("mp"),
        P(dp, None, None, "mp"),
    )
    results = (
        P(dp, None, None, "mp"),
        P(dp, None, None, "mp"),
        P(None, None, "mp"),
        P("mp"),
        P("mp"),
        P(None, "mp"),
        P("mp"),
        P("mp", None),
        P("mp"),
    )
    return jax.shard_map(
        functools.partial(per_device, sizes=(chips, cores, parts)),
        mesh=fine,
        in_specs=specs,
        out_specs=results,
        check_vma=False,
    )
```

```python
import functools

import jax
import jax.numpy as jnp
import numpy as np
from jax import lax
from jax.experimental import pallas as pl
from jax.experimental.pallas import tpu as pltpu
from jax.sharding import Mesh
from jax.sharding import PartitionSpec as P

F32 = jnp.float32
BF = jnp.bfloat16
EPSILON = 1e-05
INV_ROOT_TWO_PI = 0.3989422804014327
LANES = 128
LEFT = 8
MIB = 2**20
TILE = 256


def ceil_to(value, unit):
    return -(-value // unit) * unit


def lane_tiles(width):
    return -(-width // LANES)


def spread_rows(rows):
    count, width = rows.shape
    tiles = lane_tiles(width)
    flat = jnp.pad(rows.astype(F32), ((0, 0), (0, tiles * LANES - width)))
    flat = flat.reshape(count, tiles, 1, LANES).transpose(1, 0, 2, 3)
    return jnp.broadcast_to(flat, (tiles, count, 8, LANES))


def after(*values):
    return lax.optimization_barrier(values)


def params(mib, **more):
    return pltpu.CompilerParams(vmem_limit_bytes=mib * MIB, **more)


def whole(array):
    zeros = (0,) * array.ndim
    return pl.BlockSpec(array.shape, lambda n, at: zeros)


EAGERNESS = 6


def cost(micros):
    return pl.CostEstimate(flops=int(micros * 1.15e9 / EAGERNESS), bytes_accessed=0, transcendentals=0)


def clear_borders(dst, half, side):
    tiles, _, cols, _ = dst.shape
    for t in range(tiles):
        for r in list(range(half)) + list(range(half + side, side + 2 * half)):
            dst[t, r] = jnp.zeros((cols, LANES), F32)

        @pl.loop(0, side)
        def _(r):
            dst[t, r + half, 0:LEFT, :] = jnp.zeros((LEFT, LANES), F32)
            dst[t, r + half, LEFT + side : cols, :] = jnp.zeros((cols - LEFT - side, LANES), F32)


def fill_masked(dst, x_ref, m_ref, half):
    _, side, _, width = x_ref.shape
    for t in range(lane_tiles(width)):
        lo, hi = t * LANES, min((t + 1) * LANES, width)

        @pl.loop(0, side)
        def _(r):
            value = x_ref[0, r, :, lo:hi].astype(F32) * m_ref[0, r, :, : hi - lo].astype(F32)
            dst[t, r + half, LEFT : LEFT + side, 0 : hi - lo] = value


def conv_rows(src, w_ref, t, r0, c0, rows, groups, taps, flipped):
    half = taps // 2
    acc = [jnp.zeros((groups, 8, LANES), F32) for _ in range(rows)]
    for b in range(taps):
        shift = (taps - 1 - b) if flipped else b
        weights = [w_ref[t, a * taps + b] for a in range(taps)]
        for i in range(rows + taps - 1):
            x = src[t, r0 + i, pl.ds(LEFT + c0 + shift - half, groups * 8), :].reshape(groups, 8, LANES)
            for r in range(max(0, i - taps + 1), min(rows, i + 1)):
                a = taps - 1 - (i - r) if flipped else i - r
                acc[r] = acc[r] + x * weights[a][None]
    return acc


def forward_kernel(x_ref, m_ref, w_ref, conv_ref, stat_ref, xs, *, taps, rows, groups):
    _, side, _, width = x_ref.shape
    parts = conv_ref.shape[0]
    half = taps // 2
    clear_borders(xs, half, side)
    fill_masked(xs, x_ref, m_ref, half)
    for t in range(lane_tiles(width)):
        lo, hi = t * LANES, min((t + 1) * LANES, width)

        def block(i, carry):
            first, second = carry
            r0 = i * rows
            for c0 in range(0, side, groups * 8):
                acc = conv_rows(xs, w_ref, t, r0, c0, rows, groups, taps, False)
                for r in range(rows):
                    m = m_ref[0, r0 + r, c0 : c0 + groups * 8, :].astype(F32).reshape(groups, 8, LANES)
                    cm = acc[r] * m
                    first = first + jnp.sum(cm, axis=0)
                    second = second + jnp.sum(cm * acc[r], axis=0)
                    if rows % parts == 0:
                        part, row = r % parts, i * (rows // parts) + r // parts
                    else:
                        part, row = lax.rem(r0 + r, parts), lax.div(r0 + r, parts)
                    conv_ref[part, 0, row, c0 : c0 + groups * 8, lo:hi] = acc[r].reshape(groups * 8, LANES)[:, : hi - lo]
            return first, second

        zero = jnp.zeros((8, LANES), F32)
        first, second = lax.fori_loop(0, side // rows, block, (zero, zero))
        stat_ref[0, 0, t] = first
        stat_ref[0, 1, t] = second


def conv_forward(x, lane_mask, wide_taps, taps, parts, rows=12, groups=2):
    crops, side, _, width = x.shape
    tiles, half = lane_tiles(width), taps // 2
    return pl.pallas_call(
        functools.partial(forward_kernel, taps=taps, rows=rows, groups=groups),
        grid=(crops,),
        in_specs=[
            pl.BlockSpec((1, side, side, width), lambda n: (n, 0, 0, 0)),
            pl.BlockSpec((1, side, side, LANES), lambda n: (n, 0, 0, 0)),
            pl.BlockSpec(wide_taps.shape, lambda n: (0, 0, 0, 0)),
        ],
        out_specs=[
            pl.BlockSpec((parts, 1, side // parts, side, width), lambda n: (0, n, 0, 0, 0)),
            pl.BlockSpec((1, 2, tiles, 8, LANES), lambda n: (n, 0, 0, 0, 0)),
        ],
        out_shape=[
            jax.ShapeDtypeStruct((parts, crops, side // parts, side, width), F32),
            jax.ShapeDtypeStruct((crops, 2, tiles, 8, LANES), F32),
        ],
        scratch_shapes=[pltpu.VMEM((tiles, side + 2 * half, LEFT + side + 8, LANES), F32)],
        compiler_params=params(32),
        cost_estimate=cost(22),
        name="depthwise_forward",
    )(x, lane_mask, wide_taps)


def chooser(slot_of_cell, start, count):
    cells = slot_of_cell.shape[1]
    rows = lax.broadcasted_iota(jnp.int32, (count, cells), 0) + start
    return jnp.where(rows == slot_of_cell, 1.0, 0.0).astype(BF)


def nt(left, right):
    return lax.dot_general(left, right, (((1,), (1,)), ((), ())), preferred_element_type=F32)


def nn(left, right):
    return jnp.dot(left, right, preferred_element_type=F32)


def segments(base, over):
    cuts = sorted({*range(0, base + over, TILE), base, base + over})
    return [
        (int(lo >= base), lo - base if lo >= base else lo, lo, hi - lo) for lo, hi in zip(cuts, cuts[1:]) if hi <= base + over
    ]


def pack_columns(values, slots, used, base_ref, over_ref):
    width = values.shape[0]
    for is_over, lo, start, count in segments(base_ref.shape[1], over_ref.shape[1]):
        ref = over_ref if is_over else base_ref

        @pl.when(start < used)
        def _():
            ref[:width, lo : lo + count] = nt(values, chooser(slots, start, count)).astype(BF)

        @pl.when(start >= used)
        def _():
            ref[:width, lo : lo + count] = jnp.zeros((width, count), BF)

        if width < ref.shape[0]:
            ref[width:, lo : lo + count] = jnp.zeros((ref.shape[0] - width, count), BF)


def pack_normed_kernel(at_ref, conv_ref, vec_ref, slot_ref, *out_refs):
    k = pl.program_id(0)
    base_refs, over_ref = out_refs[:-1], out_refs[-1]
    part = lax.rem(at_ref[0] + k, len(base_refs))
    normed = (conv_ref[0] * vec_ref[0:1, :] + vec_ref[1:2, :]).T.astype(BF)
    for j, base_ref in enumerate(base_refs):

        @pl.when(k == j)
        def _():
            pack_columns(normed, slot_ref[0], at_ref[1 + part], base_ref, over_ref.at[part])


def pack_normed(at, conv, vec, slots, base, over):
    parts, cells, width = conv.shape
    wide = ceil_to(width, 8)
    part = lambda k, at: (lax.rem(at[0] + k, parts), 0, 0)
    *pieces, more = pl.pallas_call(
        pack_normed_kernel,
        grid_spec=pltpu.PrefetchScalarGridSpec(
            num_scalar_prefetch=1,
            grid=(parts,),
            in_specs=[
                pl.BlockSpec((1, cells, width), part),
                pl.BlockSpec(vec.shape, lambda k, at: (0, 0)),
                pl.BlockSpec((1, 1, cells), part),
            ],
            out_specs=[pl.BlockSpec((wide, base), lambda k, at: (0, 0))] * parts
            + [pl.BlockSpec((parts, wide, over), lambda k, at: (0, 0, 0))],
        ),
        out_shape=[jax.ShapeDtypeStruct((wide, base), BF)] * parts + [jax.ShapeDtypeStruct((parts, wide, over), BF)],
        compiler_params=params(32),
        cost_estimate=cost(8),
        name="pack_normed",
    )(at, conv, vec, slots)
    return pieces, more


def pack_cotangent_kernel(at_ref, cot_ref, m_ref, slot_ref, base_ref, over_ref, sum_ref, rows):
    crops, side, _, width = cot_ref.shape
    part, parts = pl.program_id(0), pl.num_programs(0)
    per = rows.shape[0] // (crops * side)
    total = jnp.zeros((8, width), F32)
    for n in range(crops):

        def body(i, total):
            r = i * parts + part
            masks = [m_ref[n, r, :, : min(LANES, width - lo)] for lo in range(0, width, LANES)]
            mask = jnp.concatenate(masks, axis=1) if len(masks) > 1 else masks[0]
            value = cot_ref[n, r].astype(F32) * mask.astype(F32)
            rows[pl.ds(pl.multiple_of((n * per + i) * side, 8), side), :] = value
            return total + jnp.sum(value.reshape(side // 8, 8, width), axis=0)

        total = lax.fori_loop(0, per, body, total)

    @pl.when(part == 0)
    def _():
        sum_ref[...] = total

    @pl.when(part > 0)
    def _():
        sum_ref[...] += total

    pack_columns(rows[...].T.astype(BF), slot_ref[0], at_ref[1 + part], base_ref.at[0], over_ref.at[0])


def pack_cotangent(at, cot, lane_mask, slots, base, over):
    crops, side, _, width = cot.shape
    parts, _, cells = slots.shape
    wide = ceil_to(width, 8)
    return pl.pallas_call(
        pack_cotangent_kernel,
        grid_spec=pltpu.PrefetchScalarGridSpec(
            num_scalar_prefetch=1,
            grid=(parts,),
            in_specs=[
                pl.BlockSpec(cot.shape, lambda k, at: (0, 0, 0, 0)),
                pl.BlockSpec(lane_mask.shape, lambda k, at: (0, 0, 0, 0)),
                pl.BlockSpec((1, 1, cells), lambda k, at: (k, 0, 0)),
            ],
            out_specs=[
                pl.BlockSpec((1, wide, base), lambda k, at: (k, 0, 0)),
                pl.BlockSpec((1, wide, over), lambda k, at: (k, 0, 0)),
                pl.BlockSpec((8, width), lambda k, at: (0, 0)),
            ],
            scratch_shapes=[pltpu.VMEM((cells, width), F32)],
        ),
        out_shape=[
            jax.ShapeDtypeStruct((parts, wide, base), BF),
            jax.ShapeDtypeStruct((parts, wide, over), BF),
            jax.ShapeDtypeStruct((8, width), F32),
        ],
        compiler_params=params(40),
        cost_estimate=cost(10),
        name="pack_cotangent",
    )(at, cot, lane_mask, slots)


def expand(base_ref, over_ref, slot_column, used, acc):
    cells, width = acc.shape
    acc[...] = jnp.zeros_like(acc)
    for is_over, lo, start, count in segments(base_ref.shape[1], over_ref.shape[1]):
        ref = over_ref if is_over else base_ref

        @pl.when(start < used)
        def _():
            lanes = lax.broadcasted_iota(jnp.int32, (cells, LANES), 1) + start
            choice = jnp.concatenate(
                [jnp.where(lanes + j == slot_column, 1.0, 0.0).astype(BF) for j in range(0, count, LANES)], axis=1
            )
            acc[...] += nt(choice, ref[:width, lo : lo + count])


def output_kernel(at_ref, x_ref, m_ref, bias_ref, column_ref, *refs):
    piece_refs, out_ref, acc = refs[:-2], refs[-2], refs[-1]
    parts = len(piece_refs) - 1
    _, side, _, width = x_ref.shape
    per = side // parts
    for k in range(parts):
        part = lax.rem(at_ref[0] + k, parts)
        expand(piece_refs[k], piece_refs[parts].at[0, part], column_ref[part, 0], at_ref[1 + part], acc)

        @pl.loop(0, per)
        def _(i):
            r = i * parts + part
            start = pl.multiple_of(i * side, 8)
            for lo in range(0, width, LANES):
                hi = min(lo + LANES, width)
                value = x_ref[0, r, :, lo:hi].astype(F32) + acc[pl.ds(start, side), lo:hi] + bias_ref[0:1, lo:hi]
                out_ref[0, r, :, lo:hi] = (m_ref[0, r, :, : hi - lo].astype(F32) * value).astype(BF)


def make_output(at, x, lane_mask, bias, columns, pieces):
    parts = len(pieces) - 1
    crops, side, _, width = x.shape
    cells = side * side // parts
    field = pl.BlockSpec((1, side, side, width), lambda n, at: (n, 0, 0, 0))
    return pl.pallas_call(
        output_kernel,
        grid_spec=pltpu.PrefetchScalarGridSpec(
            num_scalar_prefetch=1,
            grid=(crops,),
            in_specs=[
                field,
                pl.BlockSpec((1, side, side, LANES), lambda n, at: (n, 0, 0, 0)),
                pl.BlockSpec((1, width), lambda n, at: (0, 0)),
                pl.BlockSpec((parts, 1, cells, LANES), lambda n, at: (0, n, 0, 0)),
            ]
            + [whole(p) for p in pieces],
            out_specs=field,
            scratch_shapes=[pltpu.VMEM((cells, width), F32)],
        ),
        out_shape=jax.ShapeDtypeStruct(x.shape, BF),
        compiler_params=params(40),
        cost_estimate=cost(12),
        name="make_output",
    )(at, x, lane_mask, bias, columns, *pieces)


def input_gradient_kernel(at_ref, m_ref, cot_ref, conv_ref, w_ref, v_ref, column_ref, *refs, taps, rows, groups):
    piece_refs, dx_ref, gs_ref, acc_ref = refs[:-3], refs[-3], refs[-2], refs[-1]
    gs = gs_ref.at[0]
    parts = len(piece_refs) - 1
    _, side, _, width = cot_ref.shape
    per = side // parts
    half = taps // 2
    clear_borders(gs, half, side)
    for k in range(parts):
        part = lax.rem(at_ref[0] + k, parts)
        expand(piece_refs[k], piece_refs[parts].at[1, part], column_ref[part, 0], at_ref[1 + part], acc_ref)

        @pl.loop(0, per)
        def _(i):
            r = i * parts + part
            start = pl.multiple_of(i * side, 8)
            for t in range(lane_tiles(width)):
                lo, hi = t * LANES, min((t + 1) * LANES, width)
                n = hi - lo
                shape = (side // 8, 8, n)
                m = m_ref[0, r, :, :n].astype(F32).reshape(shape)
                centred = conv_ref[part, 0, i, :, lo:hi].reshape(shape) - v_ref[t, 0, :, :n][None]
                gn = acc_ref[pl.ds(start, side), lo:hi].reshape(shape)
                g = v_ref[t, 1, :, :n][None] * gn - m * (v_ref[t, 2, :, :n][None] + centred * v_ref[t, 3, :, :n][None])
                gs[t, r + half, LEFT : LEFT + side, 0:n] = g.reshape(side, n)

    for t in range(lane_tiles(width)):
        lo, hi = t * LANES, min((t + 1) * LANES, width)
        n = hi - lo

        @pl.loop(0, side // rows)
        def _(i):
            r0 = i * rows
            for c0 in range(0, side, groups * 8):
                acc = conv_rows(gs, w_ref, t, r0, c0, rows, groups, taps, True)
                for r in range(rows):
                    m = m_ref[0, r0 + r, c0 : c0 + groups * 8, :n].astype(F32)
                    cot = cot_ref[0, r0 + r, c0 : c0 + groups * 8, lo:hi].astype(F32)
                    value = m * (cot + acc[r].reshape(groups * 8, LANES)[:, :n])
                    dx_ref[0, r0 + r, c0 : c0 + groups * 8, lo:hi] = value.astype(BF)


def input_gradient(at, lane_mask, cot, conv, wide_taps, vectors, columns, pieces, taps, rows=12, groups=2):
    parts = len(pieces) - 1
    crops, side, _, width = cot.shape
    tiles, half = lane_tiles(width), taps // 2
    cells = side * side // parts
    field = pl.BlockSpec((1, side, side, width), lambda n, at: (n, 0, 0, 0))
    padded = (tiles, side + 2 * half, LEFT + side + 8, LANES)
    return pl.pallas_call(
        functools.partial(input_gradient_kernel, taps=taps, rows=rows, groups=groups),
        grid_spec=pltpu.PrefetchScalarGridSpec(
            num_scalar_prefetch=1,
            grid=(crops,),
            in_specs=[
                pl.BlockSpec((1, side, side, LANES), lambda n, at: (n, 0, 0, 0)),
                field,
                pl.BlockSpec((parts, 1, side // parts, side, width), lambda n, at: (0, n, 0, 0, 0)),
                pl.BlockSpec(wide_taps.shape, lambda n, at: (0, 0, 0, 0)),
                pl.BlockSpec(vectors.shape, lambda n, at: (0, 0, 0, 0)),
                pl.BlockSpec((parts, 1, cells, LANES), lambda n, at: (0, n, 0, 0)),
            ]
            + [whole(p) for p in pieces],
            out_specs=[field, pl.BlockSpec((1, *padded), lambda n, at: (n, 0, 0, 0, 0))],
            scratch_shapes=[pltpu.VMEM((cells, width), F32)],
        ),
        out_shape=[jax.ShapeDtypeStruct(cot.shape, BF), jax.ShapeDtypeStruct((crops, *padded), F32)],
        compiler_params=params(48),
        cost_estimate=cost(28),
        name="input_gradient",
    )(at, lane_mask, cot, conv, wide_taps, vectors, columns, *pieces)


def taps_gradient_kernel(x_ref, m_ref, gs_ref, dw_ref, xs, *, taps, rows, groups):
    _, side, _, width = x_ref.shape
    half = taps // 2
    span = groups * 8

    @pl.when(pl.program_id(0) == 0)
    def _():
        dw_ref[...] = jnp.zeros_like(dw_ref)

    clear_borders(xs, half, side)
    fill_masked(xs, x_ref, m_ref, half)
    for t in range(lane_tiles(width)):

        @pl.loop(0, side // rows)
        def _(i):
            r0 = i * rows
            for c0 in range(0, side, span):
                grads = [
                    gs_ref[0, t, r0 + half + r, LEFT + c0 : LEFT + c0 + span, :].reshape(groups, 8, LANES)
                    for r in range(rows)
                ]
                for b in range(taps):
                    acc = [jnp.zeros((groups, 8, LANES), F32) for _ in range(taps)]
                    for j in range(rows + taps - 1):
                        x = xs[t, r0 + j, pl.ds(LEFT + c0 + b - half, span), :].reshape(groups, 8, LANES)
                        for r in range(max(0, j - taps + 1), min(rows, j + 1)):
                            acc[j - r] = acc[j - r] + x * grads[r]
                    for a in range(taps):
                        dw_ref[t, a * taps + b] += jnp.sum(acc[a], axis=0)


def taps_gradient(x, lane_mask, gs, taps, rows=8, groups=2):
    crops, side, _, width = x.shape
    tiles = lane_tiles(width)
    return pl.pallas_call(
        functools.partial(taps_gradient_kernel, taps=taps, rows=rows, groups=groups),
        grid=(crops,),
        in_specs=[
            pl.BlockSpec((1, side, side, width), lambda n: (n, 0, 0, 0)),
            pl.BlockSpec((1, side, side, LANES), lambda n: (n, 0, 0, 0)),
            pl.BlockSpec((1, *gs.shape[1:]), lambda n: (n, 0, 0, 0, 0)),
        ],
        out_specs=pl.BlockSpec((tiles, taps * taps, 8, LANES), lambda n: (0, 0, 0, 0)),
        out_shape=jax.ShapeDtypeStruct((tiles, taps * taps, 8, LANES), F32),
        scratch_shapes=[pltpu.VMEM(gs.shape[1:], F32)],
        compiler_params=params(40),
        cost_estimate=cost(22),
        name="taps_gradient",
    )(x, lane_mask, gs)


def finish_kernel(both_ref, up_ref, down_ref, bias_ref, rows, *, parts, width, share):
    ranks, _, _, wide = both_ref.shape
    units = down_ref.shape[0]
    wide_width = (wide - 8) // parts
    for which in range(2):
        for d in range(ranks):
            count = min(share, units - d * share)
            if count > 0:
                rows[d * share : d * share + count, :] = both_ref[d, which].astype(F32)[:count]
        if which == 0:
            turned = rows[...].T
            for s in range(parts):
                up_ref[s * width : (s + 1) * width, :] = turned[s * wide_width : s * wide_width + width, :units]
            bias_ref[...] = turned[wide - 8 :, :units]
        else:
            for s in range(parts):
                down_ref[:, s * width : (s + 1) * width] = rows[:units, s * wide_width : s * wide_width + width]


def finish(both, parts, width, share, units):
    ranks, _, slab, wide = both.shape
    channels = parts * width
    return pl.pallas_call(
        functools.partial(finish_kernel, parts=parts, width=width, share=share),
        out_shape=[
            jax.ShapeDtypeStruct((channels, units), F32),
            jax.ShapeDtypeStruct((units, channels), F32),
            jax.ShapeDtypeStruct((8, units), F32),
        ],
        scratch_shapes=[pltpu.VMEM((ceil_to(units, LANES), wide), F32)],
        compiler_params=params(40),
        cost_estimate=cost(5),
        name="finish_weight_gradients",
    )(both)


def gelu_pair(value):
    u = 1.0 + 0.23164189 * jnp.abs(value)
    t = pl.reciprocal(u, approx=True)
    t = t * (2.0 - u * t)
    bell = jnp.exp2(value * value * -0.72134752)
    poly = 0.530702715
    for term in (-0.7265760135, 0.7107068705, -0.142248368, 0.127414796):
        poly = poly * t + term
    tail = poly * t * bell
    below = jnp.where(value >= 0, 1.0 - tail, tail)
    return value * below, below + value * bell * INV_ROOT_TWO_PI


def pointwise_kernel(at_ref, *refs, chips, parts, width, base, over):
    up_refs, down_refs = refs[:chips], refs[chips : 2 * chips]
    data, more_ref, rest = refs[2 * chips : 2 * chips + 4], refs[2 * chips + 4], refs[2 * chips + 5 :]
    outs, (weight_grad_ref, sums_ref) = rest[:8], rest[8:10]
    up_w, down_w, up_t, down_t, up_acc, down_acc, x_place, g_place, hidden, grad_pre = rest[10:]
    whose, c = pl.program_id(0), pl.program_id(1)
    last = (whose == 1) & (c == pl.num_programs(1) - 1)
    _, slab, wide = up_refs[0].shape
    units = chips * parts * slab
    channels = parts * width
    block = units // 8
    me, chip = at_ref[0], at_ref[1 + 2 * parts]
    used = at_ref[1 + whose * parts + me]

    @pl.when((whose == 0) & (c == 0))
    def _():
        for refs, dst in ((up_refs, up_w), (down_refs, down_w)):
            for p in range(chips):
                for q in range(0, parts, 2):
                    pair = jnp.concatenate([refs[p][q].astype(F32), refs[p][q + 1].astype(F32)], axis=0)
                    row = (p * parts + q) * slab
                    dst[row : row + 2 * slab, :] = pair.astype(BF)
        for u in range(0, units, LANES):
            for src, dst in ((up_w, up_t), (down_w, down_t)):
                dst[:, u : u + LANES] = src[u : u + LANES, :].astype(F32).T[:channels, :].astype(BF)
        up_acc[...] = jnp.zeros_like(up_acc)
        down_acc[...] = jnp.zeros_like(down_acc)
        sums_ref[...] = jnp.zeros_like(sums_ref)
        ones = jnp.where(lax.broadcasted_iota(jnp.int32, (8, TILE), 0) == 0, 1.0, 0.0)
        x_place[channels:, :] = ones
        g_place[channels:, :] = jnp.zeros((8, TILE), F32)

    def spots(step):
        first, end = step * TILE, (step + 1) * TILE
        found = []
        if first < base:
            n = min(end, base) - first
            found.append((0, slice(0, n), slice(0, n)))
        if end > base and first < base + over:
            lo, hi = max(first, base), min(end, base + over)
            found.append((1, slice(lo - base, hi - base), slice(lo - first, hi - first)))
        return found

    whole = base // TILE
    steps = -(-(base + over) // TILE)
    cases = ([(c < whole, spots(0))] if whole else []) + [(c == step, spots(step)) for step in range(whole, steps)]
    for side in range(2):
        for case, found in cases:
            here = (whose == side) & case
            x_refs = (data[side], more_ref.at[side, 0])
            g_refs = (data[2 + side], more_ref.at[side, 1])

            @pl.when(here & (c * TILE < used))
            def _():
                for refs, place in ((x_refs, x_place), (g_refs, g_place)):
                    for s in range(parts):
                        k = lax.rem(me - s + parts, parts) if place is x_place else s
                        at = slice(s * width, (s + 1) * width)
                        values = [refs[is_over][s if is_over else k, :, lanes].astype(F32) for is_over, lanes, _ in found]
                        filled = sum(v.shape[1] for v in values)
                        if filled < TILE:
                            values.append(jnp.zeros((width, TILE - filled), F32))
                        place[at, :] = jnp.concatenate(values, axis=1) if len(values) > 1 else values[0]

    @pl.when(c * TILE < used)
    def _():
        x = x_place[...].astype(BF)
        g = g_place[...].astype(BF)

        for i in range(units // block):
            at = pl.ds(i * block, block)
            pre = nn(up_w[at, :], x)
            grad_hidden = nn(down_w[at, :], g)
            value, slope = gelu_pair(pre)
            h = value.astype(BF)
            gp = (grad_hidden * slope).astype(BF)
            hidden[at, :] = h
            grad_pre[at, :] = gp

        for lo in range(0, wide, 2 * LANES):
            hi = min(lo + 2 * LANES, wide)
            up_acc[:, lo:hi] += nt(grad_pre[...], x[lo:hi, :])
            down_acc[:, lo:hi] += nt(hidden[...], g[lo:hi, :])

        def fold(v):
            return sum(v[:, lo : lo + LANES] for lo in range(0, TILE, LANES))

        for s in range(parts):
            rows = slice(s * width, (s + 1) * width)
            k = lax.rem(me - s + parts, parts)
            branch = nn(down_t[rows, :], hidden[...])
            normed = nn(up_t[rows, :], grad_pre[...])
            sums_ref[k, 0] += fold(normed)
            sums_ref[k, 1] += fold(normed * x_place[rows, :])
            for side in range(2):
                for case, found in cases:

                    @pl.when((whose == side) & case)
                    def _():
                        for is_over, lanes, tile in found:
                            to = 2 * side + is_over
                            for value, ref in ((branch, outs[to]), (normed, outs[4 + to])):
                                ref[s if is_over else k, :, lanes] = value[:, tile].astype(ref.dtype)

    @pl.when(last)
    def _():
        for p in range(chips):
            for q in range(parts):
                row = (p * parts + q) * slab
                to = (chip ^ p, q)
                weight_grad_ref[to[0], to[1], 0] = up_acc[row : row + slab, :].astype(BF)
                weight_grad_ref[to[0], to[1], 1] = down_acc[row : row + slab, :].astype(BF)


def pointwise(at, ups, downs, data):
    chips = len(ups)
    parts, width, base = data[0].shape
    over = data[4].shape[4]
    _, slab, wide = ups[0].shape
    units, channels = chips * parts * slab, parts * width
    base_tiles = -(-base // TILE)

    def tile(side, is_over):
        if is_over:
            return pl.BlockSpec((parts, width, over), lambda whose, c, at: (0, 0, 0))

        def place(whose, c, at):
            end = jnp.minimum(jnp.maximum((at[1 + side * parts + at[0]] - 1) // TILE, 0), base_tiles - 1)
            return (0, 0, jnp.where(whose == side, jnp.minimum(c, end), 0 if side else end))

        return pl.BlockSpec((parts, width, TILE), place)

    tiles = [tile(side, is_over) for side in range(2) for is_over in range(2)]
    kinds = [F32, F32, BF, BF]
    result = [jax.ShapeDtypeStruct((parts, width, n), kind) for n, kind in zip((base, over, base, over), kinds)]
    return pl.pallas_call(
        functools.partial(pointwise_kernel, chips=chips, parts=parts, width=width, base=base, over=over),
        grid_spec=pltpu.PrefetchScalarGridSpec(
            num_scalar_prefetch=1,
            grid=(2, -(-(base + over) // TILE)),
            in_specs=[
                pl.BlockSpec(ups[0].shape, lambda w, c, at: (0, 0, 0), pipeline_mode=pl.Buffered(1))
                for _ in range(2 * chips)
            ]
            + [tile(0, 0), tile(1, 0), tile(0, 0), tile(1, 0)]
            + [pl.BlockSpec(data[4].shape, lambda w, c, at: (0, 0, 0, 0, 0), pipeline_mode=pl.Buffered(1))],
            out_specs=tiles
            + tiles
            + [
                pl.BlockSpec((chips, parts, 2, slab, wide), lambda w, c, at: (0, 0, 0, 0, 0)),
                pl.BlockSpec((parts, 2, width, LANES), lambda w, c, at: (0, 0, 0, 0)),
            ],
            scratch_shapes=[
                pltpu.VMEM((units, wide), BF),
                pltpu.VMEM((units, wide), BF),
                pltpu.VMEM((channels, units), BF),
                pltpu.VMEM((channels, units), BF),
                pltpu.VMEM((units, wide), F32),
                pltpu.VMEM((units, wide), F32),
                pltpu.VMEM((wide, TILE), F32),
                pltpu.VMEM((wide, TILE), F32),
                pltpu.VMEM((units, TILE), BF),
                pltpu.VMEM((units, TILE), BF),
            ],
        ),
        out_shape=result
        + result
        + [
            jax.ShapeDtypeStruct((chips, parts, 2, slab, wide), BF),
            jax.ShapeDtypeStruct((parts, 2, width, LANES), F32),
        ],
        compiler_params=params(62),
        cost_estimate=cost(70),
        name="pointwise",
    )(at, *ups, *downs, *data)


def per_device(
    inputs,
    crop_sizes,
    land_mask,
    conv_weight,
    norm_gain,
    norm_shift,
    up_weight,
    up_bias,
    down_weight,
    down_bias,
    cotangent,
    *,
    sizes,
):
    chips, cores, parts = sizes
    crops, side, _, width = inputs.shape
    taps = conv_weight.shape[0]
    cells = crops * side * side // parts
    local_units = up_weight.shape[1]
    channels = up_weight.shape[0]
    me = lax.axis_index("mp")
    core = lax.axis_index("core")
    chip = lax.axis_index("xy")

    def ring(k):
        return [(i, (i + k) % parts) for i in range(parts)]

    def everywhere(value, axes):
        for axis in axes:
            size = {"xy": chips, "core": cores, "mp": parts}[axis]
            if size <= 4:
                others = [lax.ppermute(value, axis, [(i, i ^ j) for i in range(size)]) for j in range(1, size)]
                value = sum(others, value)
                continue
            step = 1
            while step < size:
                value = value + lax.ppermute(value, axis, [(i, i ^ step) for i in range(size)])
                step *= 2
        return value

    def ring_back(k):
        return [(i, (i - k) % parts) for i in range(parts)]

    def to_parts(pieces, ring=ring):
        return [pieces[0]] + [lax.ppermute(pieces[k], "mp", ring(k)) for k in range(1, parts)]

    def exchange(by_part):
        return lax.all_to_all(by_part, "mp", 0, 0, tiled=True)

    swap = [(i, cores - 1 - i) for i in range(cores)]

    def to_core(value):
        return lax.ppermute(value, "core", swap)

    share = -(-local_units // (chips * cores))
    slab = ceil_to(share, 8)
    wide_width = ceil_to(width, 8)
    wide = parts * wide_width + 8
    rank = chip * cores + core
    spare = chips * cores * share - local_units

    def take(rows):
        rows = jnp.pad(rows, ((0, spare), (0, 0))) if spare else rows
        rows = lax.dynamic_slice_in_dim(rows, rank * share, share, axis=0)
        if wide_width > width:
            rows = jnp.pad(rows.reshape(share, parts, width), ((0, 0), (0, 0), (0, wide_width - width)))
        return rows.reshape(share, -1)

    own_bias = up_bias[:, None]
    own_bias = jnp.pad(own_bias, ((0, spare), (0, 0))) if spare else own_bias
    own_bias = lax.dynamic_slice_in_dim(own_bias, rank * share, share, axis=0)
    up_rows = jnp.pad(jnp.concatenate([take(up_weight.T), own_bias], axis=1), ((0, slab - share), (0, 7)))
    down_rows = jnp.pad(take(down_weight), ((0, slab - share), (0, 8)))
    rows = lax.all_gather(jnp.stack([up_rows, down_rows]), "mp", axis=1, tiled=False)

    def over_plane(own, bits):
        held = {0: own}
        for bit in bits:
            pairs = [(i, i ^ bit) for i in range(chips)]
            held.update({p ^ bit: lax.ppermute(value, "xy", pairs) for p, value in list(held.items())})
        return [held[p] for p in range(chips)]

    index = jnp.arange(side, dtype=jnp.int32)
    inside = (index[None, :, None] < crop_sizes[:, 0][:, None, None]) & (
        index[None, None, :] < crop_sizes[:, 1][:, None, None]
    )
    usable = jnp.where(inside, land_mask, 0)
    lane_mask = jnp.broadcast_to(usable[..., None].astype(BF), usable.shape + (LANES,))
    by_part = usable.reshape(crops, side // parts, parts, side).transpose(2, 0, 1, 3).reshape(parts, -1, side)
    by_part = by_part.astype(F32)
    lines = by_part.shape[1]
    upto = jnp.dot(by_part, jnp.triu(jnp.ones((side, side), F32)))
    before = jnp.dot(upto[:, :, -1], jnp.triu(jnp.ones((lines, lines), F32), 1))
    slots = jnp.where(by_part > 0, upto + before[:, :, None] - 1, -1).astype(jnp.int32)
    counts = jnp.sum(by_part, axis=(1, 2)).astype(jnp.int32)
    columns = jnp.broadcast_to(slots.reshape(parts, crops, -1)[..., None], (parts, crops, cells // crops, LANES))
    slots = slots.reshape(parts, 1, cells)
    at = jnp.concatenate([me[None].astype(jnp.int32), counts, to_core(counts), chip[None].astype(jnp.int32)])

    base = ceil_to(cells * 7 // 9, LANES)
    over = ceil_to(cells, LANES) - base
    over_full = jnp.where(jnp.max(counts) > base, 1.0, 0.0)

    cot_base, cot_over, down_bias_local = pack_cotangent(at, cotangent, lane_mask, slots, base, over)
    inputs, cot_base = after(inputs, cot_base)
    grad_base = exchange(cot_base)

    wide_taps = spread_rows(conv_weight.reshape(taps * taps, width))
    convolved, stats = conv_forward(inputs, lane_mask, wide_taps, taps, parts)
    stats = jnp.sum(stats, axis=(0, 3)).reshape(2, -1)[:, :width]
    extra = jnp.pad(jnp.stack([jnp.sum(by_part), over_full])[None], ((0, 0), (0, width - 2)))
    stats = everywhere(jnp.concatenate([stats, extra, jnp.sum(down_bias_local, axis=0)[None]]), ("core", "xy"))
    stats, rows = after(stats, rows)
    bits = [1 << j for j in range(chips.bit_length() - 1)]

    def double(held, bit):
        pairs = [(i, i ^ bit) for i in range(chips)]
        return {**held, **{p ^ bit: lax.ppermute(value, "xy", pairs) for p, value in held.items()}}

    ups, downs = {0: rows[0]}, {0: rows[1]}
    ups, downs = double(ups, bits[0]), double(downs, bits[-1])
    ocean_count = stats[2, 0]
    overflows = stats[2, 1] > 0
    down_bias_grad = stats[3]
    channel_mean = stats[0] / ocean_count
    inv_std = lax.rsqrt(stats[1] / ocean_count - channel_mean * channel_mean + EPSILON)
    gain = norm_gain.astype(F32)
    shift = norm_shift.astype(F32)
    scale = gain * inv_std

    affine = jnp.stack([scale, shift - channel_mean * scale])
    normed_base, normed_over = pack_normed(at, convolved.reshape(parts, cells, width), affine, slots, base, over)
    places = sorted(ups), sorted(downs)
    *both, grad_base = after(*normed_base, *[ups[p] for p in places[0]], *[downs[p] for p in places[1]], grad_base)
    normed_base, held = both[:parts], both[parts:]
    ups, downs = dict(zip(places[0], held)), dict(zip(places[1], held[len(ups) :]))
    for j in range(1, len(bits)):
        ups, downs = double(ups, bits[j]), double(downs, bits[-1 - j])
    ups, downs = [ups[p] for p in range(chips)], [downs[p] for p in range(chips)]
    *both, crowded, columns = after(*to_parts(normed_base), *ups, *downs, overflows, columns)
    x_base, ups, downs = jnp.stack(both[:parts]), both[parts : parts + chips], both[parts + chips :]

    def overflow_in():
        own = jnp.stack([exchange(normed_over), exchange(cot_over)])
        return jnp.stack([own, to_core(own)])

    more = lax.cond(crowded, overflow_in, lambda: jnp.zeros((2, 2, parts, wide_width, over), BF))
    data = [x_base, to_core(x_base), grad_base, to_core(grad_base), more]
    *sums_out, weight_grad, sums = pointwise(at, ups, downs, data)
    branch, normed = list(sums_out[:4]), list(sums_out[4:])

    def over_cores(own, far):
        return (own + to_core(far).astype(F32)).astype(BF)

    def home(total):
        return to_parts([total[k] for k in range(parts)], ring_back)

    sums = everywhere(jnp.sum(sums, axis=3), ("core", "xy"))
    sums = sum(to_parts([sums[k] for k in range(parts)], ring_back))[:, :width]
    total, sums = after(over_cores(normed[0], normed[2]), sums)
    normed_base = home(total)
    total = over_cores(branch[0], branch[2])
    crowded, total, sums, *normed_base = after(overflows, total, sums, *normed_base)

    def overflow_out():
        return jnp.stack([exchange(over_cores(v[1], v[3])) for v in (branch, normed)])

    more = lax.cond(crowded, overflow_out, lambda: jnp.zeros((2, parts, wide_width, over), BF))
    total, more = after(total, more)
    branch_base = home(total)

    shift_grad = sums[0]
    gain_grad = (sums[1] - shift * shift_grad) / gain
    vectors = jnp.stack([channel_mean, scale, scale * shift_grad / ocean_count, scale * inv_std * gain_grad / ocean_count])
    input_grad, grad_conv = input_gradient(
        at, lane_mask, cotangent, convolved, wide_taps, spread_rows(vectors), columns, [*normed_base, more], taps
    )

    own = lax.psum_scatter(weight_grad, "xy", scatter_dimension=0, tiled=False)
    own, grad_conv, *branch_base = after(own, grad_conv, *branch_base)
    taps_local = taps_gradient(inputs, lane_mask, grad_conv, taps)
    own = lax.psum_scatter(own, "mp", scatter_dimension=0, tiled=False)
    own, taps_local = after(own, taps_local)
    both = lax.all_gather(own, ("xy", "core"), axis=0, tiled=False)
    taps_local, *branch_base = after(taps_local, *branch_base)
    output = make_output(at, inputs, lane_mask, down_bias.astype(F32)[None], columns, [*branch_base, more])
    taps_local = jnp.sum(taps_local, axis=2).transpose(1, 0, 2).reshape(taps * taps, -1)
    conv_weight_grad = everywhere(taps_local, ("core", "xy"))[:, :width].reshape(taps, taps, width)
    up_weight_grad, down_weight_grad, bias_rows = finish(both, parts, width, share, local_units)
    up_bias_grad = bias_rows[0]
    return (
        output,
        input_grad,
        conv_weight_grad,
        gain_grad,
        shift_grad,
        up_weight_grad,
        up_bias_grad,
        down_weight_grad,
        down_bias_grad,
    )


def solution(mesh):
    cores = 2
    parts = mesh.shape["mp"]
    chips = mesh.shape["dp"] // cores
    fine = Mesh(np.asarray(mesh.devices).reshape(chips, cores, parts), ("xy", "core", "mp"))
    dp = ("xy", "core")
    specs = (
        P(dp, None, None, "mp"),
        P(dp, None),
        P(dp, None, None),
        P(None, None, "mp"),
        P("mp"),
        P("mp"),
        P(None, "mp"),
        P("mp"),
        P("mp", None),
        P("mp"),
        P(dp, None, None, "mp"),
    )
    results = (
        P(dp, None, None, "mp"),
        P(dp, None, None, "mp"),
        P(None, None, "mp"),
        P("mp"),
        P("mp"),
        P(None, "mp"),
        P("mp"),
        P("mp", None),
        P("mp"),
    )
    return jax.shard_map(
        functools.partial(per_device, sizes=(chips, cores, parts)),
        mesh=fine,
        in_specs=specs,
        out_specs=results,
        check_vma=False,
    )
```

```python
import functools

import jax
import jax.numpy as jnp
import numpy as np
from jax import lax
from jax.experimental import pallas as pl
from jax.experimental.pallas import tpu as pltpu
from jax.sharding import Mesh
from jax.sharding import PartitionSpec as P

F32 = jnp.float32
BF = jnp.bfloat16
EPSILON = 1e-05
INV_ROOT_TWO_PI = 0.3989422804014327
LANES = 128
LEFT = 8
MIB = 2**20
TILE = 256


def ceil_to(value, unit):
    return -(-value // unit) * unit


def lane_tiles(width):
    return -(-width // LANES)


def spread_rows(rows):
    count, width = rows.shape
    tiles = lane_tiles(width)
    flat = jnp.pad(rows.astype(F32), ((0, 0), (0, tiles * LANES - width)))
    flat = flat.reshape(count, tiles, 1, LANES).transpose(1, 0, 2, 3)
    return jnp.broadcast_to(flat, (tiles, count, 8, LANES))


def after(*values):
    return lax.optimization_barrier(values)


def params(mib, **more):
    return pltpu.CompilerParams(vmem_limit_bytes=mib * MIB, **more)


def whole(array):
    zeros = (0,) * array.ndim
    return pl.BlockSpec(array.shape, lambda n, at: zeros)


EAGERNESS = 6


def cost(micros):
    return pl.CostEstimate(flops=int(micros * 1.15e9 / EAGERNESS), bytes_accessed=0, transcendentals=0)


def clear_borders(dst, half, side):
    tiles, _, cols, _ = dst.shape
    for t in range(tiles):
        for r in list(range(half)) + list(range(half + side, side + 2 * half)):
            dst[t, r] = jnp.zeros((cols, LANES), F32)

        @pl.loop(0, side)
        def _(r):
            dst[t, r + half, 0:LEFT, :] = jnp.zeros((LEFT, LANES), F32)
            dst[t, r + half, LEFT + side : cols, :] = jnp.zeros((cols - LEFT - side, LANES), F32)


def fill_masked(dst, x_ref, m_ref, half):
    _, side, _, width = x_ref.shape
    for t in range(lane_tiles(width)):
        lo, hi = t * LANES, min((t + 1) * LANES, width)

        @pl.loop(0, side)
        def _(r):
            value = x_ref[0, r, :, lo:hi].astype(F32) * m_ref[0, r, :, : hi - lo].astype(F32)
            dst[t, r + half, LEFT : LEFT + side, 0 : hi - lo] = value


def conv_rows(src, w_ref, t, r0, c0, rows, groups, taps, flipped):
    half = taps // 2
    acc = [jnp.zeros((groups, 8, LANES), F32) for _ in range(rows)]
    for b in range(taps):
        shift = (taps - 1 - b) if flipped else b
        weights = [w_ref[t, a * taps + b] for a in range(taps)]
        for i in range(rows + taps - 1):
            x = src[t, r0 + i, pl.ds(LEFT + c0 + shift - half, groups * 8), :].reshape(groups, 8, LANES)
            for r in range(max(0, i - taps + 1), min(rows, i + 1)):
                a = taps - 1 - (i - r) if flipped else i - r
                acc[r] = acc[r] + x * weights[a][None]
    return acc


def forward_kernel(x_ref, m_ref, w_ref, conv_ref, stat_ref, xs, *, taps, rows, groups):
    _, side, _, width = x_ref.shape
    parts = conv_ref.shape[0]
    half = taps // 2
    clear_borders(xs, half, side)
    fill_masked(xs, x_ref, m_ref, half)
    for t in range(lane_tiles(width)):
        lo, hi = t * LANES, min((t + 1) * LANES, width)

        def block(i, carry):
            first, second = carry
            r0 = i * rows
            for c0 in range(0, side, groups * 8):
                acc = conv_rows(xs, w_ref, t, r0, c0, rows, groups, taps, False)
                for r in range(rows):
                    m = m_ref[0, r0 + r, c0 : c0 + groups * 8, :].astype(F32).reshape(groups, 8, LANES)
                    cm = acc[r] * m
                    first = first + jnp.sum(cm, axis=0)
                    second = second + jnp.sum(cm * acc[r], axis=0)
                    if rows % parts == 0:
                        part, row = r % parts, i * (rows // parts) + r // parts
                    else:
                        part, row = lax.rem(r0 + r, parts), lax.div(r0 + r, parts)
                    conv_ref[part, 0, row, c0 : c0 + groups * 8, lo:hi] = acc[r].reshape(groups * 8, LANES)[:, : hi - lo]
            return first, second

        zero = jnp.zeros((8, LANES), F32)
        first, second = lax.fori_loop(0, side // rows, block, (zero, zero))
        stat_ref[0, 0, t] = first
        stat_ref[0, 1, t] = second


def conv_forward(x, lane_mask, wide_taps, taps, parts, rows=12, groups=2):
    crops, side, _, width = x.shape
    tiles, half = lane_tiles(width), taps // 2
    return pl.pallas_call(
        functools.partial(forward_kernel, taps=taps, rows=rows, groups=groups),
        grid=(crops,),
        in_specs=[
            pl.BlockSpec((1, side, side, width), lambda n: (n, 0, 0, 0)),
            pl.BlockSpec((1, side, side, LANES), lambda n: (n, 0, 0, 0)),
            pl.BlockSpec(wide_taps.shape, lambda n: (0, 0, 0, 0)),
        ],
        out_specs=[
            pl.BlockSpec((parts, 1, side // parts, side, width), lambda n: (0, n, 0, 0, 0)),
            pl.BlockSpec((1, 2, tiles, 8, LANES), lambda n: (n, 0, 0, 0, 0)),
        ],
        out_shape=[
            jax.ShapeDtypeStruct((parts, crops, side // parts, side, width), F32),
            jax.ShapeDtypeStruct((crops, 2, tiles, 8, LANES), F32),
        ],
        scratch_shapes=[pltpu.VMEM((tiles, side + 2 * half, LEFT + side + 8, LANES), F32)],
        compiler_params=params(32),
        cost_estimate=cost(22),
        name="depthwise_forward",
    )(x, lane_mask, wide_taps)


def chooser(slot_of_cell, start, count):
    cells = slot_of_cell.shape[1]
    rows = lax.broadcasted_iota(jnp.int32, (count, cells), 0) + start
    return jnp.where(rows == slot_of_cell, 1.0, 0.0).astype(BF)


def nt(left, right):
    return lax.dot_general(left, right, (((1,), (1,)), ((), ())), preferred_element_type=F32)


def nn(left, right):
    return jnp.dot(left, right, preferred_element_type=F32)


def segments(base, over):
    cuts = sorted({*range(0, base + over, TILE), base, base + over})
    return [
        (int(lo >= base), lo - base if lo >= base else lo, lo, hi - lo) for lo, hi in zip(cuts, cuts[1:]) if hi <= base + over
    ]


def pack_columns(values, slots, used, base_ref, over_ref):
    width = values.shape[0]
    for is_over, lo, start, count in segments(base_ref.shape[1], over_ref.shape[1]):
        ref = over_ref if is_over else base_ref

        @pl.when(start < used)
        def _():
            ref[:width, lo : lo + count] = nt(values, chooser(slots, start, count)).astype(BF)

        @pl.when(start >= used)
        def _():
            ref[:width, lo : lo + count] = jnp.zeros((width, count), BF)

        if width < ref.shape[0]:
            ref[width:, lo : lo + count] = jnp.zeros((ref.shape[0] - width, count), BF)


def pack_normed_kernel(at_ref, conv_ref, vec_ref, slot_ref, *out_refs):
    k = pl.program_id(0)
    base_refs, over_ref = out_refs[:-1], out_refs[-1]
    part = lax.rem(at_ref[0] + k, len(base_refs))
    normed = (conv_ref[0] * vec_ref[0:1, :] + vec_ref[1:2, :]).T.astype(BF)
    for j, base_ref in enumerate(base_refs):

        @pl.when(k == j)
        def _():
            pack_columns(normed, slot_ref[0], at_ref[1 + part], base_ref, over_ref.at[part])


def pack_normed(at, conv, vec, slots, base, over):
    parts, cells, width = conv.shape
    wide = ceil_to(width, 8)
    part = lambda k, at: (lax.rem(at[0] + k, parts), 0, 0)
    *pieces, more = pl.pallas_call(
        pack_normed_kernel,
        grid_spec=pltpu.PrefetchScalarGridSpec(
            num_scalar_prefetch=1,
            grid=(parts,),
            in_specs=[
                pl.BlockSpec((1, cells, width), part),
                pl.BlockSpec(vec.shape, lambda k, at: (0, 0)),
                pl.BlockSpec((1, 1, cells), part),
            ],
            out_specs=[pl.BlockSpec((wide, base), lambda k, at: (0, 0))] * parts
            + [pl.BlockSpec((parts, wide, over), lambda k, at: (0, 0, 0))],
        ),
        out_shape=[jax.ShapeDtypeStruct((wide, base), BF)] * parts + [jax.ShapeDtypeStruct((parts, wide, over), BF)],
        compiler_params=params(32),
        cost_estimate=cost(8),
        name="pack_normed",
    )(at, conv, vec, slots)
    return pieces, more


def pack_cotangent_kernel(at_ref, cot_ref, m_ref, slot_ref, base_ref, over_ref, sum_ref, rows):
    crops, side, _, width = cot_ref.shape
    part, parts = pl.program_id(0), pl.num_programs(0)
    per = rows.shape[0] // (crops * side)
    total = jnp.zeros((8, width), F32)
    for n in range(crops):

        def body(i, total):
            r = i * parts + part
            masks = [m_ref[n, r, :, : min(LANES, width - lo)] for lo in range(0, width, LANES)]
            mask = jnp.concatenate(masks, axis=1) if len(masks) > 1 else masks[0]
            value = cot_ref[n, r].astype(F32) * mask.astype(F32)
            rows[pl.ds(pl.multiple_of((n * per + i) * side, 8), side), :] = value
            return total + jnp.sum(value.reshape(side // 8, 8, width), axis=0)

        total = lax.fori_loop(0, per, body, total)

    @pl.when(part == 0)
    def _():
        sum_ref[...] = total

    @pl.when(part > 0)
    def _():
        sum_ref[...] += total

    pack_columns(rows[...].T.astype(BF), slot_ref[0], at_ref[1 + part], base_ref.at[0], over_ref.at[0])


def pack_cotangent(at, cot, lane_mask, slots, base, over):
    crops, side, _, width = cot.shape
    parts, _, cells = slots.shape
    wide = ceil_to(width, 8)
    return pl.pallas_call(
        pack_cotangent_kernel,
        grid_spec=pltpu.PrefetchScalarGridSpec(
            num_scalar_prefetch=1,
            grid=(parts,),
            in_specs=[
                pl.BlockSpec(cot.shape, lambda k, at: (0, 0, 0, 0)),
                pl.BlockSpec(lane_mask.shape, lambda k, at: (0, 0, 0, 0)),
                pl.BlockSpec((1, 1, cells), lambda k, at: (k, 0, 0)),
            ],
            out_specs=[
                pl.BlockSpec((1, wide, base), lambda k, at: (k, 0, 0)),
                pl.BlockSpec((1, wide, over), lambda k, at: (k, 0, 0)),
                pl.BlockSpec((8, width), lambda k, at: (0, 0)),
            ],
            scratch_shapes=[pltpu.VMEM((cells, width), F32)],
        ),
        out_shape=[
            jax.ShapeDtypeStruct((parts, wide, base), BF),
            jax.ShapeDtypeStruct((parts, wide, over), BF),
            jax.ShapeDtypeStruct((8, width), F32),
        ],
        compiler_params=params(40),
        cost_estimate=cost(10),
        name="pack_cotangent",
    )(at, cot, lane_mask, slots)


def expand(base_ref, over_ref, slot_column, reach, acc):
    cells, width = acc.shape
    acc[...] = jnp.zeros_like(acc)
    for is_over, lo, start, count in segments(base_ref.shape[1], over_ref.shape[1]):
        ref = over_ref if is_over else base_ref

        @pl.when((start < reach[1]) & (start + count > reach[0]))
        def _():
            lanes = lax.broadcasted_iota(jnp.int32, (cells, LANES), 1) + start
            choice = jnp.concatenate(
                [jnp.where(lanes + j == slot_column, 1.0, 0.0).astype(BF) for j in range(0, count, LANES)], axis=1
            )
            acc[...] += nt(choice, ref[:width, lo : lo + count])


def reach_of(at_ref, parts, part, crop):
    crops = (at_ref.shape[0] - (2 + 2 * parts)) // parts - 1
    place = 2 + 2 * parts + part * (crops + 1) + crop
    return at_ref[place], at_ref[place + 1]


def output_kernel(at_ref, x_ref, m_ref, bias_ref, column_ref, *refs):
    piece_refs, out_ref, acc = refs[:-2], refs[-2], refs[-1]
    parts = len(piece_refs) - 1
    _, side, _, width = x_ref.shape
    per = side // parts
    for k in range(parts):
        part = lax.rem(at_ref[0] + k, parts)
        reach = reach_of(at_ref, parts, part, pl.program_id(0))
        expand(piece_refs[k], piece_refs[parts].at[0, part], column_ref[part, 0], reach, acc)

        @pl.loop(0, per)
        def _(i):
            r = i * parts + part
            start = pl.multiple_of(i * side, 8)
            for lo in range(0, width, LANES):
                hi = min(lo + LANES, width)
                value = x_ref[0, r, :, lo:hi].astype(F32) + acc[pl.ds(start, side), lo:hi] + bias_ref[0:1, lo:hi]
                out_ref[0, r, :, lo:hi] = (m_ref[0, r, :, : hi - lo].astype(F32) * value).astype(BF)


def make_output(at, x, lane_mask, bias, columns, pieces):
    parts = len(pieces) - 1
    crops, side, _, width = x.shape
    cells = side * side // parts
    field = pl.BlockSpec((1, side, side, width), lambda n, at: (n, 0, 0, 0))
    return pl.pallas_call(
        output_kernel,
        grid_spec=pltpu.PrefetchScalarGridSpec(
            num_scalar_prefetch=1,
            grid=(crops,),
            in_specs=[
                field,
                pl.BlockSpec((1, side, side, LANES), lambda n, at: (n, 0, 0, 0)),
                pl.BlockSpec((1, width), lambda n, at: (0, 0)),
                pl.BlockSpec((parts, 1, cells, LANES), lambda n, at: (0, n, 0, 0)),
            ]
            + [whole(p) for p in pieces],
            out_specs=field,
            scratch_shapes=[pltpu.VMEM((cells, width), F32)],
        ),
        out_shape=jax.ShapeDtypeStruct(x.shape, BF),
        compiler_params=params(60),
        cost_estimate=cost(12),
        name="make_output",
    )(at, x, lane_mask, bias, columns, *pieces)


def input_gradient_kernel(at_ref, m_ref, cot_ref, conv_ref, w_ref, v_ref, column_ref, *refs, taps, rows, groups):
    piece_refs, dx_ref, gs_ref, acc_ref = refs[:-3], refs[-3], refs[-2], refs[-1]
    gs = gs_ref.at[0]
    parts = len(piece_refs) - 1
    _, side, _, width = cot_ref.shape
    per = side // parts
    half = taps // 2
    clear_borders(gs, half, side)
    for k in range(parts):
        part = lax.rem(at_ref[0] + k, parts)
        reach = reach_of(at_ref, parts, part, pl.program_id(0))
        expand(piece_refs[k], piece_refs[parts].at[1, part], column_ref[part, 0], reach, acc_ref)

        @pl.loop(0, per)
        def _(i):
            r = i * parts + part
            start = pl.multiple_of(i * side, 8)
            for t in range(lane_tiles(width)):
                lo, hi = t * LANES, min((t + 1) * LANES, width)
                n = hi - lo
                shape = (side // 8, 8, n)
                m = m_ref[0, r, :, :n].astype(F32).reshape(shape)
                centred = conv_ref[part, 0, i, :, lo:hi].reshape(shape) - v_ref[t, 0, :, :n][None]
                gn = acc_ref[pl.ds(start, side), lo:hi].reshape(shape)
                g = v_ref[t, 1, :, :n][None] * gn - m * (v_ref[t, 2, :, :n][None] + centred * v_ref[t, 3, :, :n][None])
                gs[t, r + half, LEFT : LEFT + side, 0:n] = g.reshape(side, n)

    for t in range(lane_tiles(width)):
        lo, hi = t * LANES, min((t + 1) * LANES, width)
        n = hi - lo

        @pl.loop(0, side // rows)
        def _(i):
            r0 = i * rows
            for c0 in range(0, side, groups * 8):
                acc = conv_rows(gs, w_ref, t, r0, c0, rows, groups, taps, True)
                for r in range(rows):
                    m = m_ref[0, r0 + r, c0 : c0 + groups * 8, :n].astype(F32)
                    cot = cot_ref[0, r0 + r, c0 : c0 + groups * 8, lo:hi].astype(F32)
                    value = m * (cot + acc[r].reshape(groups * 8, LANES)[:, :n])
                    dx_ref[0, r0 + r, c0 : c0 + groups * 8, lo:hi] = value.astype(BF)


def input_gradient(at, lane_mask, cot, conv, wide_taps, vectors, columns, pieces, taps, rows=12, groups=2):
    parts = len(pieces) - 1
    crops, side, _, width = cot.shape
    tiles, half = lane_tiles(width), taps // 2
    cells = side * side // parts
    field = pl.BlockSpec((1, side, side, width), lambda n, at: (n, 0, 0, 0))
    padded = (tiles, side + 2 * half, LEFT + side + 8, LANES)
    return pl.pallas_call(
        functools.partial(input_gradient_kernel, taps=taps, rows=rows, groups=groups),
        grid_spec=pltpu.PrefetchScalarGridSpec(
            num_scalar_prefetch=1,
            grid=(crops,),
            in_specs=[
                pl.BlockSpec((1, side, side, LANES), lambda n, at: (n, 0, 0, 0)),
                field,
                pl.BlockSpec((parts, 1, side // parts, side, width), lambda n, at: (0, n, 0, 0, 0)),
                pl.BlockSpec(wide_taps.shape, lambda n, at: (0, 0, 0, 0)),
                pl.BlockSpec(vectors.shape, lambda n, at: (0, 0, 0, 0)),
                pl.BlockSpec((parts, 1, cells, LANES), lambda n, at: (0, n, 0, 0)),
            ]
            + [whole(p) for p in pieces],
            out_specs=[field, pl.BlockSpec((1, *padded), lambda n, at: (n, 0, 0, 0, 0))],
            scratch_shapes=[pltpu.VMEM((cells, width), F32)],
        ),
        out_shape=[jax.ShapeDtypeStruct(cot.shape, BF), jax.ShapeDtypeStruct((crops, *padded), F32)],
        compiler_params=params(60),
        cost_estimate=cost(28),
        name="input_gradient",
    )(at, lane_mask, cot, conv, wide_taps, vectors, columns, *pieces)


def taps_gradient_kernel(x_ref, m_ref, gs_ref, dw_ref, xs, *, taps, rows, groups):
    _, side, _, width = x_ref.shape
    half = taps // 2
    span = groups * 8

    @pl.when(pl.program_id(0) == 0)
    def _():
        dw_ref[...] = jnp.zeros_like(dw_ref)

    clear_borders(xs, half, side)
    fill_masked(xs, x_ref, m_ref, half)
    for t in range(lane_tiles(width)):

        @pl.loop(0, side // rows)
        def _(i):
            r0 = i * rows
            for c0 in range(0, side, span):
                grads = [
                    gs_ref[0, t, r0 + half + r, LEFT + c0 : LEFT + c0 + span, :].reshape(groups, 8, LANES)
                    for r in range(rows)
                ]
                for b in range(taps):
                    acc = [jnp.zeros((groups, 8, LANES), F32) for _ in range(taps)]
                    for j in range(rows + taps - 1):
                        x = xs[t, r0 + j, pl.ds(LEFT + c0 + b - half, span), :].reshape(groups, 8, LANES)
                        for r in range(max(0, j - taps + 1), min(rows, j + 1)):
                            acc[j - r] = acc[j - r] + x * grads[r]
                    for a in range(taps):
                        dw_ref[t, a * taps + b] += jnp.sum(acc[a], axis=0)


def taps_gradient(x, lane_mask, gs, taps, rows=8, groups=2):
    crops, side, _, width = x.shape
    tiles = lane_tiles(width)
    return pl.pallas_call(
        functools.partial(taps_gradient_kernel, taps=taps, rows=rows, groups=groups),
        grid=(crops,),
        in_specs=[
            pl.BlockSpec((1, side, side, width), lambda n: (n, 0, 0, 0)),
            pl.BlockSpec((1, side, side, LANES), lambda n: (n, 0, 0, 0)),
            pl.BlockSpec((1, *gs.shape[1:]), lambda n: (n, 0, 0, 0, 0)),
        ],
        out_specs=pl.BlockSpec((tiles, taps * taps, 8, LANES), lambda n: (0, 0, 0, 0)),
        out_shape=jax.ShapeDtypeStruct((tiles, taps * taps, 8, LANES), F32),
        scratch_shapes=[pltpu.VMEM(gs.shape[1:], F32)],
        compiler_params=params(60),
        cost_estimate=cost(22),
        name="taps_gradient",
    )(x, lane_mask, gs)


def finish_kernel(both_ref, up_ref, down_ref, bias_ref, rows, *, parts, width, share):
    ranks, _, _, wide = both_ref.shape
    units = down_ref.shape[0]
    wide_width = (wide - 8) // parts
    for which in range(2):
        for d in range(ranks):
            count = min(share, units - d * share)
            if count > 0:
                rows[d * share : d * share + count, :] = both_ref[d, which].astype(F32)[:count]
        if which == 0:
            turned = rows[...].T
            for s in range(parts):
                up_ref[s * width : (s + 1) * width, :] = turned[s * wide_width : s * wide_width + width, :units]
            bias_ref[...] = turned[wide - 8 :, :units]
        else:
            for s in range(parts):
                down_ref[:, s * width : (s + 1) * width] = rows[:units, s * wide_width : s * wide_width + width]


def finish(both, parts, width, share, units):
    ranks, _, slab, wide = both.shape
    channels = parts * width
    return pl.pallas_call(
        functools.partial(finish_kernel, parts=parts, width=width, share=share),
        out_shape=[
            jax.ShapeDtypeStruct((channels, units), F32),
            jax.ShapeDtypeStruct((units, channels), F32),
            jax.ShapeDtypeStruct((8, units), F32),
        ],
        scratch_shapes=[pltpu.VMEM((ceil_to(units, LANES), wide), F32)],
        compiler_params=params(40),
        cost_estimate=cost(5),
        name="finish_weight_gradients",
    )(both)


def gelu_pair(value):
    u = 1.0 + 0.23164189 * jnp.abs(value)
    t = pl.reciprocal(u, approx=True)
    t = t * (2.0 - u * t)
    bell = jnp.exp2(value * value * -0.72134752)
    poly = 0.530702715
    for term in (-0.7265760135, 0.7107068705, -0.142248368, 0.127414796):
        poly = poly * t + term
    tail = poly * t * bell
    below = jnp.where(value >= 0, 1.0 - tail, tail)
    return value * below, below + value * bell * INV_ROOT_TWO_PI


def pointwise_kernel(at_ref, *refs, chips, parts, width, base, over):
    up_refs, down_refs = refs[:chips], refs[chips : 2 * chips]
    data, more_ref, rest = refs[2 * chips : 2 * chips + 4], refs[2 * chips + 4], refs[2 * chips + 5 :]
    outs, (weight_grad_ref, sums_ref) = rest[:8], rest[8:10]
    up_w, down_w, up_t, down_t, up_acc, down_acc, x_place, g_place, hidden, grad_pre = rest[10:]
    whose, c = pl.program_id(0), pl.program_id(1)
    last = (whose == 1) & (c == pl.num_programs(1) - 1)
    _, slab, wide = up_refs[0].shape
    units = chips * parts * slab
    channels = parts * width
    block = units // 8
    me, chip = at_ref[0], at_ref[1 + 2 * parts]
    used = at_ref[1 + whose * parts + me]

    @pl.when((whose == 0) & (c == 0))
    def _():
        for refs, dst in ((up_refs, up_w), (down_refs, down_w)):
            for p in range(chips):
                for q in range(0, parts, 2):
                    pair = jnp.concatenate([refs[p][q].astype(F32), refs[p][q + 1].astype(F32)], axis=0)
                    row = (p * parts + q) * slab
                    dst[row : row + 2 * slab, :] = pair.astype(BF)
        for u in range(0, units, LANES):
            for src, dst in ((up_w, up_t), (down_w, down_t)):
                dst[:, u : u + LANES] = src[u : u + LANES, :].astype(F32).T[:channels, :].astype(BF)
        up_acc[...] = jnp.zeros_like(up_acc)
        down_acc[...] = jnp.zeros_like(down_acc)
        sums_ref[...] = jnp.zeros_like(sums_ref)
        ones = jnp.where(lax.broadcasted_iota(jnp.int32, (8, TILE), 0) == 0, 1.0, 0.0)
        x_place[channels:, :] = ones
        g_place[channels:, :] = jnp.zeros((8, TILE), F32)

    def spots(step):
        first, end = step * TILE, (step + 1) * TILE
        found = []
        if first < base:
            n = min(end, base) - first
            found.append((0, slice(0, n), slice(0, n)))
        if end > base and first < base + over:
            lo, hi = max(first, base), min(end, base + over)
            found.append((1, slice(lo - base, hi - base), slice(lo - first, hi - first)))
        return found

    whole = base // TILE
    steps = -(-(base + over) // TILE)
    cases = ([(c < whole, spots(0))] if whole else []) + [(c == step, spots(step)) for step in range(whole, steps)]
    for side in range(2):
        for case, found in cases:
            here = (whose == side) & case
            x_refs = (data[side], more_ref.at[side, 0])
            g_refs = (data[2 + side], more_ref.at[side, 1])

            @pl.when(here & (c * TILE < used))
            def _():
                for refs, place in ((x_refs, x_place), (g_refs, g_place)):
                    for s in range(parts):
                        k = lax.rem(me - s + parts, parts) if place is x_place else s
                        at = slice(s * width, (s + 1) * width)
                        values = [refs[is_over][s if is_over else k, :, lanes].astype(F32) for is_over, lanes, _ in found]
                        filled = sum(v.shape[1] for v in values)
                        if filled < TILE:
                            values.append(jnp.zeros((width, TILE - filled), F32))
                        place[at, :] = jnp.concatenate(values, axis=1) if len(values) > 1 else values[0]

    @pl.when(c * TILE < used)
    def _():
        x = x_place[...].astype(BF)
        g = g_place[...].astype(BF)

        for i in range(units // block):
            at = pl.ds(i * block, block)
            pre = nn(up_w[at, :], x)
            grad_hidden = nn(down_w[at, :], g)
            value, slope = gelu_pair(pre)
            h = value.astype(BF)
            gp = (grad_hidden * slope).astype(BF)
            hidden[at, :] = h
            grad_pre[at, :] = gp

        for lo in range(0, wide, 2 * LANES):
            hi = min(lo + 2 * LANES, wide)
            up_acc[:, lo:hi] += nt(grad_pre[...], x[lo:hi, :])
            down_acc[:, lo:hi] += nt(hidden[...], g[lo:hi, :])

        def fold(v):
            return sum(v[:, lo : lo + LANES] for lo in range(0, TILE, LANES))

        for s in range(parts):
            rows = slice(s * width, (s + 1) * width)
            k = lax.rem(me - s + parts, parts)
            branch = nn(down_t[rows, :], hidden[...])
            normed = nn(up_t[rows, :], grad_pre[...])
            sums_ref[k, 0] += fold(normed)
            sums_ref[k, 1] += fold(normed * x_place[rows, :])
            for side in range(2):
                for case, found in cases:

                    @pl.when((whose == side) & case)
                    def _():
                        for is_over, lanes, tile in found:
                            to = 2 * side + is_over
                            for value, ref in ((branch, outs[to]), (normed, outs[4 + to])):
                                ref[s if is_over else k, :, lanes] = value[:, tile].astype(ref.dtype)

    @pl.when(last)
    def _():
        for p in range(chips):
            for q in range(parts):
                row = (p * parts + q) * slab
                to = (chip ^ p, q)
                weight_grad_ref[to[0], to[1], 0] = up_acc[row : row + slab, :].astype(BF)
                weight_grad_ref[to[0], to[1], 1] = down_acc[row : row + slab, :].astype(BF)


def pointwise(at, ups, downs, data):
    chips = len(ups)
    parts, width, base = data[0].shape
    over = data[4].shape[4]
    _, slab, wide = ups[0].shape
    units, channels = chips * parts * slab, parts * width
    base_tiles = -(-base // TILE)

    def tile(side, is_over):
        if is_over:
            return pl.BlockSpec((parts, width, over), lambda whose, c, at: (0, 0, 0))

        def place(whose, c, at):
            end = jnp.minimum(jnp.maximum((at[1 + side * parts + at[0]] - 1) // TILE, 0), base_tiles - 1)
            return (0, 0, jnp.where(whose == side, jnp.minimum(c, end), 0 if side else end))

        return pl.BlockSpec((parts, width, TILE), place)

    tiles = [tile(side, is_over) for side in range(2) for is_over in range(2)]
    kinds = [F32, F32, BF, BF]
    result = [jax.ShapeDtypeStruct((parts, width, n), kind) for n, kind in zip((base, over, base, over), kinds)]
    return pl.pallas_call(
        functools.partial(pointwise_kernel, chips=chips, parts=parts, width=width, base=base, over=over),
        grid_spec=pltpu.PrefetchScalarGridSpec(
            num_scalar_prefetch=1,
            grid=(2, -(-(base + over) // TILE)),
            in_specs=[
                pl.BlockSpec(ups[0].shape, lambda w, c, at: (0, 0, 0), pipeline_mode=pl.Buffered(1))
                for _ in range(2 * chips)
            ]
            + [tile(0, 0), tile(1, 0), tile(0, 0), tile(1, 0)]
            + [pl.BlockSpec(data[4].shape, lambda w, c, at: (0, 0, 0, 0, 0), pipeline_mode=pl.Buffered(1))],
            out_specs=tiles
            + tiles
            + [
                pl.BlockSpec((chips, parts, 2, slab, wide), lambda w, c, at: (0, 0, 0, 0, 0)),
                pl.BlockSpec((parts, 2, width, LANES), lambda w, c, at: (0, 0, 0, 0)),
            ],
            scratch_shapes=[
                pltpu.VMEM((units, wide), BF),
                pltpu.VMEM((units, wide), BF),
                pltpu.VMEM((channels, units), BF),
                pltpu.VMEM((channels, units), BF),
                pltpu.VMEM((units, wide), F32),
                pltpu.VMEM((units, wide), F32),
                pltpu.VMEM((wide, TILE), F32),
                pltpu.VMEM((wide, TILE), F32),
                pltpu.VMEM((units, TILE), BF),
                pltpu.VMEM((units, TILE), BF),
            ],
        ),
        out_shape=result
        + result
        + [
            jax.ShapeDtypeStruct((chips, parts, 2, slab, wide), BF),
            jax.ShapeDtypeStruct((parts, 2, width, LANES), F32),
        ],
        compiler_params=params(62),
        cost_estimate=cost(70),
        name="pointwise",
    )(at, *ups, *downs, *data)


def per_device(
    inputs,
    crop_sizes,
    land_mask,
    conv_weight,
    norm_gain,
    norm_shift,
    up_weight,
    up_bias,
    down_weight,
    down_bias,
    cotangent,
    *,
    sizes,
):
    chips, cores, parts = sizes
    crops, side, _, width = inputs.shape
    taps = conv_weight.shape[0]
    cells = crops * side * side // parts
    local_units = up_weight.shape[1]
    channels = up_weight.shape[0]
    me = lax.axis_index("mp")
    core = lax.axis_index("core")
    chip = lax.axis_index("xy")

    def ring(k):
        return [(i, (i + k) % parts) for i in range(parts)]

    def everywhere(value, axes):
        for axis in axes:
            size = {"xy": chips, "core": cores, "mp": parts}[axis]
            if size <= 4:
                others = [lax.ppermute(value, axis, [(i, i ^ j) for i in range(size)]) for j in range(1, size)]
                value = sum(others, value)
                continue
            step = 1
            while step < size:
                value = value + lax.ppermute(value, axis, [(i, i ^ step) for i in range(size)])
                step *= 2
        return value

    def ring_back(k):
        return [(i, (i - k) % parts) for i in range(parts)]

    def to_parts(pieces, ring=ring):
        return [pieces[0]] + [lax.ppermute(pieces[k], "mp", ring(k)) for k in range(1, parts)]

    def exchange(by_part):
        return lax.all_to_all(by_part, "mp", 0, 0, tiled=True)

    swap = [(i, cores - 1 - i) for i in range(cores)]

    def to_core(value):
        return lax.ppermute(value, "core", swap)

    share = -(-local_units // (chips * cores))
    slab = ceil_to(share, 8)
    wide_width = ceil_to(width, 8)
    wide = parts * wide_width + 8
    rank = chip * cores + core
    spare = chips * cores * share - local_units

    def take(rows):
        rows = jnp.pad(rows, ((0, spare), (0, 0))) if spare else rows
        rows = lax.dynamic_slice_in_dim(rows, rank * share, share, axis=0)
        if wide_width > width:
            rows = jnp.pad(rows.reshape(share, parts, width), ((0, 0), (0, 0), (0, wide_width - width)))
        return rows.reshape(share, -1)

    own_bias = up_bias[:, None]
    own_bias = jnp.pad(own_bias, ((0, spare), (0, 0))) if spare else own_bias
    own_bias = lax.dynamic_slice_in_dim(own_bias, rank * share, share, axis=0)
    up_rows = jnp.pad(jnp.concatenate([take(up_weight.T), own_bias], axis=1), ((0, slab - share), (0, 7)))
    down_rows = jnp.pad(take(down_weight), ((0, slab - share), (0, 8)))
    rows = lax.all_gather(jnp.stack([up_rows, down_rows]), "mp", axis=1, tiled=False)

    def over_plane(own, bits):
        held = {0: own}
        for bit in bits:
            pairs = [(i, i ^ bit) for i in range(chips)]
            held.update({p ^ bit: lax.ppermute(value, "xy", pairs) for p, value in list(held.items())})
        return [held[p] for p in range(chips)]

    index = jnp.arange(side, dtype=jnp.int32)
    inside = (index[None, :, None] < crop_sizes[:, 0][:, None, None]) & (
        index[None, None, :] < crop_sizes[:, 1][:, None, None]
    )
    usable = jnp.where(inside, land_mask, 0)
    lane_mask = jnp.broadcast_to(usable[..., None].astype(BF), usable.shape + (LANES,))
    by_part = usable.reshape(crops, side // parts, parts, side).transpose(2, 0, 1, 3).reshape(parts, -1, side)
    by_part = by_part.astype(F32)
    lines = by_part.shape[1]
    upto = jnp.dot(by_part, jnp.triu(jnp.ones((side, side), F32)))
    before = jnp.dot(upto[:, :, -1], jnp.triu(jnp.ones((lines, lines), F32), 1))
    slots = jnp.where(by_part > 0, upto + before[:, :, None] - 1, -1).astype(jnp.int32)
    counts = jnp.sum(by_part, axis=(1, 2)).astype(jnp.int32)
    columns = jnp.broadcast_to(slots.reshape(parts, crops, -1)[..., None], (parts, crops, cells // crops, LANES))
    slots = slots.reshape(parts, 1, cells)
    ends = jnp.cumsum(jnp.sum(by_part.reshape(parts, crops, -1), axis=2), axis=1)
    reaches = jnp.pad(ends, ((0, 0), (1, 0))).astype(jnp.int32).reshape(-1)
    at = jnp.concatenate([me[None].astype(jnp.int32), counts, to_core(counts), chip[None].astype(jnp.int32), reaches])

    base = ceil_to(cells * 7 // 9, LANES)
    over = ceil_to(cells, LANES) - base
    over_full = jnp.where(jnp.max(counts) > base, 1.0, 0.0)

    cot_base, cot_over, down_bias_local = pack_cotangent(at, cotangent, lane_mask, slots, base, over)
    inputs, cot_base = after(inputs, cot_base)
    grad_base = exchange(cot_base)

    wide_taps = spread_rows(conv_weight.reshape(taps * taps, width))
    convolved, stats = conv_forward(inputs, lane_mask, wide_taps, taps, parts)
    stats = jnp.sum(stats, axis=(0, 3)).reshape(2, -1)[:, :width]
    extra = jnp.pad(jnp.stack([jnp.sum(by_part), over_full])[None], ((0, 0), (0, width - 2)))
    stats = everywhere(jnp.concatenate([stats, extra, jnp.sum(down_bias_local, axis=0)[None]]), ("core", "xy"))
    stats, rows = after(stats, rows)
    bits = [1 << j for j in range(chips.bit_length() - 1)]

    def double(held, bit):
        pairs = [(i, i ^ bit) for i in range(chips)]
        return {**held, **{p ^ bit: lax.ppermute(value, "xy", pairs) for p, value in held.items()}}

    ups, downs = {0: rows[0]}, {0: rows[1]}
    ups, downs = double(ups, bits[0]), double(downs, bits[-1])
    ocean_count = stats[2, 0]
    overflows = stats[2, 1] > 0
    down_bias_grad = stats[3]
    channel_mean = stats[0] / ocean_count
    inv_std = lax.rsqrt(stats[1] / ocean_count - channel_mean * channel_mean + EPSILON)
    gain = norm_gain.astype(F32)
    shift = norm_shift.astype(F32)
    scale = gain * inv_std

    affine = jnp.stack([scale, shift - channel_mean * scale])
    normed_base, normed_over = pack_normed(at, convolved.reshape(parts, cells, width), affine, slots, base, over)
    places = sorted(ups), sorted(downs)
    *both, grad_base = after(*normed_base, *[ups[p] for p in places[0]], *[downs[p] for p in places[1]], grad_base)
    normed_base, held = both[:parts], both[parts:]
    ups, downs = dict(zip(places[0], held)), dict(zip(places[1], held[len(ups) :]))
    for j in range(1, len(bits)):
        ups, downs = double(ups, bits[j]), double(downs, bits[-1 - j])
    ups, downs = [ups[p] for p in range(chips)], [downs[p] for p in range(chips)]
    *both, crowded = after(*to_parts(normed_base), *ups, *downs, overflows)
    x_base, ups, downs = jnp.stack(both[:parts]), both[parts : parts + chips], both[parts + chips :]

    def overflow_in():
        own = jnp.stack([exchange(normed_over), exchange(cot_over)])
        return jnp.stack([own, to_core(own)])

    more = lax.cond(crowded, overflow_in, lambda: jnp.zeros((2, 2, parts, wide_width, over), BF))
    data = [x_base, to_core(x_base), grad_base, to_core(grad_base), more]
    *sums_out, weight_grad, sums = pointwise(at, ups, downs, data)
    branch, normed = list(sums_out[:4]), list(sums_out[4:])

    def over_cores(own, far):
        far = to_core(far)
        return [(own[k] + far[k].astype(F32)).astype(BF) for k in range(parts)]

    def home(total):
        return to_parts(total, ring_back)

    sums = everywhere(jnp.sum(sums, axis=3), ("core", "xy"))
    sums = sum(to_parts([sums[k] for k in range(parts)], ring_back))[:, :width]
    total, sums = after(tuple(over_cores(normed[0], normed[2])), sums)
    normed_base = home(total)
    total = over_cores(branch[0], branch[2])
    crowded, total, sums, columns, *normed_base = after(overflows, tuple(total), sums, columns, *normed_base)

    def overflow_out():
        return jnp.stack([exchange(jnp.stack(over_cores(v[1], v[3]))) for v in (branch, normed)])

    more = lax.cond(crowded, overflow_out, lambda: jnp.zeros((2, parts, wide_width, over), BF))

    shift_grad = sums[0]
    gain_grad = (sums[1] - shift * shift_grad) / gain
    vectors = jnp.stack([channel_mean, scale, scale * shift_grad / ocean_count, scale * inv_std * gain_grad / ocean_count])
    total, more = after(total, more)
    branch_base = home(total)

    own = lax.psum_scatter(weight_grad, "xy", scatter_dimension=0, tiled=False)
    own, vectors, *normed_base = after(own, spread_rows(vectors), *normed_base)
    own = lax.psum_scatter(own, "mp", scatter_dimension=0, tiled=False)
    input_grad, grad_conv = input_gradient(
        at, lane_mask, cotangent, convolved, wide_taps, vectors, columns, [*normed_base, more], taps
    )
    own, grad_conv = after(own, grad_conv)
    both = lax.all_gather(own, ("xy", "core"), axis=0, tiled=False)
    taps_local = taps_gradient(inputs, lane_mask, grad_conv, taps)
    output = make_output(at, inputs, lane_mask, down_bias.astype(F32)[None], columns, [*branch_base, more])
    taps_local = jnp.sum(taps_local, axis=2).transpose(1, 0, 2).reshape(taps * taps, -1)
    conv_weight_grad = everywhere(taps_local, ("core", "xy"))[:, :width].reshape(taps, taps, width)
    up_weight_grad, down_weight_grad, bias_rows = finish(both, parts, width, share, local_units)
    up_bias_grad = bias_rows[0]
    return (
        output,
        input_grad,
        conv_weight_grad,
        gain_grad,
        shift_grad,
        up_weight_grad,
        up_bias_grad,
        down_weight_grad,
        down_bias_grad,
    )


def solution(mesh):
    cores = 2
    parts = mesh.shape["mp"]
    chips = mesh.shape["dp"] // cores
    fine = Mesh(np.asarray(mesh.devices).reshape(chips, cores, parts), ("xy", "core", "mp"))
    dp = ("xy", "core")
    specs = (
        P(dp, None, None, "mp"),
        P(dp, None),
        P(dp, None, None),
        P(None, None, "mp"),
        P("mp"),
        P("mp"),
        P(None, "mp"),
        P("mp"),
        P("mp", None),
        P("mp"),
        P(dp, None, None, "mp"),
    )
    results = (
        P(dp, None, None, "mp"),
        P(dp, None, None, "mp"),
        P(None, None, "mp"),
        P("mp"),
        P("mp"),
        P(None, "mp"),
        P("mp"),
        P("mp", None),
        P("mp"),
    )
    return jax.shard_map(
        functools.partial(per_device, sizes=(chips, cores, parts)),
        mesh=fine,
        in_specs=specs,
        out_specs=results,
        check_vma=False,
    )
```

```python
import functools

import jax
import jax.numpy as jnp
import numpy as np
from jax import lax
from jax.experimental import pallas as pl
from jax.experimental.pallas import tpu as pltpu
from jax.sharding import Mesh
from jax.sharding import PartitionSpec as P

F32 = jnp.float32
BF = jnp.bfloat16
EPSILON = 1e-05
INV_ROOT_TWO_PI = 0.3989422804014327
LANES = 128
LEFT = 8
MIB = 2**20
TILE = 256


def ceil_to(value, unit):
    return -(-value // unit) * unit


def lane_tiles(width):
    return -(-width // LANES)


def spread_rows(rows):
    count, width = rows.shape
    tiles = lane_tiles(width)
    flat = jnp.pad(rows.astype(F32), ((0, 0), (0, tiles * LANES - width)))
    flat = flat.reshape(count, tiles, 1, LANES).transpose(1, 0, 2, 3)
    return jnp.broadcast_to(flat, (tiles, count, 8, LANES))


def after(*values):
    return lax.optimization_barrier(values)


def params(mib, **more):
    return pltpu.CompilerParams(vmem_limit_bytes=mib * MIB, **more)


def whole(array):
    zeros = (0,) * array.ndim
    return pl.BlockSpec(array.shape, lambda n, at: zeros)


EAGERNESS = 6


def cost(micros):
    return pl.CostEstimate(flops=int(micros * 1.15e9 / EAGERNESS), bytes_accessed=0, transcendentals=0)


def clear_borders(dst, half, side):
    tiles, _, cols, _ = dst.shape
    for t in range(tiles):
        for r in list(range(half)) + list(range(half + side, side + 2 * half)):
            dst[t, r] = jnp.zeros((cols, LANES), F32)

        @pl.loop(0, side)
        def _(r):
            dst[t, r + half, 0:LEFT, :] = jnp.zeros((LEFT, LANES), F32)
            dst[t, r + half, LEFT + side : cols, :] = jnp.zeros((cols - LEFT - side, LANES), F32)


def fill_masked(dst, x_ref, m_ref, half):
    _, side, _, width = x_ref.shape
    for t in range(lane_tiles(width)):
        lo, hi = t * LANES, min((t + 1) * LANES, width)

        @pl.loop(0, side)
        def _(r):
            value = x_ref[0, r, :, lo:hi].astype(F32) * m_ref[0, r, :, : hi - lo].astype(F32)
            dst[t, r + half, LEFT : LEFT + side, 0 : hi - lo] = value


def conv_rows(src, w_ref, t, r0, c0, rows, groups, taps, flipped):
    half = taps // 2
    acc = [jnp.zeros((groups, 8, LANES), F32) for _ in range(rows)]
    for b in range(taps):
        shift = (taps - 1 - b) if flipped else b
        weights = [w_ref[t, a * taps + b] for a in range(taps)]
        for i in range(rows + taps - 1):
            x = src[t, r0 + i, pl.ds(LEFT + c0 + shift - half, groups * 8), :].reshape(groups, 8, LANES)
            for r in range(max(0, i - taps + 1), min(rows, i + 1)):
                a = taps - 1 - (i - r) if flipped else i - r
                acc[r] = acc[r] + x * weights[a][None]
    return acc


def forward_kernel(x_ref, m_ref, w_ref, conv_ref, stat_ref, xs, *, taps, rows, groups):
    _, side, _, width = x_ref.shape
    parts = conv_ref.shape[0]
    half = taps // 2
    clear_borders(xs, half, side)
    fill_masked(xs, x_ref, m_ref, half)
    for t in range(lane_tiles(width)):
        lo, hi = t * LANES, min((t + 1) * LANES, width)

        def block(i, carry):
            first, second = carry
            r0 = i * rows
            for c0 in range(0, side, groups * 8):
                acc = conv_rows(xs, w_ref, t, r0, c0, rows, groups, taps, False)
                for r in range(rows):
                    m = m_ref[0, r0 + r, c0 : c0 + groups * 8, :].astype(F32).reshape(groups, 8, LANES)
                    cm = acc[r] * m
                    first = first + jnp.sum(cm, axis=0)
                    second = second + jnp.sum(cm * acc[r], axis=0)
                    if rows % parts == 0:
                        part, row = r % parts, i * (rows // parts) + r // parts
                    else:
                        part, row = lax.rem(r0 + r, parts), lax.div(r0 + r, parts)
                    conv_ref[part, 0, row, c0 : c0 + groups * 8, lo:hi] = acc[r].reshape(groups * 8, LANES)[:, : hi - lo]
            return first, second

        zero = jnp.zeros((8, LANES), F32)
        first, second = lax.fori_loop(0, side // rows, block, (zero, zero))
        stat_ref[0, 0, t] = first
        stat_ref[0, 1, t] = second


def conv_forward(x, lane_mask, wide_taps, taps, parts, rows=12, groups=2):
    crops, side, _, width = x.shape
    tiles, half = lane_tiles(width), taps // 2
    return pl.pallas_call(
        functools.partial(forward_kernel, taps=taps, rows=rows, groups=groups),
        grid=(crops,),
        in_specs=[
            pl.BlockSpec((1, side, side, width), lambda n: (n, 0, 0, 0)),
            pl.BlockSpec((1, side, side, LANES), lambda n: (n, 0, 0, 0)),
            pl.BlockSpec(wide_taps.shape, lambda n: (0, 0, 0, 0)),
        ],
        out_specs=[
            pl.BlockSpec((parts, 1, side // parts, side, width), lambda n: (0, n, 0, 0, 0)),
            pl.BlockSpec((1, 2, tiles, 8, LANES), lambda n: (n, 0, 0, 0, 0)),
        ],
        out_shape=[
            jax.ShapeDtypeStruct((parts, crops, side // parts, side, width), F32),
            jax.ShapeDtypeStruct((crops, 2, tiles, 8, LANES), F32),
        ],
        scratch_shapes=[pltpu.VMEM((tiles, side + 2 * half, LEFT + side + 8, LANES), F32)],
        compiler_params=params(32),
        cost_estimate=cost(22),
        name="depthwise_forward",
    )(x, lane_mask, wide_taps)


def chooser(slot_of_cell, start, count):
    cells = slot_of_cell.shape[1]
    rows = lax.broadcasted_iota(jnp.int32, (count, cells), 0) + start
    return jnp.where(rows == slot_of_cell, 1.0, 0.0).astype(BF)


def nt(left, right):
    return lax.dot_general(left, right, (((1,), (1,)), ((), ())), preferred_element_type=F32)


def nn(left, right):
    return jnp.dot(left, right, preferred_element_type=F32)


def segments(base, over):
    cuts = sorted({*range(0, base + over, TILE), base, base + over})
    return [
        (int(lo >= base), lo - base if lo >= base else lo, lo, hi - lo) for lo, hi in zip(cuts, cuts[1:]) if hi <= base + over
    ]


def pack_columns(values, slots, used, base_ref, over_ref):
    width = values.shape[0]
    for is_over, lo, start, count in segments(base_ref.shape[1], over_ref.shape[1]):
        ref = over_ref if is_over else base_ref

        @pl.when(start < used)
        def _():
            ref[:width, lo : lo + count] = nt(values, chooser(slots, start, count)).astype(BF)

        @pl.when(start >= used)
        def _():
            ref[:width, lo : lo + count] = jnp.zeros((width, count), BF)

        if width < ref.shape[0]:
            ref[width:, lo : lo + count] = jnp.zeros((ref.shape[0] - width, count), BF)


def pack_normed_kernel(at_ref, conv_ref, vec_ref, slot_ref, base_ref, over_ref):
    normed = (conv_ref[0] * vec_ref[0:1, :] + vec_ref[1:2, :]).T.astype(BF)
    used = at_ref[1 + pl.program_id(0)]
    pack_columns(normed, slot_ref[0], used, base_ref.at[0], over_ref.at[0])


def pack_normed(at, conv, vec, slots, base, over):
    parts, cells, width = conv.shape
    wide = ceil_to(width, 8)
    return pl.pallas_call(
        pack_normed_kernel,
        grid_spec=pltpu.PrefetchScalarGridSpec(
            num_scalar_prefetch=1,
            grid=(parts,),
            in_specs=[
                pl.BlockSpec((1, cells, width), lambda k, at: (k, 0, 0)),
                pl.BlockSpec(vec.shape, lambda k, at: (0, 0)),
                pl.BlockSpec((1, 1, cells), lambda k, at: (k, 0, 0)),
            ],
            out_specs=[
                pl.BlockSpec((1, wide, base), lambda k, at: (k, 0, 0)),
                pl.BlockSpec((1, wide, over), lambda k, at: (k, 0, 0)),
            ],
        ),
        out_shape=[jax.ShapeDtypeStruct((parts, wide, base), BF), jax.ShapeDtypeStruct((parts, wide, over), BF)],
        compiler_params=params(32),
        cost_estimate=cost(8),
        name="pack_normed",
    )(at, conv, vec, slots)


def pack_cotangent_kernel(at_ref, cot_ref, m_ref, slot_ref, base_ref, over_ref, sum_ref, rows):
    crops, side, _, width = cot_ref.shape
    part, parts = pl.program_id(0), pl.num_programs(0)
    per = rows.shape[0] // (crops * side)
    total = jnp.zeros((8, width), F32)
    for n in range(crops):

        def body(i, total):
            r = i * parts + part
            masks = [m_ref[n, r, :, : min(LANES, width - lo)] for lo in range(0, width, LANES)]
            mask = jnp.concatenate(masks, axis=1) if len(masks) > 1 else masks[0]
            value = cot_ref[n, r].astype(F32) * mask.astype(F32)
            rows[pl.ds(pl.multiple_of((n * per + i) * side, 8), side), :] = value
            return total + jnp.sum(value.reshape(side // 8, 8, width), axis=0)

        total = lax.fori_loop(0, per, body, total)

    @pl.when(part == 0)
    def _():
        sum_ref[...] = total

    @pl.when(part > 0)
    def _():
        sum_ref[...] += total

    pack_columns(rows[...].T.astype(BF), slot_ref[0], at_ref[1 + part], base_ref.at[0], over_ref.at[0])


def pack_cotangent(at, cot, lane_mask, slots, base, over):
    crops, side, _, width = cot.shape
    parts, _, cells = slots.shape
    wide = ceil_to(width, 8)
    return pl.pallas_call(
        pack_cotangent_kernel,
        grid_spec=pltpu.PrefetchScalarGridSpec(
            num_scalar_prefetch=1,
            grid=(parts,),
            in_specs=[
                pl.BlockSpec(cot.shape, lambda k, at: (0, 0, 0, 0)),
                pl.BlockSpec(lane_mask.shape, lambda k, at: (0, 0, 0, 0)),
                pl.BlockSpec((1, 1, cells), lambda k, at: (k, 0, 0)),
            ],
            out_specs=[
                pl.BlockSpec((1, wide, base), lambda k, at: (k, 0, 0)),
                pl.BlockSpec((1, wide, over), lambda k, at: (k, 0, 0)),
                pl.BlockSpec((8, width), lambda k, at: (0, 0)),
            ],
            scratch_shapes=[pltpu.VMEM((cells, width), F32)],
        ),
        out_shape=[
            jax.ShapeDtypeStruct((parts, wide, base), BF),
            jax.ShapeDtypeStruct((parts, wide, over), BF),
            jax.ShapeDtypeStruct((8, width), F32),
        ],
        compiler_params=params(40),
        cost_estimate=cost(10),
        name="pack_cotangent",
    )(at, cot, lane_mask, slots)


def expand(base_ref, over_ref, slot_column, reach, acc):
    cells, width = acc.shape
    acc[...] = jnp.zeros_like(acc)
    for is_over, lo, start, count in segments(base_ref.shape[1], over_ref.shape[1]):
        ref = over_ref if is_over else base_ref

        @pl.when((start < reach[1]) & (start + count > reach[0]))
        def _():
            lanes = lax.broadcasted_iota(jnp.int32, (cells, LANES), 1) + start
            choice = jnp.concatenate(
                [jnp.where(lanes + j == slot_column, 1.0, 0.0).astype(BF) for j in range(0, count, LANES)], axis=1
            )
            acc[...] += nt(choice, ref[:width, lo : lo + count])


def reach_of(at_ref, parts, part, crop):
    crops = (at_ref.shape[0] - (2 + 2 * parts)) // parts - 1
    place = 2 + 2 * parts + part * (crops + 1) + crop
    return at_ref[place], at_ref[place + 1]


def output_kernel(at_ref, x_ref, m_ref, bias_ref, column_ref, *refs):
    piece_refs, out_ref, acc = refs[:-2], refs[-2], refs[-1]
    parts = len(piece_refs) - 1
    _, side, _, width = x_ref.shape
    per = side // parts
    for k in range(parts):
        part = lax.rem(at_ref[0] + k, parts)
        reach = reach_of(at_ref, parts, part, pl.program_id(0))
        expand(piece_refs[k], piece_refs[parts].at[0, part], column_ref[part, 0], reach, acc)

        @pl.loop(0, per)
        def _(i):
            r = i * parts + part
            start = pl.multiple_of(i * side, 8)
            for lo in range(0, width, LANES):
                hi = min(lo + LANES, width)
                value = x_ref[0, r, :, lo:hi].astype(F32) + acc[pl.ds(start, side), lo:hi] + bias_ref[0:1, lo:hi]
                out_ref[0, r, :, lo:hi] = (m_ref[0, r, :, : hi - lo].astype(F32) * value).astype(BF)


def make_output(at, x, lane_mask, bias, columns, pieces):
    parts = len(pieces) - 1
    crops, side, _, width = x.shape
    cells = side * side // parts
    field = pl.BlockSpec((1, side, side, width), lambda n, at: (n, 0, 0, 0))
    return pl.pallas_call(
        output_kernel,
        grid_spec=pltpu.PrefetchScalarGridSpec(
            num_scalar_prefetch=1,
            grid=(crops,),
            in_specs=[
                field,
                pl.BlockSpec((1, side, side, LANES), lambda n, at: (n, 0, 0, 0)),
                pl.BlockSpec((1, width), lambda n, at: (0, 0)),
                pl.BlockSpec((parts, 1, cells, LANES), lambda n, at: (0, n, 0, 0)),
            ]
            + [whole(p) for p in pieces],
            out_specs=field,
            scratch_shapes=[pltpu.VMEM((cells, width), F32)],
        ),
        out_shape=jax.ShapeDtypeStruct(x.shape, BF),
        compiler_params=params(60),
        cost_estimate=cost(12),
        name="make_output",
    )(at, x, lane_mask, bias, columns, *pieces)


def input_gradient_kernel(at_ref, m_ref, cot_ref, conv_ref, w_ref, v_ref, column_ref, *refs, taps, rows, groups):
    piece_refs, dx_ref, gs_ref, acc_ref = refs[:-3], refs[-3], refs[-2], refs[-1]
    gs = gs_ref.at[0]
    parts = len(piece_refs) - 1
    _, side, _, width = cot_ref.shape
    per = side // parts
    half = taps // 2
    clear_borders(gs, half, side)
    for k in range(parts):
        part = lax.rem(at_ref[0] + k, parts)
        reach = reach_of(at_ref, parts, part, pl.program_id(0))
        expand(piece_refs[k], piece_refs[parts].at[1, part], column_ref[part, 0], reach, acc_ref)

        @pl.loop(0, per)
        def _(i):
            r = i * parts + part
            start = pl.multiple_of(i * side, 8)
            for t in range(lane_tiles(width)):
                lo, hi = t * LANES, min((t + 1) * LANES, width)
                n = hi - lo
                shape = (side // 8, 8, n)
                m = m_ref[0, r, :, :n].astype(F32).reshape(shape)
                centred = conv_ref[part, 0, i, :, lo:hi].reshape(shape) - v_ref[t, 0, :, :n][None]
                gn = acc_ref[pl.ds(start, side), lo:hi].reshape(shape)
                g = v_ref[t, 1, :, :n][None] * gn - m * (v_ref[t, 2, :, :n][None] + centred * v_ref[t, 3, :, :n][None])
                gs[t, r + half, LEFT : LEFT + side, 0:n] = g.reshape(side, n)

    for t in range(lane_tiles(width)):
        lo, hi = t * LANES, min((t + 1) * LANES, width)
        n = hi - lo

        @pl.loop(0, side // rows)
        def _(i):
            r0 = i * rows
            for c0 in range(0, side, groups * 8):
                acc = conv_rows(gs, w_ref, t, r0, c0, rows, groups, taps, True)
                for r in range(rows):
                    m = m_ref[0, r0 + r, c0 : c0 + groups * 8, :n].astype(F32)
                    cot = cot_ref[0, r0 + r, c0 : c0 + groups * 8, lo:hi].astype(F32)
                    value = m * (cot + acc[r].reshape(groups * 8, LANES)[:, :n])
                    dx_ref[0, r0 + r, c0 : c0 + groups * 8, lo:hi] = value.astype(BF)


def input_gradient(at, lane_mask, cot, conv, wide_taps, vectors, columns, pieces, taps, rows=12, groups=2):
    parts = len(pieces) - 1
    crops, side, _, width = cot.shape
    tiles, half = lane_tiles(width), taps // 2
    cells = side * side // parts
    field = pl.BlockSpec((1, side, side, width), lambda n, at: (n, 0, 0, 0))
    padded = (tiles, side + 2 * half, LEFT + side + 8, LANES)
    return pl.pallas_call(
        functools.partial(input_gradient_kernel, taps=taps, rows=rows, groups=groups),
        grid_spec=pltpu.PrefetchScalarGridSpec(
            num_scalar_prefetch=1,
            grid=(crops,),
            in_specs=[
                pl.BlockSpec((1, side, side, LANES), lambda n, at: (n, 0, 0, 0)),
                field,
                pl.BlockSpec((parts, 1, side // parts, side, width), lambda n, at: (0, n, 0, 0, 0)),
                pl.BlockSpec(wide_taps.shape, lambda n, at: (0, 0, 0, 0)),
                pl.BlockSpec(vectors.shape, lambda n, at: (0, 0, 0, 0)),
                pl.BlockSpec((parts, 1, cells, LANES), lambda n, at: (0, n, 0, 0)),
            ]
            + [whole(p) for p in pieces],
            out_specs=[field, pl.BlockSpec((1, *padded), lambda n, at: (n, 0, 0, 0, 0))],
            scratch_shapes=[pltpu.VMEM((cells, width), F32)],
        ),
        out_shape=[jax.ShapeDtypeStruct(cot.shape, BF), jax.ShapeDtypeStruct((crops, *padded), F32)],
        compiler_params=params(60),
        cost_estimate=cost(28),
        name="input_gradient",
    )(at, lane_mask, cot, conv, wide_taps, vectors, columns, *pieces)


def taps_gradient_kernel(x_ref, m_ref, gs_ref, dw_ref, xs, *, taps, rows, groups):
    _, side, _, width = x_ref.shape
    half = taps // 2
    span = groups * 8

    @pl.when(pl.program_id(0) == 0)
    def _():
        dw_ref[...] = jnp.zeros_like(dw_ref)

    clear_borders(xs, half, side)
    fill_masked(xs, x_ref, m_ref, half)
    for t in range(lane_tiles(width)):

        @pl.loop(0, side // rows)
        def _(i):
            r0 = i * rows
            for c0 in range(0, side, span):
                grads = [
                    gs_ref[0, t, r0 + half + r, LEFT + c0 : LEFT + c0 + span, :].reshape(groups, 8, LANES)
                    for r in range(rows)
                ]
                for b in range(taps):
                    acc = [jnp.zeros((groups, 8, LANES), F32) for _ in range(taps)]
                    for j in range(rows + taps - 1):
                        x = xs[t, r0 + j, pl.ds(LEFT + c0 + b - half, span), :].reshape(groups, 8, LANES)
                        for r in range(max(0, j - taps + 1), min(rows, j + 1)):
                            acc[j - r] = acc[j - r] + x * grads[r]
                    for a in range(taps):
                        dw_ref[t, a * taps + b] += jnp.sum(acc[a], axis=0)


def taps_gradient(x, lane_mask, gs, taps, rows=8, groups=2):
    crops, side, _, width = x.shape
    tiles = lane_tiles(width)
    return pl.pallas_call(
        functools.partial(taps_gradient_kernel, taps=taps, rows=rows, groups=groups),
        grid=(crops,),
        in_specs=[
            pl.BlockSpec((1, side, side, width), lambda n: (n, 0, 0, 0)),
            pl.BlockSpec((1, side, side, LANES), lambda n: (n, 0, 0, 0)),
            pl.BlockSpec((1, *gs.shape[1:]), lambda n: (n, 0, 0, 0, 0)),
        ],
        out_specs=pl.BlockSpec((tiles, taps * taps, 8, LANES), lambda n: (0, 0, 0, 0)),
        out_shape=jax.ShapeDtypeStruct((tiles, taps * taps, 8, LANES), F32),
        scratch_shapes=[pltpu.VMEM(gs.shape[1:], F32)],
        compiler_params=params(60),
        cost_estimate=cost(22),
        name="taps_gradient",
    )(x, lane_mask, gs)


def finish_kernel(both_ref, up_ref, down_ref, bias_ref, rows, *, parts, width, share):
    ranks, _, _, wide = both_ref.shape
    units = down_ref.shape[0]
    wide_width = (wide - 8) // parts
    for which in range(2):
        for d in range(ranks):
            count = min(share, units - d * share)
            if count > 0:
                rows[d * share : d * share + count, :] = both_ref[d, which].astype(F32)[:count]
        if which == 0:
            turned = rows[...].T
            for s in range(parts):
                up_ref[s * width : (s + 1) * width, :] = turned[s * wide_width : s * wide_width + width, :units]
            bias_ref[...] = turned[wide - 8 :, :units]
        else:
            for s in range(parts):
                down_ref[:, s * width : (s + 1) * width] = rows[:units, s * wide_width : s * wide_width + width]


def finish(both, parts, width, share, units):
    ranks, _, slab, wide = both.shape
    channels = parts * width
    return pl.pallas_call(
        functools.partial(finish_kernel, parts=parts, width=width, share=share),
        out_shape=[
            jax.ShapeDtypeStruct((channels, units), F32),
            jax.ShapeDtypeStruct((units, channels), F32),
            jax.ShapeDtypeStruct((8, units), F32),
        ],
        scratch_shapes=[pltpu.VMEM((ceil_to(units, LANES), wide), F32)],
        compiler_params=params(40),
        cost_estimate=cost(5),
        name="finish_weight_gradients",
    )(both)


def gelu_pair(value):
    u = 1.0 + 0.23164189 * jnp.abs(value)
    t = pl.reciprocal(u, approx=True)
    t = t * (2.0 - u * t)
    bell = jnp.exp2(value * value * -0.72134752)
    poly = 0.530702715
    for term in (-0.7265760135, 0.7107068705, -0.142248368, 0.127414796):
        poly = poly * t + term
    tail = poly * t * bell
    below = jnp.where(value >= 0, 1.0 - tail, tail)
    return value * below, below + value * bell * INV_ROOT_TWO_PI


def pointwise_kernel(at_ref, *refs, chips, parts, width, base, over):
    up_refs, down_refs = refs[:chips], refs[chips : 2 * chips]
    data, more_ref, rest = refs[2 * chips : 2 * chips + 4], refs[2 * chips + 4], refs[2 * chips + 5 :]
    outs, (weight_grad_ref, sums_ref) = rest[:8], rest[8:10]
    up_w, down_w, up_t, down_t, up_acc, down_acc, x_place, g_place, hidden, grad_pre = rest[10:]
    whose, c = pl.program_id(0), pl.program_id(1)
    last = (whose == 1) & (c == pl.num_programs(1) - 1)
    _, slab, wide = up_refs[0].shape
    units = chips * parts * slab
    channels = parts * width
    block = LANES
    me, chip = at_ref[0], at_ref[1 + 2 * parts]
    used = at_ref[1 + whose * parts + me]

    @pl.when((whose == 0) & (c == 0))
    def _():
        for refs, dst in ((up_refs, up_w), (down_refs, down_w)):
            for p in range(chips):
                for q in range(0, parts, 2):
                    pair = jnp.concatenate([refs[p][q].astype(F32), refs[p][q + 1].astype(F32)], axis=0)
                    row = (p * parts + q) * slab
                    dst[row : row + 2 * slab, :] = pair.astype(BF)
        for u in range(0, units, LANES):
            for src, dst in ((up_w, up_t), (down_w, down_t)):
                dst[:, u : u + LANES] = src[u : u + LANES, :].astype(F32).T[:channels, :].astype(BF)
        up_acc[...] = jnp.zeros_like(up_acc)
        down_acc[...] = jnp.zeros_like(down_acc)
        sums_ref[...] = jnp.zeros_like(sums_ref)
        ones = jnp.where(lax.broadcasted_iota(jnp.int32, (8, TILE), 0) == 0, 1.0, 0.0)
        x_place[channels:, :] = ones
        g_place[channels:, :] = jnp.zeros((8, TILE), F32)

    def spots(step):
        first, end = step * TILE, (step + 1) * TILE
        found = []
        if first < base:
            n = min(end, base) - first
            found.append((0, slice(0, n), slice(0, n)))
        if end > base and first < base + over:
            lo, hi = max(first, base), min(end, base + over)
            found.append((1, slice(lo - base, hi - base), slice(lo - first, hi - first)))
        return found

    whole = base // TILE
    steps = -(-(base + over) // TILE)
    cases = ([(c < whole, spots(0))] if whole else []) + [(c == step, spots(step)) for step in range(whole, steps)]
    for side in range(2):
        for case, found in cases:
            here = (whose == side) & case
            x_refs = (data[side], more_ref.at[side, 0])
            g_refs = (data[2 + side], more_ref.at[side, 1])

            @pl.when(here & (c * TILE < used))
            def _():
                for refs, place in ((x_refs, x_place), (g_refs, g_place)):
                    for s in range(parts):
                        at = slice(s * width, (s + 1) * width)
                        values = [refs[is_over][s, :, lanes].astype(F32) for is_over, lanes, _ in found]
                        filled = sum(v.shape[1] for v in values)
                        if filled < TILE:
                            values.append(jnp.zeros((width, TILE - filled), F32))
                        place[at, :] = jnp.concatenate(values, axis=1) if len(values) > 1 else values[0]

    @pl.when(c * TILE < used)
    def _():
        x = x_place[...].astype(BF)
        g = g_place[...].astype(BF)

        for i in range(units // block):
            at = pl.ds(i * block, block)
            pre = nn(up_w[at, :], x)
            grad_hidden = nn(down_w[at, :], g)
            value, slope = gelu_pair(pre)
            h = value.astype(BF)
            gp = (grad_hidden * slope).astype(BF)
            hidden[at, :] = h
            grad_pre[at, :] = gp

        for lo in range(0, wide, 2 * LANES):
            hi = min(lo + 2 * LANES, wide)
            up_acc[:, lo:hi] += nt(grad_pre[...], x[lo:hi, :])
            down_acc[:, lo:hi] += nt(hidden[...], g[lo:hi, :])

        def fold(v):
            return sum(v[:, lo : lo + LANES] for lo in range(0, TILE, LANES))

        branches = nn(down_t[...], hidden[...])
        normeds = nn(up_t[...], grad_pre[...])
        for s in range(parts):
            rows = slice(s * width, (s + 1) * width)
            k = lax.rem(me - s + parts, parts)
            branch, normed = branches[rows, :], normeds[rows, :]
            sums_ref[k, 0] += fold(normed)
            sums_ref[k, 1] += fold(normed * x_place[rows, :])
            for side in range(2):
                for case, found in cases:

                    @pl.when((whose == side) & case)
                    def _():
                        for is_over, lanes, tile in found:
                            to = 2 * side + is_over
                            for value, ref in ((branch, outs[to]), (normed, outs[4 + to])):
                                ref[s if is_over else k, :, lanes] = value[:, tile].astype(ref.dtype)

    @pl.when(last)
    def _():
        for p in range(chips):
            for q in range(parts):
                row = (p * parts + q) * slab
                to = (chip ^ p, q)
                weight_grad_ref[to[0], to[1], 0] = up_acc[row : row + slab, :].astype(BF)
                weight_grad_ref[to[0], to[1], 1] = down_acc[row : row + slab, :].astype(BF)


def pointwise(at, ups, downs, data):
    chips = len(ups)
    parts, width, base = data[0].shape
    over = data[4].shape[4]
    _, slab, wide = ups[0].shape
    units, channels = chips * parts * slab, parts * width
    base_tiles = -(-base // TILE)

    def tile(side, is_over):
        if is_over:
            return pl.BlockSpec((parts, width, over), lambda whose, c, at: (0, 0, 0))

        def place(whose, c, at):
            end = jnp.minimum(jnp.maximum((at[1 + side * parts + at[0]] - 1) // TILE, 0), base_tiles - 1)
            return (0, 0, jnp.where(whose == side, jnp.minimum(c, end), 0 if side else end))

        return pl.BlockSpec((parts, width, TILE), place)

    tiles = [tile(side, is_over) for side in range(2) for is_over in range(2)]
    kinds = [F32, F32, BF, BF]
    result = [jax.ShapeDtypeStruct((parts, width, n), kind) for n, kind in zip((base, over, base, over), kinds)]
    return pl.pallas_call(
        functools.partial(pointwise_kernel, chips=chips, parts=parts, width=width, base=base, over=over),
        grid_spec=pltpu.PrefetchScalarGridSpec(
            num_scalar_prefetch=1,
            grid=(2, -(-(base + over) // TILE)),
            in_specs=[
                pl.BlockSpec(ups[0].shape, lambda w, c, at: (0, 0, 0), pipeline_mode=pl.Buffered(1))
                for _ in range(2 * chips)
            ]
            + [tile(0, 0), tile(1, 0), tile(0, 0), tile(1, 0)]
            + [pl.BlockSpec(data[4].shape, lambda w, c, at: (0, 0, 0, 0, 0), pipeline_mode=pl.Buffered(1))],
            out_specs=tiles
            + tiles
            + [
                pl.BlockSpec((chips, parts, 2, slab, wide), lambda w, c, at: (0, 0, 0, 0, 0)),
                pl.BlockSpec((parts, 2, width, LANES), lambda w, c, at: (0, 0, 0, 0)),
            ],
            scratch_shapes=[
                pltpu.VMEM((units, wide), BF),
                pltpu.VMEM((units, wide), BF),
                pltpu.VMEM((channels, units), BF),
                pltpu.VMEM((channels, units), BF),
                pltpu.VMEM((units, wide), F32),
                pltpu.VMEM((units, wide), F32),
                pltpu.VMEM((wide, TILE), F32),
                pltpu.VMEM((wide, TILE), F32),
                pltpu.VMEM((units, TILE), BF),
                pltpu.VMEM((units, TILE), BF),
            ],
        ),
        out_shape=result
        + result
        + [
            jax.ShapeDtypeStruct((chips, parts, 2, slab, wide), BF),
            jax.ShapeDtypeStruct((parts, 2, width, LANES), F32),
        ],
        compiler_params=params(62),
        cost_estimate=cost(70),
        name="pointwise",
    )(at, *ups, *downs, *data)


def per_device(
    inputs,
    crop_sizes,
    land_mask,
    conv_weight,
    norm_gain,
    norm_shift,
    up_weight,
    up_bias,
    down_weight,
    down_bias,
    cotangent,
    *,
    sizes,
):
    chips, cores, parts = sizes
    crops, side, _, width = inputs.shape
    taps = conv_weight.shape[0]
    cells = crops * side * side // parts
    local_units = up_weight.shape[1]
    channels = up_weight.shape[0]
    me = lax.axis_index("mp")
    core = lax.axis_index("core")
    chip = lax.axis_index("xy")

    def ring(k):
        return [(i, (i + k) % parts) for i in range(parts)]

    def everywhere(value, axes):
        for axis in axes:
            size = {"xy": chips, "core": cores, "mp": parts}[axis]
            if size <= 4:
                others = [lax.ppermute(value, axis, [(i, i ^ j) for i in range(size)]) for j in range(1, size)]
                value = sum(others, value)
                continue
            step = 1
            while step < size:
                value = value + lax.ppermute(value, axis, [(i, i ^ step) for i in range(size)])
                step *= 2
        return value

    def ring_back(k):
        return [(i, (i - k) % parts) for i in range(parts)]

    def to_parts(pieces, ring=ring):
        return [pieces[0]] + [lax.ppermute(pieces[k], "mp", ring(k)) for k in range(1, parts)]

    def exchange(by_part):
        return lax.all_to_all(by_part, "mp", 0, 0, tiled=True)

    swap = [(i, cores - 1 - i) for i in range(cores)]

    def to_core(value):
        return lax.ppermute(value, "core", swap)

    share = -(-local_units // (chips * cores))
    slab = ceil_to(share, 8)
    wide_width = ceil_to(width, 8)
    wide = parts * wide_width + 8
    rank = chip * cores + core
    spare = chips * cores * share - local_units

    def take(rows):
        rows = jnp.pad(rows, ((0, spare), (0, 0))) if spare else rows
        rows = lax.dynamic_slice_in_dim(rows, rank * share, share, axis=0)
        if wide_width > width:
            rows = jnp.pad(rows.reshape(share, parts, width), ((0, 0), (0, 0), (0, wide_width - width)))
        return rows.reshape(share, -1)

    own_bias = up_bias[:, None]
    own_bias = jnp.pad(own_bias, ((0, spare), (0, 0))) if spare else own_bias
    own_bias = lax.dynamic_slice_in_dim(own_bias, rank * share, share, axis=0)
    up_rows = jnp.pad(jnp.concatenate([take(up_weight.T), own_bias], axis=1), ((0, slab - share), (0, 7)))
    down_rows = jnp.pad(take(down_weight), ((0, slab - share), (0, 8)))
    rows = lax.all_gather(jnp.stack([up_rows, down_rows]), "mp", axis=1, tiled=False)

    def over_plane(own, bits):
        held = {0: own}
        for bit in bits:
            pairs = [(i, i ^ bit) for i in range(chips)]
            held.update({p ^ bit: lax.ppermute(value, "xy", pairs) for p, value in list(held.items())})
        return [held[p] for p in range(chips)]

    index = jnp.arange(side, dtype=jnp.int32)
    inside = (index[None, :, None] < crop_sizes[:, 0][:, None, None]) & (
        index[None, None, :] < crop_sizes[:, 1][:, None, None]
    )
    usable = jnp.where(inside, land_mask, 0)
    lane_mask = jnp.broadcast_to(usable[..., None].astype(BF), usable.shape + (LANES,))
    by_part = usable.reshape(crops, side // parts, parts, side).transpose(2, 0, 1, 3).reshape(parts, -1, side)
    by_part = by_part.astype(F32)
    lines = by_part.shape[1]
    upto = jnp.dot(by_part, jnp.triu(jnp.ones((side, side), F32)))
    before = jnp.dot(upto[:, :, -1], jnp.triu(jnp.ones((lines, lines), F32), 1))
    slots = jnp.where(by_part > 0, upto + before[:, :, None] - 1, -1).astype(jnp.int32)
    counts = jnp.sum(by_part, axis=(1, 2)).astype(jnp.int32)
    columns = jnp.broadcast_to(slots.reshape(parts, crops, -1)[..., None], (parts, crops, cells // crops, LANES))
    slots = slots.reshape(parts, 1, cells)
    ends = jnp.cumsum(jnp.sum(by_part.reshape(parts, crops, -1), axis=2), axis=1)
    reaches = jnp.pad(ends, ((0, 0), (1, 0))).astype(jnp.int32).reshape(-1)
    at = jnp.concatenate([me[None].astype(jnp.int32), counts, to_core(counts), chip[None].astype(jnp.int32), reaches])

    base = ceil_to(cells * 7 // 9, LANES)
    over = ceil_to(cells, LANES) - base
    over_full = jnp.where(jnp.max(counts) > base, 1.0, 0.0)

    cot_base, cot_over, down_bias_local = pack_cotangent(at, cotangent, lane_mask, slots, base, over)
    inputs, cot_base = after(inputs, cot_base)
    grad_base = exchange(cot_base)

    wide_taps = spread_rows(conv_weight.reshape(taps * taps, width))
    convolved, stats = conv_forward(inputs, lane_mask, wide_taps, taps, parts)
    stats = jnp.sum(stats, axis=(0, 3)).reshape(2, -1)[:, :width]
    extra = jnp.pad(jnp.stack([jnp.sum(by_part), over_full])[None], ((0, 0), (0, width - 2)))
    stats = everywhere(jnp.concatenate([stats, extra, jnp.sum(down_bias_local, axis=0)[None]]), ("core", "xy"))
    stats, rows = after(stats, rows)
    bits = [1 << j for j in range(chips.bit_length() - 1)]

    def double(held, bit):
        pairs = [(i, i ^ bit) for i in range(chips)]
        return {**held, **{p ^ bit: lax.ppermute(value, "xy", pairs) for p, value in held.items()}}

    ups, downs = {0: rows[0]}, {0: rows[1]}
    ups, downs = double(ups, bits[0]), double(downs, bits[-1])
    ocean_count = stats[2, 0]
    overflows = stats[2, 1] > 0
    down_bias_grad = stats[3]
    channel_mean = stats[0] / ocean_count
    inv_std = lax.rsqrt(stats[1] / ocean_count - channel_mean * channel_mean + EPSILON)
    gain = norm_gain.astype(F32)
    shift = norm_shift.astype(F32)
    scale = gain * inv_std

    affine = jnp.stack([scale, shift - channel_mean * scale])
    normed_base, normed_over = pack_normed(at, convolved.reshape(parts, cells, width), affine, slots, base, over)
    places = sorted(ups), sorted(downs)
    normed_base, grad_base, *held = after(
        normed_base, grad_base, *[ups[p] for p in places[0]], *[downs[p] for p in places[1]]
    )
    ups, downs = dict(zip(places[0], held)), dict(zip(places[1], held[len(ups) :]))
    for j in range(1, len(bits)):
        ups, downs = double(ups, bits[j]), double(downs, bits[-1 - j])
    ups, downs = [ups[p] for p in range(chips)], [downs[p] for p in range(chips)]
    x_base, crowded, *held = after(exchange(normed_base), overflows, *ups, *downs)
    ups, downs = held[:chips], held[chips:]

    def overflow_in():
        own = jnp.stack([exchange(normed_over), exchange(cot_over)])
        return jnp.stack([own, to_core(own)])

    more = lax.cond(crowded, overflow_in, lambda: jnp.zeros((2, 2, parts, wide_width, over), BF))
    data = [x_base, to_core(x_base), grad_base, to_core(grad_base), more]
    *sums_out, weight_grad, sums = pointwise(at, ups, downs, data)
    branch, normed = list(sums_out[:4]), list(sums_out[4:])

    def over_cores(own, far):
        far = to_core(far)
        return [(own[k] + far[k].astype(F32)).astype(BF) for k in range(parts)]

    def home(total):
        return to_parts(total, ring_back)

    sums = everywhere(jnp.sum(sums, axis=3), ("core", "xy"))
    sums = sum(to_parts([sums[k] for k in range(parts)], ring_back))[:, :width]
    total, sums = after(tuple(over_cores(normed[0], normed[2])), sums)
    normed_base = home(total)
    total = over_cores(branch[0], branch[2])
    crowded, total, sums, columns, *normed_base = after(overflows, tuple(total), sums, columns, *normed_base)

    def overflow_out():
        return jnp.stack([exchange(jnp.stack(over_cores(v[1], v[3]))) for v in (branch, normed)])

    more = lax.cond(crowded, overflow_out, lambda: jnp.zeros((2, parts, wide_width, over), BF))

    shift_grad = sums[0]
    gain_grad = (sums[1] - shift * shift_grad) / gain
    vectors = jnp.stack([channel_mean, scale, scale * shift_grad / ocean_count, scale * inv_std * gain_grad / ocean_count])
    total, more = after(total, more)
    branch_base = home(total)

    own = lax.psum_scatter(weight_grad, "xy", scatter_dimension=0, tiled=False)
    own, vectors, *normed_base = after(own, spread_rows(vectors), *normed_base)
    own = lax.psum_scatter(own, "mp", scatter_dimension=0, tiled=False)
    input_grad, grad_conv = input_gradient(
        at, lane_mask, cotangent, convolved, wide_taps, vectors, columns, [*normed_base, more], taps
    )
    own, grad_conv = after(own, grad_conv)
    both = lax.all_gather(own, ("xy", "core"), axis=0, tiled=False)
    taps_local = taps_gradient(inputs, lane_mask, grad_conv, taps)
    output = make_output(at, inputs, lane_mask, down_bias.astype(F32)[None], columns, [*branch_base, more])
    taps_local = jnp.sum(taps_local, axis=2).transpose(1, 0, 2).reshape(taps * taps, -1)
    conv_weight_grad = everywhere(taps_local, ("core", "xy"))[:, :width].reshape(taps, taps, width)
    up_weight_grad, down_weight_grad, bias_rows = finish(both, parts, width, share, local_units)
    up_bias_grad = bias_rows[0]
    return (
        output,
        input_grad,
        conv_weight_grad,
        gain_grad,
        shift_grad,
        up_weight_grad,
        up_bias_grad,
        down_weight_grad,
        down_bias_grad,
    )


def solution(mesh):
    cores = 2
    parts = mesh.shape["mp"]
    chips = mesh.shape["dp"] // cores
    fine = Mesh(np.asarray(mesh.devices).reshape(chips, cores, parts), ("xy", "core", "mp"))
    dp = ("xy", "core")
    specs = (
        P(dp, None, None, "mp"),
        P(dp, None),
        P(dp, None, None),
        P(None, None, "mp"),
        P("mp"),
        P("mp"),
        P(None, "mp"),
        P("mp"),
        P("mp", None),
        P("mp"),
        P(dp, None, None, "mp"),
    )
    results = (
        P(dp, None, None, "mp"),
        P(dp, None, None, "mp"),
        P(None, None, "mp"),
        P("mp"),
        P("mp"),
        P(None, "mp"),
        P("mp"),
        P("mp", None),
        P("mp"),
    )
    return jax.shard_map(
        functools.partial(per_device, sizes=(chips, cores, parts)),
        mesh=fine,
        in_specs=specs,
        out_specs=results,
        check_vma=False,
    )
```

```python
import functools

import jax
import jax.numpy as jnp
import numpy as np
from jax import lax
from jax.experimental import pallas as pl
from jax.experimental.pallas import tpu as pltpu
from jax.sharding import Mesh
from jax.sharding import PartitionSpec as P

F32 = jnp.float32
BF = jnp.bfloat16
EPSILON = 1e-05
INV_ROOT_TWO_PI = 0.3989422804014327
LANES = 128
LEFT = 8
MIB = 2**20
TILE = 256


def ceil_to(value, unit):
    return -(-value // unit) * unit


def lane_tiles(width):
    return -(-width // LANES)


def spread_rows(rows):
    count, width = rows.shape
    tiles = lane_tiles(width)
    flat = jnp.pad(rows.astype(F32), ((0, 0), (0, tiles * LANES - width)))
    flat = flat.reshape(count, tiles, 1, LANES).transpose(1, 0, 2, 3)
    return jnp.broadcast_to(flat, (tiles, count, 8, LANES))


def after(*values):
    return lax.optimization_barrier(values)


def params(mib, **more):
    return pltpu.CompilerParams(vmem_limit_bytes=mib * MIB, **more)


def whole(array):
    zeros = (0,) * array.ndim
    return pl.BlockSpec(array.shape, lambda n, at: zeros)


EAGERNESS = 6


def cost(micros):
    return pl.CostEstimate(flops=int(micros * 1.15e9 / EAGERNESS), bytes_accessed=0, transcendentals=0)


def clear_borders(dst, half, side):
    tiles, _, cols, _ = dst.shape
    for t in range(tiles):
        for r in list(range(half)) + list(range(half + side, side + 2 * half)):
            dst[t, r] = jnp.zeros((cols, LANES), F32)

        @pl.loop(0, side)
        def _(r):
            dst[t, r + half, 0:LEFT, :] = jnp.zeros((LEFT, LANES), F32)
            dst[t, r + half, LEFT + side : cols, :] = jnp.zeros((cols - LEFT - side, LANES), F32)


def fill_masked(dst, x_ref, m_ref, half):
    _, side, _, width = x_ref.shape
    for t in range(lane_tiles(width)):
        lo, hi = t * LANES, min((t + 1) * LANES, width)

        @pl.loop(0, side)
        def _(r):
            value = x_ref[0, r, :, lo:hi].astype(F32) * m_ref[0, r, :, : hi - lo].astype(F32)
            dst[t, r + half, LEFT : LEFT + side, 0 : hi - lo] = value


def conv_rows(src, w_ref, t, r0, c0, rows, groups, taps, flipped):
    half = taps // 2
    acc = [jnp.zeros((groups, 8, LANES), F32) for _ in range(rows)]
    for b in range(taps):
        shift = (taps - 1 - b) if flipped else b
        weights = [w_ref[t, a * taps + b] for a in range(taps)]
        for i in range(rows + taps - 1):
            x = src[t, r0 + i, pl.ds(LEFT + c0 + shift - half, groups * 8), :].reshape(groups, 8, LANES)
            for r in range(max(0, i - taps + 1), min(rows, i + 1)):
                a = taps - 1 - (i - r) if flipped else i - r
                acc[r] = acc[r] + x * weights[a][None]
    return acc


def forward_kernel(x_ref, m_ref, w_ref, conv_ref, stat_ref, xs, *, taps, rows, groups):
    _, side, _, width = x_ref.shape
    parts = conv_ref.shape[0]
    half = taps // 2
    clear_borders(xs, half, side)
    fill_masked(xs, x_ref, m_ref, half)
    for t in range(lane_tiles(width)):
        lo, hi = t * LANES, min((t + 1) * LANES, width)

        def block(i, carry):
            first, second = carry
            r0 = i * rows
            for c0 in range(0, side, groups * 8):
                acc = conv_rows(xs, w_ref, t, r0, c0, rows, groups, taps, False)
                for r in range(rows):
                    m = m_ref[0, r0 + r, c0 : c0 + groups * 8, :].astype(F32).reshape(groups, 8, LANES)
                    cm = acc[r] * m
                    first = first + jnp.sum(cm, axis=0)
                    second = second + jnp.sum(cm * acc[r], axis=0)
                    if rows % parts == 0:
                        part, row = r % parts, i * (rows // parts) + r // parts
                    else:
                        part, row = lax.rem(r0 + r, parts), lax.div(r0 + r, parts)
                    conv_ref[part, 0, row, c0 : c0 + groups * 8, lo:hi] = acc[r].reshape(groups * 8, LANES)[:, : hi - lo]
            return first, second

        zero = jnp.zeros((8, LANES), F32)
        first, second = lax.fori_loop(0, side // rows, block, (zero, zero))
        stat_ref[0, 0, t] = first
        stat_ref[0, 1, t] = second


def conv_forward(x, lane_mask, wide_taps, taps, parts, rows=12, groups=2):
    crops, side, _, width = x.shape
    tiles, half = lane_tiles(width), taps // 2
    return pl.pallas_call(
        functools.partial(forward_kernel, taps=taps, rows=rows, groups=groups),
        grid=(crops,),
        in_specs=[
            pl.BlockSpec((1, side, side, width), lambda n: (n, 0, 0, 0)),
            pl.BlockSpec((1, side, side, LANES), lambda n: (n, 0, 0, 0)),
            pl.BlockSpec(wide_taps.shape, lambda n: (0, 0, 0, 0)),
        ],
        out_specs=[
            pl.BlockSpec((parts, 1, side // parts, side, width), lambda n: (0, n, 0, 0, 0)),
            pl.BlockSpec((1, 2, tiles, 8, LANES), lambda n: (n, 0, 0, 0, 0)),
        ],
        out_shape=[
            jax.ShapeDtypeStruct((parts, crops, side // parts, side, width), F32),
            jax.ShapeDtypeStruct((crops, 2, tiles, 8, LANES), F32),
        ],
        scratch_shapes=[pltpu.VMEM((tiles, side + 2 * half, LEFT + side + 8, LANES), F32)],
        compiler_params=params(32),
        cost_estimate=cost(22),
        name="depthwise_forward",
    )(x, lane_mask, wide_taps)


def chooser(slot_of_cell, start, count):
    cells = slot_of_cell.shape[1]
    rows = lax.broadcasted_iota(jnp.int32, (count, cells), 0) + start
    return jnp.where(rows == slot_of_cell, 1.0, 0.0).astype(BF)


def nt(left, right):
    return lax.dot_general(left, right, (((1,), (1,)), ((), ())), preferred_element_type=F32)


def nn(left, right):
    return jnp.dot(left, right, preferred_element_type=F32)


def segments(base, over):
    cuts = sorted({*range(0, base + over, TILE), base, base + over})
    return [
        (int(lo >= base), lo - base if lo >= base else lo, lo, hi - lo) for lo, hi in zip(cuts, cuts[1:]) if hi <= base + over
    ]


def pack_columns(values, slots, used, base_ref, over_ref):
    width = values.shape[0]
    for is_over, lo, start, count in segments(base_ref.shape[1], over_ref.shape[1]):
        ref = over_ref if is_over else base_ref

        @pl.when(start < used)
        def _():
            ref[:width, lo : lo + count] = nt(values, chooser(slots, start, count)).astype(BF)

        @pl.when(start >= used)
        def _():
            ref[:width, lo : lo + count] = jnp.zeros((width, count), BF)

        if width < ref.shape[0]:
            ref[width:, lo : lo + count] = jnp.zeros((ref.shape[0] - width, count), BF)


def pack_normed_kernel(at_ref, conv_ref, vec_ref, slot_ref, base_ref, over_ref):
    normed = (conv_ref[0] * vec_ref[0:1, :] + vec_ref[1:2, :]).T.astype(BF)
    used = at_ref[1 + pl.program_id(0)]
    pack_columns(normed, slot_ref[0], used, base_ref.at[0], over_ref.at[0])


def pack_normed(at, conv, vec, slots, base, over):
    parts, cells, width = conv.shape
    wide = ceil_to(width, 8)
    return pl.pallas_call(
        pack_normed_kernel,
        grid_spec=pltpu.PrefetchScalarGridSpec(
            num_scalar_prefetch=1,
            grid=(parts,),
            in_specs=[
                pl.BlockSpec((1, cells, width), lambda k, at: (k, 0, 0)),
                pl.BlockSpec(vec.shape, lambda k, at: (0, 0)),
                pl.BlockSpec((1, 1, cells), lambda k, at: (k, 0, 0)),
            ],
            out_specs=[
                pl.BlockSpec((1, wide, base), lambda k, at: (k, 0, 0)),
                pl.BlockSpec((1, wide, over), lambda k, at: (k, 0, 0)),
            ],
        ),
        out_shape=[jax.ShapeDtypeStruct((parts, wide, base), BF), jax.ShapeDtypeStruct((parts, wide, over), BF)],
        compiler_params=params(32),
        cost_estimate=cost(8),
        name="pack_normed",
    )(at, conv, vec, slots)


def pack_cotangent_kernel(at_ref, cot_ref, m_ref, slot_ref, base_ref, over_ref, sum_ref, rows):
    crops, side, _, width = cot_ref.shape
    part, parts = pl.program_id(0), pl.num_programs(0)
    per = rows.shape[0] // (crops * side)
    total = jnp.zeros((8, width), F32)
    for n in range(crops):

        def body(i, total):
            r = i * parts + part
            masks = [m_ref[n, r, :, : min(LANES, width - lo)] for lo in range(0, width, LANES)]
            mask = jnp.concatenate(masks, axis=1) if len(masks) > 1 else masks[0]
            value = cot_ref[n, r].astype(F32) * mask.astype(F32)
            rows[pl.ds(pl.multiple_of((n * per + i) * side, 8), side), :] = value
            return total + jnp.sum(value.reshape(side // 8, 8, width), axis=0)

        total = lax.fori_loop(0, per, body, total)

    @pl.when(part == 0)
    def _():
        sum_ref[...] = total

    @pl.when(part > 0)
    def _():
        sum_ref[...] += total

    pack_columns(rows[...].T.astype(BF), slot_ref[0], at_ref[1 + part], base_ref.at[0], over_ref.at[0])


def pack_cotangent(at, cot, lane_mask, slots, base, over):
    crops, side, _, width = cot.shape
    parts, _, cells = slots.shape
    wide = ceil_to(width, 8)
    return pl.pallas_call(
        pack_cotangent_kernel,
        grid_spec=pltpu.PrefetchScalarGridSpec(
            num_scalar_prefetch=1,
            grid=(parts,),
            in_specs=[
                pl.BlockSpec(cot.shape, lambda k, at: (0, 0, 0, 0)),
                pl.BlockSpec(lane_mask.shape, lambda k, at: (0, 0, 0, 0)),
                pl.BlockSpec((1, 1, cells), lambda k, at: (k, 0, 0)),
            ],
            out_specs=[
                pl.BlockSpec((1, wide, base), lambda k, at: (k, 0, 0)),
                pl.BlockSpec((1, wide, over), lambda k, at: (k, 0, 0)),
                pl.BlockSpec((8, width), lambda k, at: (0, 0)),
            ],
            scratch_shapes=[pltpu.VMEM((cells, width), F32)],
        ),
        out_shape=[
            jax.ShapeDtypeStruct((parts, wide, base), BF),
            jax.ShapeDtypeStruct((parts, wide, over), BF),
            jax.ShapeDtypeStruct((8, width), F32),
        ],
        compiler_params=params(40),
        cost_estimate=cost(10),
        name="pack_cotangent",
    )(at, cot, lane_mask, slots)


def expand(base_ref, over_ref, slot_column, reach, acc):
    cells, width = acc.shape
    acc[...] = jnp.zeros_like(acc)
    for is_over, lo, start, count in segments(base_ref.shape[1], over_ref.shape[1]):
        ref = over_ref if is_over else base_ref

        @pl.when((start < reach[1]) & (start + count > reach[0]))
        def _():
            lanes = lax.broadcasted_iota(jnp.int32, (cells, LANES), 1) + start
            choice = jnp.concatenate(
                [jnp.where(lanes + j == slot_column, 1.0, 0.0).astype(BF) for j in range(0, count, LANES)], axis=1
            )
            acc[...] += nt(choice, ref[:width, lo : lo + count])


def reach_of(at_ref, parts, part, crop):
    crops = (at_ref.shape[0] - (2 + 2 * parts)) // parts - 1
    place = 2 + 2 * parts + part * (crops + 1) + crop
    return at_ref[place], at_ref[place + 1]


def output_kernel(at_ref, x_ref, m_ref, bias_ref, column_ref, *refs):
    piece_refs, out_ref, acc = refs[:-2], refs[-2], refs[-1]
    parts = len(piece_refs) - 1
    _, side, _, width = x_ref.shape
    per = side // parts
    for k in range(parts):
        part = lax.rem(at_ref[0] + k, parts)
        reach = reach_of(at_ref, parts, part, pl.program_id(0))
        expand(piece_refs[k], piece_refs[parts].at[0, part], column_ref[part, 0], reach, acc)

        @pl.loop(0, per)
        def _(i):
            r = i * parts + part
            start = pl.multiple_of(i * side, 8)
            for lo in range(0, width, LANES):
                hi = min(lo + LANES, width)
                value = x_ref[0, r, :, lo:hi].astype(F32) + acc[pl.ds(start, side), lo:hi] + bias_ref[0:1, lo:hi]
                out_ref[0, r, :, lo:hi] = (m_ref[0, r, :, : hi - lo].astype(F32) * value).astype(BF)


def make_output(at, x, lane_mask, bias, columns, pieces):
    parts = len(pieces) - 1
    crops, side, _, width = x.shape
    cells = side * side // parts
    field = pl.BlockSpec((1, side, side, width), lambda n, at: (n, 0, 0, 0))
    return pl.pallas_call(
        output_kernel,
        grid_spec=pltpu.PrefetchScalarGridSpec(
            num_scalar_prefetch=1,
            grid=(crops,),
            in_specs=[
                field,
                pl.BlockSpec((1, side, side, LANES), lambda n, at: (n, 0, 0, 0)),
                pl.BlockSpec((1, width), lambda n, at: (0, 0)),
                pl.BlockSpec((parts, 1, cells, LANES), lambda n, at: (0, n, 0, 0)),
            ]
            + [whole(p) for p in pieces],
            out_specs=field,
            scratch_shapes=[pltpu.VMEM((cells, width), F32)],
        ),
        out_shape=jax.ShapeDtypeStruct(x.shape, BF),
        compiler_params=params(60),
        cost_estimate=cost(12),
        name="make_output",
    )(at, x, lane_mask, bias, columns, *pieces)


def input_gradient_kernel(at_ref, m_ref, cot_ref, conv_ref, w_ref, v_ref, column_ref, *refs, taps, rows, groups):
    piece_refs, dx_ref, gs_ref, acc_ref = refs[:-3], refs[-3], refs[-2], refs[-1]
    gs = gs_ref.at[0]
    parts = len(piece_refs) - 1
    _, side, _, width = cot_ref.shape
    per = side // parts
    half = taps // 2
    clear_borders(gs, half, side)
    for k in range(parts):
        part = lax.rem(at_ref[0] + k, parts)
        reach = reach_of(at_ref, parts, part, pl.program_id(0))
        expand(piece_refs[k], piece_refs[parts].at[1, part], column_ref[part, 0], reach, acc_ref)

        @pl.loop(0, per)
        def _(i):
            r = i * parts + part
            start = pl.multiple_of(i * side, 8)
            for t in range(lane_tiles(width)):
                lo, hi = t * LANES, min((t + 1) * LANES, width)
                n = hi - lo
                shape = (side // 8, 8, n)
                m = m_ref[0, r, :, :n].astype(F32).reshape(shape)
                centred = conv_ref[part, 0, i, :, lo:hi].reshape(shape) - v_ref[t, 0, :, :n][None]
                gn = acc_ref[pl.ds(start, side), lo:hi].reshape(shape)
                g = v_ref[t, 1, :, :n][None] * gn - m * (v_ref[t, 2, :, :n][None] + centred * v_ref[t, 3, :, :n][None])
                gs[t, r + half, LEFT : LEFT + side, 0:n] = g.reshape(side, n)

    for t in range(lane_tiles(width)):
        lo, hi = t * LANES, min((t + 1) * LANES, width)
        n = hi - lo

        @pl.loop(0, side // rows)
        def _(i):
            r0 = i * rows
            for c0 in range(0, side, groups * 8):
                acc = conv_rows(gs, w_ref, t, r0, c0, rows, groups, taps, True)
                for r in range(rows):
                    m = m_ref[0, r0 + r, c0 : c0 + groups * 8, :n].astype(F32)
                    cot = cot_ref[0, r0 + r, c0 : c0 + groups * 8, lo:hi].astype(F32)
                    value = m * (cot + acc[r].reshape(groups * 8, LANES)[:, :n])
                    dx_ref[0, r0 + r, c0 : c0 + groups * 8, lo:hi] = value.astype(BF)


def input_gradient(at, lane_mask, cot, conv, wide_taps, vectors, columns, pieces, taps, rows=12, groups=2):
    parts = len(pieces) - 1
    crops, side, _, width = cot.shape
    tiles, half = lane_tiles(width), taps // 2
    cells = side * side // parts
    field = pl.BlockSpec((1, side, side, width), lambda n, at: (n, 0, 0, 0))
    padded = (tiles, side + 2 * half, LEFT + side + 8, LANES)
    return pl.pallas_call(
        functools.partial(input_gradient_kernel, taps=taps, rows=rows, groups=groups),
        grid_spec=pltpu.PrefetchScalarGridSpec(
            num_scalar_prefetch=1,
            grid=(crops,),
            in_specs=[
                pl.BlockSpec((1, side, side, LANES), lambda n, at: (n, 0, 0, 0)),
                field,
                pl.BlockSpec((parts, 1, side // parts, side, width), lambda n, at: (0, n, 0, 0, 0)),
                pl.BlockSpec(wide_taps.shape, lambda n, at: (0, 0, 0, 0)),
                pl.BlockSpec(vectors.shape, lambda n, at: (0, 0, 0, 0)),
                pl.BlockSpec((parts, 1, cells, LANES), lambda n, at: (0, n, 0, 0)),
            ]
            + [whole(p) for p in pieces],
            out_specs=[field, pl.BlockSpec((1, *padded), lambda n, at: (n, 0, 0, 0, 0))],
            scratch_shapes=[pltpu.VMEM((cells, width), F32)],
        ),
        out_shape=[jax.ShapeDtypeStruct(cot.shape, BF), jax.ShapeDtypeStruct((crops, *padded), F32)],
        compiler_params=params(60),
        cost_estimate=cost(28),
        name="input_gradient",
    )(at, lane_mask, cot, conv, wide_taps, vectors, columns, *pieces)


def taps_gradient_kernel(x_ref, m_ref, gs_ref, dw_ref, xs, *, taps, rows, groups):
    _, side, _, width = x_ref.shape
    half = taps // 2
    span = groups * 8

    @pl.when(pl.program_id(0) == 0)
    def _():
        dw_ref[...] = jnp.zeros_like(dw_ref)

    clear_borders(xs, half, side)
    fill_masked(xs, x_ref, m_ref, half)
    for t in range(lane_tiles(width)):

        @pl.loop(0, side // rows)
        def _(i):
            r0 = i * rows
            for c0 in range(0, side, span):
                grads = [
                    gs_ref[0, t, r0 + half + r, LEFT + c0 : LEFT + c0 + span, :].reshape(groups, 8, LANES)
                    for r in range(rows)
                ]
                for b in range(taps):
                    acc = [jnp.zeros((groups, 8, LANES), F32) for _ in range(taps)]
                    for j in range(rows + taps - 1):
                        x = xs[t, r0 + j, pl.ds(LEFT + c0 + b - half, span), :].reshape(groups, 8, LANES)
                        for r in range(max(0, j - taps + 1), min(rows, j + 1)):
                            acc[j - r] = acc[j - r] + x * grads[r]
                    for a in range(taps):
                        dw_ref[t, a * taps + b] += jnp.sum(acc[a], axis=0)


def taps_gradient(x, lane_mask, gs, taps, rows=8, groups=2):
    crops, side, _, width = x.shape
    tiles = lane_tiles(width)
    return pl.pallas_call(
        functools.partial(taps_gradient_kernel, taps=taps, rows=rows, groups=groups),
        grid=(crops,),
        in_specs=[
            pl.BlockSpec((1, side, side, width), lambda n: (n, 0, 0, 0)),
            pl.BlockSpec((1, side, side, LANES), lambda n: (n, 0, 0, 0)),
            pl.BlockSpec((1, *gs.shape[1:]), lambda n: (n, 0, 0, 0, 0)),
        ],
        out_specs=pl.BlockSpec((tiles, taps * taps, 8, LANES), lambda n: (0, 0, 0, 0)),
        out_shape=jax.ShapeDtypeStruct((tiles, taps * taps, 8, LANES), F32),
        scratch_shapes=[pltpu.VMEM(gs.shape[1:], F32)],
        compiler_params=params(60),
        cost_estimate=cost(22),
        name="taps_gradient",
    )(x, lane_mask, gs)


def finish_kernel(both_ref, up_ref, down_ref, bias_ref, rows, *, parts, width, share):
    ranks, _, _, wide = both_ref.shape
    units = down_ref.shape[0]
    wide_width = (wide - 8) // parts
    for which in range(2):
        for d in range(ranks):
            count = min(share, units - d * share)
            if count > 0:
                rows[d * share : d * share + count, :] = both_ref[d, which].astype(F32)[:count]
        if which == 0:
            turned = rows[...].T
            for s in range(parts):
                up_ref[s * width : (s + 1) * width, :] = turned[s * wide_width : s * wide_width + width, :units]
            bias_ref[...] = turned[wide - 8 :, :units]
        else:
            for s in range(parts):
                down_ref[:, s * width : (s + 1) * width] = rows[:units, s * wide_width : s * wide_width + width]


def finish(both, parts, width, share, units):
    ranks, _, slab, wide = both.shape
    channels = parts * width
    return pl.pallas_call(
        functools.partial(finish_kernel, parts=parts, width=width, share=share),
        out_shape=[
            jax.ShapeDtypeStruct((channels, units), F32),
            jax.ShapeDtypeStruct((units, channels), F32),
            jax.ShapeDtypeStruct((8, units), F32),
        ],
        scratch_shapes=[pltpu.VMEM((ceil_to(units, LANES), wide), F32)],
        compiler_params=params(40),
        cost_estimate=cost(5),
        name="finish_weight_gradients",
    )(both)


def gelu_pair(value):
    u = 1.0 + 0.23164189 * jnp.abs(value)
    t = pl.reciprocal(u, approx=True)
    t = t * (2.0 - u * t)
    bell = jnp.exp2(value * value * -0.72134752)
    poly = 0.530702715
    for term in (-0.7265760135, 0.7107068705, -0.142248368, 0.127414796):
        poly = poly * t + term
    tail = poly * t * bell
    below = jnp.where(value >= 0, 1.0 - tail, tail)
    return value * below, below + value * bell * INV_ROOT_TWO_PI


def pointwise_kernel(at_ref, *refs, chips, parts, width, base, over):
    up_refs, down_refs = refs[:chips], refs[chips : 2 * chips]
    data, more_ref, rest = refs[2 * chips : 2 * chips + 4], refs[2 * chips + 4], refs[2 * chips + 5 :]
    outs, (weight_grad_ref, sums_ref) = rest[:8], rest[8:10]
    up_w, down_w, up_t, down_t, up_acc, down_acc, x_place, g_place, hidden, grad_pre = rest[10:]
    whose, c = pl.program_id(0), pl.program_id(1)
    last = (whose == 1) & (c == pl.num_programs(1) - 1)
    _, slab, wide = up_refs[0].shape
    units = chips * parts * slab
    channels = parts * width
    block = LANES
    me, chip = at_ref[0], at_ref[1 + 2 * parts]
    used = at_ref[1 + whose * parts + me]

    @pl.when((whose == 0) & (c == 0))
    def _():
        for refs, dst in ((up_refs, up_w), (down_refs, down_w)):
            for p in range(chips):
                for q in range(0, parts, 2):
                    pair = jnp.concatenate([refs[p][q].astype(F32), refs[p][q + 1].astype(F32)], axis=0)
                    row = (p * parts + q) * slab
                    dst[row : row + 2 * slab, :] = pair.astype(BF)
        for u in range(0, units, LANES):
            for src, dst in ((up_w, up_t), (down_w, down_t)):
                dst[:, u : u + LANES] = src[u : u + LANES, :].astype(F32).T[:channels, :].astype(BF)
        up_acc[...] = jnp.zeros_like(up_acc)
        down_acc[...] = jnp.zeros_like(down_acc)
        sums_ref[...] = jnp.zeros_like(sums_ref)
        ones = jnp.where(lax.broadcasted_iota(jnp.int32, (8, TILE), 0) == 0, 1.0, 0.0)
        x_place[channels:, :] = ones
        g_place[channels:, :] = jnp.zeros((8, TILE), F32)

    def spots(step):
        first, end = step * TILE, (step + 1) * TILE
        found = []
        if first < base:
            n = min(end, base) - first
            found.append((0, slice(0, n), slice(0, n)))
        if end > base and first < base + over:
            lo, hi = max(first, base), min(end, base + over)
            found.append((1, slice(lo - base, hi - base), slice(lo - first, hi - first)))
        return found

    whole = base // TILE
    steps = -(-(base + over) // TILE)
    cases = ([(c < whole, spots(0))] if whole else []) + [(c == step, spots(step)) for step in range(whole, steps)]
    for side in range(2):
        for case, found in cases:
            here = (whose == side) & case
            x_refs = (data[side], more_ref.at[side, 0])
            g_refs = (data[2 + side], more_ref.at[side, 1])

            @pl.when(here & (c * TILE < used))
            def _():
                for refs, place in ((x_refs, x_place), (g_refs, g_place)):
                    for s in range(parts):
                        at = slice(s * width, (s + 1) * width)
                        values = [refs[is_over][s, :, lanes].astype(F32) for is_over, lanes, _ in found]
                        filled = sum(v.shape[1] for v in values)
                        if filled < TILE:
                            values.append(jnp.zeros((width, TILE - filled), F32))
                        place[at, :] = jnp.concatenate(values, axis=1) if len(values) > 1 else values[0]

    @pl.when(c * TILE < used)
    def _():
        x = x_place[...].astype(BF)
        g = g_place[...].astype(BF)

        for i in range(units // block):
            at = pl.ds(i * block, block)
            pre = nn(up_w[at, :], x)
            grad_hidden = nn(down_w[at, :], g)
            value, slope = gelu_pair(pre)
            h = value.astype(BF)
            gp = (grad_hidden * slope).astype(BF)
            hidden[at, :] = h
            grad_pre[at, :] = gp

        for lo in range(0, wide, 2 * LANES):
            hi = min(lo + 2 * LANES, wide)
            up_acc[:, lo:hi] += nt(grad_pre[...], x[lo:hi, :])
            down_acc[:, lo:hi] += nt(hidden[...], g[lo:hi, :])

        def fold(v):
            return sum(v[:, lo : lo + LANES] for lo in range(0, TILE, LANES))

        branches = nn(down_t[...], hidden[...])
        normeds = nn(up_t[...], grad_pre[...])
        for s in range(parts):
            rows = slice(s * width, (s + 1) * width)
            k = lax.rem(me - s + parts, parts)
            branch, normed = branches[rows, :], normeds[rows, :]
            sums_ref[k, 0] += fold(normed)
            sums_ref[k, 1] += fold(normed * x_place[rows, :])
            for side in range(2):
                for case, found in cases:

                    @pl.when((whose == side) & case)
                    def _():
                        for is_over, lanes, tile in found:
                            to = 2 * side + is_over
                            for value, ref in ((branch, outs[to]), (normed, outs[4 + to])):
                                ref[s if is_over else k, :, lanes] = value[:, tile].astype(ref.dtype)

    @pl.when(last)
    def _():
        for p in range(chips):
            for q in range(parts):
                row = (p * parts + q) * slab
                to = (chip ^ p, q)
                weight_grad_ref[to[0], to[1], 0] = up_acc[row : row + slab, :].astype(BF)
                weight_grad_ref[to[0], to[1], 1] = down_acc[row : row + slab, :].astype(BF)


def pointwise(at, ups, downs, data):
    chips = len(ups)
    parts, width, base = data[0].shape
    over = data[4].shape[4]
    _, slab, wide = ups[0].shape
    units, channels = chips * parts * slab, parts * width
    base_tiles = -(-base // TILE)

    def tile(side, is_over):
        if is_over:
            return pl.BlockSpec((parts, width, over), lambda whose, c, at: (0, 0, 0))

        def place(whose, c, at):
            end = jnp.minimum(jnp.maximum((at[1 + side * parts + at[0]] - 1) // TILE, 0), base_tiles - 1)
            return (0, 0, jnp.where(whose == side, jnp.minimum(c, end), 0 if side else end))

        return pl.BlockSpec((parts, width, TILE), place)

    tiles = [tile(side, is_over) for side in range(2) for is_over in range(2)]
    kinds = [F32, F32, BF, BF]
    result = [jax.ShapeDtypeStruct((parts, width, n), kind) for n, kind in zip((base, over, base, over), kinds)]
    return pl.pallas_call(
        functools.partial(pointwise_kernel, chips=chips, parts=parts, width=width, base=base, over=over),
        grid_spec=pltpu.PrefetchScalarGridSpec(
            num_scalar_prefetch=1,
            grid=(2, -(-(base + over) // TILE)),
            in_specs=[
                pl.BlockSpec(ups[0].shape, lambda w, c, at: (0, 0, 0), pipeline_mode=pl.Buffered(1))
                for _ in range(2 * chips)
            ]
            + [tile(0, 0), tile(1, 0), tile(0, 0), tile(1, 0)]
            + [pl.BlockSpec(data[4].shape, lambda w, c, at: (0, 0, 0, 0, 0), pipeline_mode=pl.Buffered(1))],
            out_specs=tiles
            + tiles
            + [
                pl.BlockSpec((chips, parts, 2, slab, wide), lambda w, c, at: (0, 0, 0, 0, 0)),
                pl.BlockSpec((parts, 2, width, LANES), lambda w, c, at: (0, 0, 0, 0)),
            ],
            scratch_shapes=[
                pltpu.VMEM((units, wide), BF),
                pltpu.VMEM((units, wide), BF),
                pltpu.VMEM((channels, units), BF),
                pltpu.VMEM((channels, units), BF),
                pltpu.VMEM((units, wide), F32),
                pltpu.VMEM((units, wide), F32),
                pltpu.VMEM((wide, TILE), F32),
                pltpu.VMEM((wide, TILE), F32),
                pltpu.VMEM((units, TILE), BF),
                pltpu.VMEM((units, TILE), BF),
            ],
        ),
        out_shape=result
        + result
        + [
            jax.ShapeDtypeStruct((chips, parts, 2, slab, wide), BF),
            jax.ShapeDtypeStruct((parts, 2, width, LANES), F32),
        ],
        compiler_params=params(62),
        cost_estimate=cost(70),
        name="pointwise",
    )(at, *ups, *downs, *data)


def per_device(
    inputs,
    crop_sizes,
    land_mask,
    conv_weight,
    norm_gain,
    norm_shift,
    up_weight,
    up_bias,
    down_weight,
    down_bias,
    cotangent,
    *,
    sizes,
):
    chips, cores, parts = sizes
    crops, side, _, width = inputs.shape
    taps = conv_weight.shape[0]
    cells = crops * side * side // parts
    local_units = up_weight.shape[1]
    channels = up_weight.shape[0]
    me = lax.axis_index("mp")
    core = lax.axis_index("core")
    chip = lax.axis_index("xy")

    def ring(k):
        return [(i, (i + k) % parts) for i in range(parts)]

    def everywhere(value, axes):
        for axis in axes:
            size = {"xy": chips, "core": cores, "mp": parts}[axis]
            if size <= 4:
                others = [lax.ppermute(value, axis, [(i, i ^ j) for i in range(size)]) for j in range(1, size)]
                value = sum(others, value)
                continue
            step = 1
            while step < size:
                value = value + lax.ppermute(value, axis, [(i, i ^ step) for i in range(size)])
                step *= 2
        return value

    def ring_back(k):
        return [(i, (i - k) % parts) for i in range(parts)]

    def to_parts(pieces, ring=ring):
        return [pieces[0]] + [lax.ppermute(pieces[k], "mp", ring(k)) for k in range(1, parts)]

    def exchange(by_part):
        return lax.all_to_all(by_part, "mp", 0, 0, tiled=True)

    swap = [(i, cores - 1 - i) for i in range(cores)]

    def to_core(value):
        return lax.ppermute(value, "core", swap)

    share = -(-local_units // (chips * cores))
    slab = ceil_to(share, 8)
    wide_width = ceil_to(width, 8)
    wide = parts * wide_width + 8
    rank = chip * cores + core
    spare = chips * cores * share - local_units

    def take(rows):
        rows = jnp.pad(rows, ((0, spare), (0, 0))) if spare else rows
        rows = lax.dynamic_slice_in_dim(rows, rank * share, share, axis=0)
        if wide_width > width:
            rows = jnp.pad(rows.reshape(share, parts, width), ((0, 0), (0, 0), (0, wide_width - width)))
        return rows.reshape(share, -1)

    own_bias = up_bias[:, None]
    own_bias = jnp.pad(own_bias, ((0, spare), (0, 0))) if spare else own_bias
    own_bias = lax.dynamic_slice_in_dim(own_bias, rank * share, share, axis=0)
    up_rows = jnp.pad(jnp.concatenate([take(up_weight.T), own_bias], axis=1), ((0, slab - share), (0, 7)))
    down_rows = jnp.pad(take(down_weight), ((0, slab - share), (0, 8)))
    rows = lax.all_gather(jnp.stack([up_rows, down_rows]), "mp", axis=1, tiled=False)

    def over_plane(own, bits):
        held = {0: own}
        for bit in bits:
            pairs = [(i, i ^ bit) for i in range(chips)]
            held.update({p ^ bit: lax.ppermute(value, "xy", pairs) for p, value in list(held.items())})
        return [held[p] for p in range(chips)]

    index = jnp.arange(side, dtype=jnp.int32)
    inside = (index[None, :, None] < crop_sizes[:, 0][:, None, None]) & (
        index[None, None, :] < crop_sizes[:, 1][:, None, None]
    )
    usable = jnp.where(inside, land_mask, 0)
    lane_mask = jnp.broadcast_to(usable[..., None].astype(BF), usable.shape + (LANES,))
    by_part = usable.reshape(crops, side // parts, parts, side).transpose(2, 0, 1, 3).reshape(parts, -1, side)
    by_part = by_part.astype(F32)
    lines = by_part.shape[1]
    upto = jnp.dot(by_part, jnp.triu(jnp.ones((side, side), F32)))
    before = jnp.dot(upto[:, :, -1], jnp.triu(jnp.ones((lines, lines), F32), 1))
    slots = jnp.where(by_part > 0, upto + before[:, :, None] - 1, -1).astype(jnp.int32)
    counts = jnp.sum(by_part, axis=(1, 2)).astype(jnp.int32)
    columns = jnp.broadcast_to(slots.reshape(parts, crops, -1)[..., None], (parts, crops, cells // crops, LANES))
    slots = slots.reshape(parts, 1, cells)
    ends = jnp.cumsum(jnp.sum(by_part.reshape(parts, crops, -1), axis=2), axis=1)
    reaches = jnp.pad(ends, ((0, 0), (1, 0))).astype(jnp.int32).reshape(-1)
    at = jnp.concatenate([me[None].astype(jnp.int32), counts, to_core(counts), chip[None].astype(jnp.int32), reaches])

    base = ceil_to(cells * 7 // 9, LANES)
    over = ceil_to(cells, LANES) - base
    over_full = jnp.where(jnp.max(counts) > base, 1.0, 0.0)

    cot_base, cot_over, down_bias_local = pack_cotangent(at, cotangent, lane_mask, slots, base, over)
    inputs, cot_base = after(inputs, cot_base)
    grad_base = exchange(cot_base)

    wide_taps = spread_rows(conv_weight.reshape(taps * taps, width))
    convolved, stats = conv_forward(inputs, lane_mask, wide_taps, taps, parts)
    stats = jnp.sum(stats, axis=(0, 3)).reshape(2, -1)[:, :width]
    extra = jnp.pad(jnp.stack([jnp.sum(by_part), over_full])[None], ((0, 0), (0, width - 2)))
    stats = everywhere(jnp.concatenate([stats, extra, jnp.sum(down_bias_local, axis=0)[None]]), ("core", "xy"))
    stats, rows = after(stats, rows)
    bits = [1 << j for j in range(chips.bit_length() - 1)]

    def double(held, bit):
        pairs = [(i, i ^ bit) for i in range(chips)]
        return {**held, **{p ^ bit: lax.ppermute(value, "xy", pairs) for p, value in held.items()}}

    ups, downs = {0: rows[0]}, {0: rows[1]}
    ups, downs = double(ups, bits[0]), double(downs, bits[-1])
    ocean_count = stats[2, 0]
    overflows = stats[2, 1] > 0
    down_bias_grad = stats[3]
    channel_mean = stats[0] / ocean_count
    inv_std = lax.rsqrt(stats[1] / ocean_count - channel_mean * channel_mean + EPSILON)
    gain = norm_gain.astype(F32)
    shift = norm_shift.astype(F32)
    scale = gain * inv_std

    affine = jnp.stack([scale, shift - channel_mean * scale])
    normed_base, normed_over = pack_normed(at, convolved.reshape(parts, cells, width), affine, slots, base, over)
    places = sorted(ups), sorted(downs)
    normed_base, grad_base = after(normed_base, grad_base)
    held = [ups[p] for p in places[0]] + [downs[p] for p in places[1]]
    ups, downs = dict(zip(places[0], held)), dict(zip(places[1], held[len(ups) :]))
    for j in range(1, len(bits)):
        ups, downs = double(ups, bits[j]), double(downs, bits[-1 - j])
    ups, downs = [ups[p] for p in range(chips)], [downs[p] for p in range(chips)]
    x_base, crowded, *held = after(exchange(normed_base), overflows, *ups, *downs)
    ups, downs = held[:chips], held[chips:]

    def overflow_in():
        own = jnp.stack([exchange(normed_over), exchange(cot_over)])
        return jnp.stack([own, to_core(own)])

    more = lax.cond(crowded, overflow_in, lambda: jnp.zeros((2, 2, parts, wide_width, over), BF))
    data = [x_base, to_core(x_base), grad_base, to_core(grad_base), more]
    *sums_out, weight_grad, sums = pointwise(at, ups, downs, data)
    branch, normed = list(sums_out[:4]), list(sums_out[4:])

    def over_cores(own, far):
        far = to_core(far)
        return [(own[k] + far[k].astype(F32)).astype(BF) for k in range(parts)]

    def home(total):
        return to_parts(total, ring_back)

    sums = everywhere(jnp.sum(sums, axis=3), ("core", "xy"))
    sums = sum(to_parts([sums[k] for k in range(parts)], ring_back))[:, :width]
    total, sums = after(tuple(over_cores(normed[0], normed[2])), sums)
    normed_base = home(total)
    total = over_cores(branch[0], branch[2])
    crowded, total, sums, columns, *normed_base = after(overflows, tuple(total), sums, columns, *normed_base)

    def overflow_out():
        return jnp.stack([exchange(jnp.stack(over_cores(v[1], v[3]))) for v in (branch, normed)])

    more = lax.cond(crowded, overflow_out, lambda: jnp.zeros((2, parts, wide_width, over), BF))

    shift_grad = sums[0]
    gain_grad = (sums[1] - shift * shift_grad) / gain
    vectors = jnp.stack([channel_mean, scale, scale * shift_grad / ocean_count, scale * inv_std * gain_grad / ocean_count])
    total, more = after(total, more)
    branch_base = home(total)

    own = lax.psum_scatter(weight_grad, "xy", scatter_dimension=0, tiled=False)
    own, vectors, *normed_base = after(own, spread_rows(vectors), *normed_base)
    own = lax.psum_scatter(own, "mp", scatter_dimension=0, tiled=False)
    input_grad, grad_conv = input_gradient(
        at, lane_mask, cotangent, convolved, wide_taps, vectors, columns, [*normed_base, more], taps
    )
    own, grad_conv = after(own, grad_conv)
    both = lax.all_gather(own, ("xy", "core"), axis=0, tiled=False)
    taps_local = taps_gradient(inputs, lane_mask, grad_conv, taps)
    output = make_output(at, inputs, lane_mask, down_bias.astype(F32)[None], columns, [*branch_base, more])
    taps_local = jnp.sum(taps_local, axis=2).transpose(1, 0, 2).reshape(taps * taps, -1)
    conv_weight_grad = everywhere(taps_local, ("core", "xy"))[:, :width].reshape(taps, taps, width)
    up_weight_grad, down_weight_grad, bias_rows = finish(both, parts, width, share, local_units)
    up_bias_grad = bias_rows[0]
    return (
        output,
        input_grad,
        conv_weight_grad,
        gain_grad,
        shift_grad,
        up_weight_grad,
        up_bias_grad,
        down_weight_grad,
        down_bias_grad,
    )


def solution(mesh):
    cores = 2
    parts = mesh.shape["mp"]
    chips = mesh.shape["dp"] // cores
    fine = Mesh(np.asarray(mesh.devices).reshape(chips, cores, parts), ("xy", "core", "mp"))
    dp = ("xy", "core")
    specs = (
        P(dp, None, None, "mp"),
        P(dp, None),
        P(dp, None, None),
        P(None, None, "mp"),
        P("mp"),
        P("mp"),
        P(None, "mp"),
        P("mp"),
        P("mp", None),
        P("mp"),
        P(dp, None, None, "mp"),
    )
    results = (
        P(dp, None, None, "mp"),
        P(dp, None, None, "mp"),
        P(None, None, "mp"),
        P("mp"),
        P("mp"),
        P(None, "mp"),
        P("mp"),
        P("mp", None),
        P("mp"),
    )
    return jax.shard_map(
        functools.partial(per_device, sizes=(chips, cores, parts)),
        mesh=fine,
        in_specs=specs,
        out_specs=results,
        check_vma=False,
    )
```
